32 devices in a mesh: groups: 2 (over y), cuts: 2 (over x), row: 4 (over z), sub: 2 (over core).
Axes of the slice: x: 2, y: 2, z: 4, core: 2. Of those that a mesh axis runs over, the one named last changes fastest.
Arguments:
- hop: bfloat16 [48, 6, 128, 128], P(('groups', 'row')), parts along dimension 0, may hold values from -0.21875 to 0.21875
- pattern: int32 [48, 6], P(('groups', 'row')), parts along dimension 0, may hold values from 0 to 23, as said below
- vectors: bfloat16 [2, 6144, 512], P('cuts', ('groups', 'row'), 'sub'), parts along dimension 1, may hold values from -6 to 6
- counts: int32 [4], P(('groups', 'cuts')), parts along dimension 0, may hold values from 256 to 512, as said below
- center: float32 [4], P(('groups', 'cuts')), parts along dimension 0, may hold values from -1 to 1
- halfwidth: float32 [4], P(('groups', 'cuts')), parts along dimension 0, may hold values from 1.5 to 3
Outputs:
- margin: float32 [4, 2, 256, 512], P(('groups', 'cuts'), 'sub', 'row'), parts along dimension 0
The draws below stay inside these ranges and needn't reach their ends.
There are 2 independent parts, one for each index of `groups`. The reference program is written for one: setup_inputs(seed, part) draws one part's arguments, and reference() takes and returns one part's arrays. A program takes and returns all parts, laid end to end along the dimension named above; each array names one. Nothing has to cross between parts.
Inputs may be any that keep to these rules, and one draw needn't show every extreme that they name: `pattern`: block row i's stored blocks lie in block columns (i + o) mod 24 for 6 distinct offsets o between -3 and 3; the offsets 0, -3 and 3 appear in every block row. `counts`: at least one slice has all 512 vectors live.
All inputs are finite; a program needn't handle non-finite values.
Results may differ from the reference program's by a relative error of at most 0.00061.
Values may be sent and summed in bfloat16 or wider, within the bound.
No kernel may reach another device: no remote copies, remote signals or barrier semaphores. Data moves between devices by JAX's collectives and lax.ppermute only.
A program may use at most 64 MiB of HBM per device.

```python
import jax
import jax.numpy as jnp

BS = 128
NNZ = 6
W = 3
NV = 512
NBR = 24
ORDER = 3072
NVH = 256
SLICES = 2


def draw_pattern(key, part):
    spare = 2 * W - 2
    candidates = jnp.concatenate([jnp.arange(-W + 1, 0, dtype=jnp.int32), jnp.arange(1, W, dtype=jnp.int32)])
    scores = jax.random.randint(key, (NBR, spare), 0, 1000, dtype=jnp.int32) * spare + jnp.arange(spare, dtype=jnp.int32)[None, :]
    chosen = jnp.argsort(scores, axis=1)[:, :NNZ - 3]
    offsets = jnp.concatenate([jnp.zeros((NBR, 1), jnp.int32), jnp.full((NBR, 1), -W, jnp.int32), jnp.full((NBR, 1), W, jnp.int32), candidates[chosen]], axis=1)
    block_rows = jnp.arange(NBR, dtype=jnp.int32)[:, None]
    return ((block_rows + offsets) % NBR).astype(jnp.int32)


def draw_counts(key, part):
    first_key = jax.random.fold_in(key, 11)
    second_key = jax.random.fold_in(key, 12)
    values = jax.random.randint(first_key, (SLICES,), NV // 2, NV + 1, dtype=jnp.int32)
    fullest = jax.random.randint(second_key, (), 0, SLICES, dtype=jnp.int32)
    return jnp.where(jnp.arange(SLICES, dtype=jnp.int32) == fullest, NV, values).astype(jnp.int32)


def levels(stream_key, dims, shards, least, high):
    loudness = 1.0
    for position, shards_of in shards:
        draws = jax.random.uniform(jax.random.fold_in(jax.random.fold_in(stream_key, 6), position), (shards_of,), jnp.float32, least / len(shards), high / len(shards))
        loudness = loudness * jnp.repeat(jnp.exp(draws), dims[position] // shards_of).reshape((-1,) + (1,) * (len(dims) - 1 - position))
    return loudness


def normal_values(key, extent, spread, reach, shards=(), kind=jnp.bfloat16):
    result = spread * jax.random.normal(key, extent, jnp.float32)
    if shards:
        result = result * levels(key, extent, shards, -0.22, 0.18)
    return jnp.clip(result, -reach, reach).astype(kind)


def setup_inputs(seed: int = 0, part: int = 0) -> dict:
    arg_keys = jax.random.split(jax.random.key(seed), 7)
    part_keys = jax.random.split(jax.random.fold_in(arg_keys[6], part), 7)
    return {
        "hop": normal_values(part_keys[0], (NBR, NNZ, BS, BS), (NNZ * BS) ** -0.5, 0.21875, ((0, 4),)),
        "pattern": draw_pattern(jax.random.fold_in(jax.random.fold_in(arg_keys[6], part), 71), part),
        "vectors": normal_values(part_keys[2], (SLICES, ORDER, NV), 1.0, 6.0, ((0, 2), (1, 4), (2, 2))),
        "counts": draw_counts(jax.random.fold_in(jax.random.fold_in(arg_keys[6], part), 71), part),
        "center": jnp.clip(jax.random.uniform(part_keys[4], (SLICES,), jnp.float32, -1.0, 1.0) * levels(part_keys[4], (SLICES,), ((0, 2),), -0.4, 0.0), -1.0, 1.0),
        "halfwidth": jnp.clip(1.5 + 1.5 * jax.random.uniform(part_keys[5], (SLICES,), jnp.float32) ** levels(part_keys[5], (SLICES,), ((0, 2),), -0.2, 0.2), 1.5, 3.0),
    }


def apply_hop(hop, pattern, field):
    blocks = field.reshape(NBR, BS, NV)
    total = jnp.zeros((NBR, BS, NV), jnp.float32)
    for k in range(NNZ):
        picked = blocks[pattern[:, k]]
        total = total + jnp.einsum("rij,rjn->rin", hop[:, k].astype(jnp.float32), picked.astype(jnp.float32))
    return total.reshape(ORDER, NV)


def reference(hop, pattern, vectors, counts, center, halfwidth):
    results = []
    for s in range(SLICES):
        live = (jnp.arange(NV, dtype=jnp.int32) < counts[s]).astype(jnp.bfloat16)
        start = vectors[s] * live[None, :]
        first_image = apply_hop(hop, pattern, start)
        step_one = ((first_image - center[s] * start.astype(jnp.float32)) / halfwidth[s]).astype(jnp.bfloat16)
        second_image = apply_hop(hop, pattern, step_one)
        filtered = (2.0 * (second_image - center[s] * step_one.astype(jnp.float32)) / halfwidth[s] - start.astype(jnp.float32)).astype(jnp.bfloat16)
        gram = jnp.dot(filtered.T, filtered, preferred_element_type=jnp.float32) / ORDER
        results.append(gram.reshape(2, NVH, NV))
    return jnp.stack(results)
```

```python
import jax
import jax.numpy as jnp
from jax import lax
from jax.experimental import pallas as pl
from jax.experimental.pallas import tpu as pltpu
from jax.sharding import PartitionSpec as P

W = 3


def band_kernel(cols_ref, hop_ref, low_ref, own_ref, high_ref):
    rows_dev, stored, block, _ = hop_ref.shape
    low_ref[...] = jnp.zeros_like(low_ref)
    own_ref[...] = jnp.zeros_like(own_ref)
    high_ref[...] = jnp.zeros_like(high_ref)
    for r in range(rows_dev):
        for k in range(stored):
            col = cols_ref[r, k]
            tile = hop_ref[r, k]

            @pl.when((col >= W) & (col < W + rows_dev))
            def _():
                at = pl.multiple_of((col - W) * block, block)
                own_ref[pl.ds(r * block, block), pl.ds(at, block)] = tile

            if r < W:
                @pl.when(col < W)
                def _():
                    at = pl.multiple_of(col * block, block)
                    low_ref[pl.ds(r * block, block), pl.ds(at, block)] = tile

            if r >= rows_dev - W:
                @pl.when(col >= W + rows_dev)
                def _():
                    at = pl.multiple_of((col - W - rows_dev) * block, block)
                    high_ref[pl.ds((r - rows_dev + W) * block, block), pl.ds(at, block)] = tile


def band_parts(hop, cols):
    rows_dev, _, block, _ = hop.shape
    wide, tall = W * block, rows_dev * block
    return pl.pallas_call(
        band_kernel,
        out_shape=(
            jax.ShapeDtypeStruct((wide, wide), hop.dtype),
            jax.ShapeDtypeStruct((tall, tall), hop.dtype),
            jax.ShapeDtypeStruct((wide, wide), hop.dtype),
        ),
        in_specs=[
            pl.BlockSpec(memory_space=pltpu.SMEM),
            pl.BlockSpec(memory_space=pltpu.VMEM),
        ],
        out_specs=[pl.BlockSpec(memory_space=pltpu.VMEM)] * 3,
        compiler_params=pltpu.CompilerParams(vmem_limit_bytes=16 * 1024 * 1024),
        cost_estimate=pl.CostEstimate(flops=0, bytes_accessed=4_000_000, transcendentals=0),
    )(cols, hop)


def mm(a, b):
    return jnp.dot(a, b, preferred_element_type=jnp.float32)


def tmm(a, b):
    return lax.dot_general(a, b, (((0,), (0,)), ((), ())), preferred_element_type=jnp.float32)


def body(hop, pattern, vectors, counts, center, halfwidth):
    rows_dev = hop.shape[0]
    block = hop.shape[2]
    half = vectors.shape[2]
    row_count = lax.axis_size("row")
    total_blocks = rows_dev * row_count
    order_total = total_blocks * block
    wide = W * block
    tall = rows_dev * block
    forward = [(i, (i + 1) % row_count) for i in range(row_count)]
    backward = [(target, source) for source, target in forward]
    swap = [(0, 1), (1, 0)]

    x = vectors[0]
    x_low, x_high = x[:wide], x[tall - wide:]
    halo_low = lax.ppermute(x_high, "row", forward)
    halo_high = lax.ppermute(x_low, "row", backward)

    first_block = lax.axis_index("row") * rows_dev
    cols = (pattern - first_block + W) % total_blocks
    band_low, band_own, band_high = band_parts(hop, cols)
    shift = center[0]
    width = halfwidth[0]

    own = mm(band_own, x)
    s_low = ((own[:wide] + mm(band_low, halo_low) - shift * x_low.astype(jnp.float32)) / width).astype(jnp.bfloat16)
    next_high = lax.ppermute(s_low, "row", backward)
    s_high = ((own[tall - wide:] + mm(band_high, halo_high) - shift * x_high.astype(jnp.float32)) / width).astype(jnp.bfloat16)
    next_low = lax.ppermute(s_high, "row", forward)

    own2 = mm(band_own[:, :wide], s_low) + mm(band_own[:, tall - wide:], s_high)
    column_ids = lax.axis_index("sub") * half + jnp.arange(half, dtype=jnp.int32)
    live = (column_ids < counts[0])[None, :]

    def finish(image, s, start):
        value = 2.0 * (image - shift * s.astype(jnp.float32)) / width - start.astype(jnp.float32)
        return jnp.where(live, value, 0.0).astype(jnp.bfloat16)

    f_high = finish(own2[tall - wide:] + mm(band_high, next_high), s_high, x_high)
    o_high = lax.ppermute(f_high, "sub", swap)
    f_low = finish(own2[:wide] + mm(band_low, next_low), s_low, x_low)
    o_low = lax.ppermute(f_low, "sub", swap)

    same = tmm(f_high, f_high) + tmm(f_low, f_low)
    cross = tmm(f_high, o_high) + tmm(f_low, o_low)
    term = jnp.concatenate([same, cross], axis=1)
    share = half // row_count
    parts = lax.all_to_all(
        term.reshape(row_count, share, 2 * half), "row", split_axis=0, concat_axis=0
    )
    gram = jnp.sum(parts, axis=0) / order_total
    a, b = gram[:, :half], gram[:, half:]
    first = lax.axis_index("sub") == 0
    margin = jnp.concatenate([jnp.where(first, a, b), jnp.where(first, b, a)], axis=1)
    return margin.reshape(1, 1, share, 2 * half)


def solution(mesh):
    in_specs = (
        P(("groups", "row"), None, None, None),
        P(("groups", "row"), None),
        P("cuts", ("groups", "row"), "sub"),
        P(("groups", "cuts")),
        P(("groups", "cuts")),
        P(("groups", "cuts")),
    )
    out_specs = P(("groups", "cuts"), "sub", "row", None)
    return jax.shard_map(body, mesh=mesh, in_specs=in_specs, out_specs=out_specs, check_vma=False)
```

```python
import functools

import jax
import jax.numpy as jnp
from jax import lax
from jax.experimental import pallas as pl
from jax.experimental.pallas import tpu as pltpu
from jax.sharding import PartitionSpec as P

W = 3
LIMIT = 16 * 1024 * 1024


def band_kernel(cols_ref, hop_ref, low_ref, own_ref, high_ref):
    rows_dev, stored, block, _ = hop_ref.shape
    low_ref[...] = jnp.zeros_like(low_ref)
    own_ref[...] = jnp.zeros_like(own_ref)
    high_ref[...] = jnp.zeros_like(high_ref)
    for r in range(rows_dev):
        for k in range(stored):
            col = cols_ref[r, k]
            tile = hop_ref[r, k]

            @pl.when((col >= W) & (col < W + rows_dev))
            def _():
                at = pl.multiple_of((col - W) * block, block)
                own_ref[pl.ds(r * block, block), pl.ds(at, block)] = tile

            if r < W:
                @pl.when(col < W)
                def _():
                    at = pl.multiple_of(col * block, block)
                    low_ref[pl.ds(r * block, block), pl.ds(at, block)] = tile

            if r >= rows_dev - W:
                @pl.when(col >= W + rows_dev)
                def _():
                    at = pl.multiple_of((col - W - rows_dev) * block, block)
                    high_ref[pl.ds((r - rows_dev + W) * block, block), pl.ds(at, block)] = tile


def band_parts(hop, cols):
    rows_dev, _, block, _ = hop.shape
    wide, tall = W * block, rows_dev * block
    return pl.pallas_call(
        band_kernel,
        out_shape=(
            jax.ShapeDtypeStruct((wide, wide), hop.dtype),
            jax.ShapeDtypeStruct((tall, tall), hop.dtype),
            jax.ShapeDtypeStruct((wide, wide), hop.dtype),
        ),
        in_specs=[
            pl.BlockSpec(memory_space=pltpu.SMEM),
            pl.BlockSpec(memory_space=pltpu.VMEM),
        ],
        out_specs=[pl.BlockSpec(memory_space=pltpu.VMEM)] * 3,
        compiler_params=pltpu.CompilerParams(vmem_limit_bytes=LIMIT),
        cost_estimate=pl.CostEstimate(flops=0, bytes_accessed=4_000_000, transcendentals=0),
    )(cols, hop)


def mm(a, b):
    return jnp.dot(a, b, preferred_element_type=jnp.float32)


def tmm(a, b):
    return lax.dot_general(a, b, (((0,), (0,)), ((), ())), preferred_element_type=jnp.float32)


def early_kernel(f_high_ref, o_high_ref, f_low_ref, out_ref):
    half = f_high_ref.shape[1]
    f_high, f_low = f_high_ref[...], f_low_ref[...]
    out_ref[:, :half] = tmm(f_high, f_high) + tmm(f_low, f_low)
    out_ref[:, half:] = tmm(f_high, o_high_ref[...])


def early_gram(f_high, o_high, f_low):
    half = f_high.shape[1]
    return pl.pallas_call(
        early_kernel,
        out_shape=jax.ShapeDtypeStruct((half, 2 * half), jnp.float32),
        in_specs=[pl.BlockSpec(memory_space=pltpu.VMEM)] * 3,
        out_specs=pl.BlockSpec(memory_space=pltpu.VMEM),
        compiler_params=pltpu.CompilerParams(vmem_limit_bytes=LIMIT),
        cost_estimate=pl.CostEstimate(flops=200_000_000, bytes_accessed=1_000_000, transcendentals=0),
    )(f_high, o_high, f_low)


def code_kernel(share, early_ref, f_low_ref, o_low_ref, out_ref):
    half = f_low_ref.shape[1]
    same = early_ref[:, :half]
    cross = early_ref[:, half:] + tmm(f_low_ref[...], o_low_ref[...])
    top = jnp.max(jnp.maximum(jnp.abs(same), jnp.abs(cross)), axis=(0, 1), keepdims=True)
    e = jnp.clip(jnp.ceil(jnp.log2(jnp.maximum(top, 1e-36))) - 14.0, -100.0, 60.0)
    scale = jnp.exp2(-e)
    row = lax.broadcasted_iota(jnp.int32, (half, half), 0)
    col = lax.broadcasted_iota(jnp.int32, (half, half), 1)
    slot = (lax.rem(row, share) == 1) & (col == row - 1)
    out_ref[:, :half] = jnp.where(slot, e, same * scale)
    out_ref[:, half:] = cross * scale


def code_terms(early, f_low, o_low, share):
    return pl.pallas_call(
        functools.partial(code_kernel, share),
        out_shape=jax.ShapeDtypeStruct(early.shape, jnp.float32),
        in_specs=[pl.BlockSpec(memory_space=pltpu.VMEM)] * 3,
        out_specs=pl.BlockSpec(memory_space=pltpu.VMEM),
        compiler_params=pltpu.CompilerParams(vmem_limit_bytes=LIMIT),
        cost_estimate=pl.CostEstimate(flops=50_000_000, bytes_accessed=1_000_000, transcendentals=0),
    )(early, f_low, o_low)


def sum_kernel(order_total, where_ref, coded_ref, *refs):
    *pieces, out_ref = refs
    share, half = out_ref.shape[0], out_ref.shape[1] // 2
    me, sub = where_ref[0], where_ref[1]
    row = lax.broadcasted_iota(jnp.int32, (share, half), 0)
    col = lax.broadcasted_iota(jnp.int32, (share, half), 1)
    start = me * share
    slot = (row == 1) & (col == start)
    twin = (row == 0) & (col == start + 1)
    same = jnp.zeros((share, half), jnp.float32)
    cross = jnp.zeros((share, half), jnp.float32)
    here = coded_ref[pl.ds(pl.multiple_of(start, 8), share), :]
    for value in [here] + [ref[...] for ref in pieces]:
        e = jnp.sum(jnp.where(slot, value[:, :half], 0.0), axis=(0, 1), keepdims=True)
        scale = jnp.exp2(e) / order_total
        same += value[:, :half] * scale
        cross += value[:, half:] * scale
    lost = jnp.sum(jnp.where(twin, same, 0.0), axis=(0, 1), keepdims=True)
    same = jnp.where(slot, lost, same)
    out_ref[:, pl.ds(pl.multiple_of(sub * half, half), half)] = same
    out_ref[:, pl.ds(pl.multiple_of((1 - sub) * half, half), half)] = cross


def sum_terms(where, coded, pieces, order_total):
    share, columns = pieces[0].shape
    return pl.pallas_call(
        functools.partial(sum_kernel, order_total),
        out_shape=jax.ShapeDtypeStruct((share, columns), jnp.float32),
        in_specs=[pl.BlockSpec(memory_space=pltpu.SMEM)]
        + [pl.BlockSpec(memory_space=pltpu.VMEM)] * (1 + len(pieces)),
        out_specs=pl.BlockSpec(memory_space=pltpu.VMEM),
        compiler_params=pltpu.CompilerParams(vmem_limit_bytes=LIMIT),
        cost_estimate=pl.CostEstimate(flops=1_000_000, bytes_accessed=1_000_000, transcendentals=0),
    )(where, coded, *pieces)


def body(hop, pattern, vectors, counts, center, halfwidth):
    rows_dev = hop.shape[0]
    block = hop.shape[2]
    half = vectors.shape[2]
    row_count = lax.axis_size("row")
    total_blocks = rows_dev * row_count
    order_total = total_blocks * block
    wide = W * block
    tall = rows_dev * block
    forward = [(i, (i + 1) % row_count) for i in range(row_count)]
    backward = [(target, source) for source, target in forward]
    swap = [(0, 1), (1, 0)]

    x = vectors[0]
    x_low, x_high = x[:wide], x[tall - wide:]
    halo_low = lax.ppermute(x_high, "row", forward)
    halo_high = lax.ppermute(x_low, "row", backward)

    first_block = lax.axis_index("row") * rows_dev
    cols = (pattern - first_block + W) % total_blocks
    band_low, band_own, band_high = band_parts(hop, cols)
    shift = center[0]
    width = halfwidth[0]

    own = mm(band_own, x)
    s_low = ((own[:wide] + mm(band_low, halo_low) - shift * x_low.astype(jnp.float32)) / width).astype(jnp.bfloat16)
    next_high = lax.ppermute(s_low, "row", backward)
    s_high = ((own[tall - wide:] + mm(band_high, halo_high) - shift * x_high.astype(jnp.float32)) / width).astype(jnp.bfloat16)
    next_low = lax.ppermute(s_high, "row", forward)

    own2 = mm(band_own[:, :wide], s_low) + mm(band_own[:, tall - wide:], s_high)
    column_ids = lax.axis_index("sub") * half + jnp.arange(half, dtype=jnp.int32)
    live = (column_ids < counts[0])[None, :]

    def finish(image, s, start):
        value = 2.0 * (image - shift * s.astype(jnp.float32)) / width - start.astype(jnp.float32)
        return jnp.where(live, value, 0.0).astype(jnp.bfloat16)

    f_high = finish(own2[tall - wide:] + mm(band_high, next_high), s_high, x_high)
    o_high = lax.ppermute(f_high, "sub", swap)
    f_low = finish(own2[:wide] + mm(band_low, next_low), s_low, x_low)
    o_low = lax.ppermute(f_low, "sub", swap)

    early = early_gram(f_high, o_high, f_low)
    coded = code_terms(early, f_low, o_low, half // row_count)
    share = half // row_count
    me = lax.axis_index("row")
    sent = coded.astype(jnp.float16)
    arrived = []
    for step in range(1, row_count):
        target = (me + step) % row_count
        piece = lax.dynamic_slice_in_dim(sent, target * share, share, axis=0)
        ring = [(i, (i + step) % row_count) for i in range(row_count)]
        arrived.append(lax.ppermute(piece, "row", ring))
    where = jnp.stack([me, lax.axis_index("sub")]).astype(jnp.int32)
    margin = sum_terms(where, coded, [p.astype(jnp.float32) for p in arrived], order_total)
    return margin.reshape(1, 1, share, 2 * half)


def solution(mesh):
    in_specs = (
        P(("groups", "row"), None, None, None),
        P(("groups", "row"), None),
        P("cuts", ("groups", "row"), "sub"),
        P(("groups", "cuts")),
        P(("groups", "cuts")),
        P(("groups", "cuts")),
    )
    out_specs = P(("groups", "cuts"), "sub", "row", None)
    return jax.shard_map(body, mesh=mesh, in_specs=in_specs, out_specs=out_specs, check_vma=False)
```

```python
import functools

import jax
import jax.numpy as jnp
from jax import lax
from jax.experimental import pallas as pl
from jax.experimental.pallas import tpu as pltpu
from jax.sharding import PartitionSpec as P

W = 3
LIMIT = 16 * 1024 * 1024
VMEM = pl.BlockSpec(memory_space=pltpu.VMEM)
SMEM = pl.BlockSpec(memory_space=pltpu.SMEM)


def call(kernel, out_shape, in_specs, flops, traffic):
    return pl.pallas_call(
        kernel,
        out_shape=out_shape,
        in_specs=in_specs,
        out_specs=jax.tree.map(lambda _: VMEM, out_shape),
        compiler_params=pltpu.CompilerParams(vmem_limit_bytes=LIMIT),
        cost_estimate=pl.CostEstimate(flops=flops, bytes_accessed=traffic, transcendentals=0),
    )


def mm(a, b):
    return jnp.dot(a, b, preferred_element_type=jnp.float32)


def tmm(a, b):
    return lax.dot_general(a, b, (((0,), (0,)), ((), ())), preferred_element_type=jnp.float32)


def band_kernel(total_blocks, pattern_ref, hop_ref, low_ref, own_ref, high_ref):
    rows_dev, stored, block, _ = hop_ref.shape
    first_block = lax.axis_index("row") * rows_dev
    low_ref[...] = jnp.zeros_like(low_ref)
    own_ref[...] = jnp.zeros_like(own_ref)
    high_ref[...] = jnp.zeros_like(high_ref)
    for r in range(rows_dev):
        for k in range(stored):
            col = lax.rem(pattern_ref[r, k] - first_block + (W + total_blocks), total_blocks)
            tile = hop_ref[r, k]

            @pl.when((col >= W) & (col < W + rows_dev))
            def _():
                at = pl.multiple_of((col - W) * block, block)
                own_ref[pl.ds(r * block, block), pl.ds(at, block)] = tile

            if r < W:
                @pl.when(col < W)
                def _():
                    at = pl.multiple_of(col * block, block)
                    low_ref[pl.ds(r * block, block), pl.ds(at, block)] = tile

            if r >= rows_dev - W:
                @pl.when(col >= W + rows_dev)
                def _():
                    at = pl.multiple_of((col - W - rows_dev) * block, block)
                    high_ref[pl.ds((r - rows_dev + W) * block, block), pl.ds(at, block)] = tile


def band_parts(hop, pattern, total_blocks):
    rows_dev, _, block, _ = hop.shape
    wide, tall = W * block, rows_dev * block
    return call(
        functools.partial(band_kernel, total_blocks),
        (
            jax.ShapeDtypeStruct((wide, wide), hop.dtype),
            jax.ShapeDtypeStruct((tall, tall), hop.dtype),
            jax.ShapeDtypeStruct((wide, wide), hop.dtype),
        ),
        [SMEM, VMEM], 0, 4_000_000,
    )(pattern, hop)


def step_kernel(table_ref, own_ref, low_ref, high_ref, halo_low_ref, halo_high_ref, x_ref, out_low_ref, out_high_ref):
    wide = low_ref.shape[0]
    shift, width = table_ref[0:1, :], table_ref[1:2, :]
    image = own_ref[:wide, :] + mm(low_ref[...], halo_low_ref[...])
    out_low_ref[...] = ((image - shift * x_ref[:wide, :].astype(jnp.float32)) / width).astype(jnp.bfloat16)
    image = own_ref[wide:, :] + mm(high_ref[...], halo_high_ref[...])
    out_high_ref[...] = ((image - shift * x_ref[wide:, :].astype(jnp.float32)) / width).astype(jnp.bfloat16)


def step(table, own, low, high, halo_low, halo_high, x):
    half = jax.ShapeDtypeStruct(halo_low.shape, jnp.bfloat16)
    return call(step_kernel, (half, half), [VMEM] * 7, 80_000_000, 1_500_000)(
        table, own, low, high, halo_low, halo_high, x)


def finish_kernel(table_ref, own_ref, low_ref, high_ref, halo_low_ref, halo_high_ref, s_low_ref, s_high_ref, x_ref, out_ref):
    wide = low_ref.shape[0]
    shift, width = table_ref[0:1, :], table_ref[1:2, :]
    live = table_ref[2:3, :] > 0.0

    def put(at, image, s):
        value = 2.0 * (image - shift * s.astype(jnp.float32)) / width - x_ref[at, :].astype(jnp.float32)
        out_ref[at, :] = jnp.where(live, value, 0.0).astype(jnp.bfloat16)

    put(pl.ds(0, wide), own_ref[:wide, :] + mm(low_ref[...], halo_low_ref[...]), s_low_ref[...])
    put(pl.ds(wide, wide), own_ref[wide:, :] + mm(high_ref[...], halo_high_ref[...]), s_high_ref[...])


def finish(table, own, low, high, halo_low, halo_high, s_low, s_high, x):
    return call(finish_kernel, jax.ShapeDtypeStruct(x.shape, jnp.bfloat16), [VMEM] * 9, 80_000_000, 1_500_000)(
        table, own, low, high, halo_low, halo_high, s_low, s_high, x)


def early_kernel(*refs):
    *mine, out_ref = refs
    parts = [ref[...] for ref in mine]
    count = (len(parts) + 1) // 2
    own = jnp.concatenate(parts[:count], axis=1)
    out_ref[...] = tmm(own, jnp.concatenate(parts, axis=1))


def early_gram(parts):
    width = parts[0].shape[1]
    half = width * ((len(parts) + 1) // 2)
    shape = jax.ShapeDtypeStruct((half, width * len(parts)), jnp.float32)
    return call(early_kernel, shape, [VMEM] * len(parts), 150_000_000, 1_500_000)(*parts)


def code_kernel(share, early_ref, *refs):
    *mine, last_ref, out_ref = refs
    half = out_ref.shape[0]
    known = early_ref.shape[1]
    own = jnp.concatenate([ref[...] for ref in mine], axis=1)
    early = early_ref[...]
    late = tmm(own, last_ref[...])
    top = jnp.maximum(
        jnp.max(jnp.abs(early), axis=(0, 1), keepdims=True),
        jnp.max(jnp.abs(late), axis=(0, 1), keepdims=True),
    )
    e = jnp.clip(jnp.ceil(jnp.log2(jnp.maximum(top, 1e-36))) - 14.0, -100.0, 60.0)
    scale = jnp.exp2(-e)
    row = lax.broadcasted_iota(jnp.int32, (half, known), 0)
    col = lax.broadcasted_iota(jnp.int32, (half, known), 1)
    slot = (lax.rem(row, share) == 1) & (col == row - 1)
    out_ref[:, :known] = jnp.where(slot, e, early * scale)
    out_ref[:, known:] = late * scale


def code_terms(early, mine, last, share):
    half = early.shape[0]
    shape = jax.ShapeDtypeStruct((half, 2 * half), jnp.float32)
    return call(functools.partial(code_kernel, share), shape, [VMEM] * (2 + len(mine)), 50_000_000, 1_500_000)(
        early, *mine, last)


def sum_kernel(order_total, coded_ref, *refs):
    *pieces, out_ref = refs
    share, half = out_ref.shape[0], out_ref.shape[1] // 2
    me, sub = lax.axis_index("row"), lax.axis_index("sub")
    head = 8
    row = lax.broadcasted_iota(jnp.int32, (head, half), 0)
    col = lax.broadcasted_iota(jnp.int32, (head, half), 1)
    start = me * share
    slot = (row == 1) & (col == start)
    twin = (row == 0) & (col == start + 1)
    same = jnp.zeros((share, half), jnp.float32)
    cross = jnp.zeros((share, half), jnp.float32)
    here = coded_ref[pl.ds(pl.multiple_of(start, 8), share), :]
    for value in [here] + [ref[...] for ref in pieces]:
        e = jnp.sum(jnp.where(slot, value[:head, :half], 0.0), axis=(0, 1), keepdims=True)
        scale = jnp.exp2(e) / order_total
        same += value[:, :half] * scale
        cross += value[:, half:] * scale
    lost = jnp.sum(jnp.where(twin, same[:head], 0.0), axis=(0, 1), keepdims=True)
    at = pl.ds(pl.multiple_of(sub * half, half), half)
    out_ref[:, at] = same
    out_ref[:head, at] = jnp.where(slot, lost, same[:head])
    out_ref[:, pl.ds(pl.multiple_of((1 - sub) * half, half), half)] = cross


def sum_terms(coded, pieces, order_total):
    shape = jax.ShapeDtypeStruct(pieces[0].shape, jnp.float32)
    return call(functools.partial(sum_kernel, order_total), shape, [VMEM] * (1 + len(pieces)), 1_000_000, 1_000_000)(
        coded, *pieces)


def body(hop, pattern, vectors, counts, center, halfwidth):
    rows_dev = hop.shape[0]
    block = hop.shape[2]
    half = vectors.shape[2]
    row_count = lax.axis_size("row")
    total_blocks = rows_dev * row_count
    order_total = total_blocks * block
    wide = W * block
    tall = rows_dev * block
    piece = half // 2
    forward = [(i, (i + 1) % row_count) for i in range(row_count)]
    backward = [(target, source) for source, target in forward]
    swap = [(0, 1), (1, 0)]

    def from_sides(low, high):
        return lax.ppermute(high, "row", forward), lax.ppermute(low, "row", backward)

    x = vectors[0]
    x0, x1 = x[:, :piece], x[:, piece:]
    halo0 = from_sides(x0[:wide], x0[wide:])
    low, own, high = band_parts(hop, pattern, total_blocks)
    low, own, high, x1 = lax.optimization_barrier((low, own, high, x1))
    halo1 = from_sides(x1[:wide], x1[wide:])

    column_ids = lax.axis_index("sub") * half + jnp.arange(half, dtype=jnp.int32)
    live = (column_ids < counts[0]).astype(jnp.float32)

    def table_of(mask):
        rows = [jnp.full((piece,), center[0]), jnp.full((piece,), halfwidth[0]), mask]
        return jnp.stack(rows + [jnp.zeros((piece,), jnp.float32)] * 5)

    table0, table1 = table_of(live[:piece]), table_of(live[piece:])

    s0 = step(table0, mm(own, x0), low, high, *halo0, x0)
    next0 = from_sides(*s0)
    s1 = step(table1, mm(own, x1), low, high, *halo1, x1)
    next1 = from_sides(*s1)

    def image(s):
        return mm(own[:, :wide], s[0]) + mm(own[:, wide:], s[1])

    f0 = finish(table0, image(s0), low, high, *next0, *s0, x0)
    o0 = lax.ppermute(f0, "sub", swap)
    f1 = finish(table1, image(s1), low, high, *next1, *s1, x1)
    o1 = lax.ppermute(f1, "sub", swap)

    share = half // row_count
    early = early_gram([f0, f1, o0])
    coded = code_terms(early, [f0, f1], o1, share)
    me = lax.axis_index("row")
    sent = coded.astype(jnp.float16)
    arrived = []
    for shift in range(1, row_count):
        target = (me + shift) % row_count
        part = lax.dynamic_slice_in_dim(sent, target * share, share, axis=0)
        ring = [(i, (i + shift) % row_count) for i in range(row_count)]
        arrived.append(lax.ppermute(part, "row", ring))
    margin = sum_terms(coded, [p.astype(jnp.float32) for p in arrived], order_total)
    return margin.reshape(1, 1, share, 2 * half)


def solution(mesh):
    in_specs = (
        P(("groups", "row"), None, None, None),
        P(("groups", "row"), None),
        P("cuts", ("groups", "row"), "sub"),
        P(("groups", "cuts")),
        P(("groups", "cuts")),
        P(("groups", "cuts")),
    )
    out_specs = P(("groups", "cuts"), "sub", "row", None)
    return jax.shard_map(body, mesh=mesh, in_specs=in_specs, out_specs=out_specs, check_vma=False)
```

```python
import functools

import jax
import jax.numpy as jnp
from jax import lax
from jax.experimental import pallas as pl
from jax.experimental.pallas import tpu as pltpu
from jax.sharding import PartitionSpec as P

W = 3
LIMIT = 16 * 1024 * 1024
VMEM = pl.BlockSpec(memory_space=pltpu.VMEM)
SMEM = pl.BlockSpec(memory_space=pltpu.SMEM)


def call(kernel, out_shape, in_specs):
    return pl.pallas_call(
        kernel,
        out_shape=out_shape,
        in_specs=in_specs,
        out_specs=jax.tree.map(lambda _: VMEM, out_shape),
        compiler_params=pltpu.CompilerParams(vmem_limit_bytes=LIMIT),
        cost_estimate=pl.CostEstimate(flops=1000, bytes_accessed=1000, transcendentals=0),
    )


def mm(a, b):
    return jnp.dot(a, b, preferred_element_type=jnp.float32)


def tmm(a, b):
    return lax.dot_general(a, b, (((0,), (0,)), ((), ())), preferred_element_type=jnp.float32)


def band_kernel(total_blocks, pattern_ref, counts_ref, center_ref, width_ref, hop_ref, x_ref, low_ref, own_ref, high_ref, image_ref, table_ref):
    rows_dev, stored, block, _ = hop_ref.shape
    first_block = lax.axis_index("row") * rows_dev
    low_ref[...] = jnp.zeros_like(low_ref)
    own_ref[...] = jnp.zeros_like(own_ref)
    high_ref[...] = jnp.zeros_like(high_ref)
    for r in range(rows_dev):
        for k in range(stored):
            col = lax.rem(pattern_ref[r, k] - first_block + (W + total_blocks), total_blocks)
            tile = hop_ref[r, k]

            @pl.when((col >= W) & (col < W + rows_dev))
            def _():
                at = pl.multiple_of((col - W) * block, block)
                own_ref[pl.ds(r * block, block), pl.ds(at, block)] = tile

            if r < W:
                @pl.when(col < W)
                def _():
                    at = pl.multiple_of(col * block, block)
                    low_ref[pl.ds(r * block, block), pl.ds(at, block)] = tile

            if r >= rows_dev - W:
                @pl.when(col >= W + rows_dev)
                def _():
                    at = pl.multiple_of((col - W - rows_dev) * block, block)
                    high_ref[pl.ds((r - rows_dev + W) * block, block), pl.ds(at, block)] = tile

    image_ref[...] = mm(own_ref[...], x_ref[...])
    half = x_ref.shape[1]
    line = lax.broadcasted_iota(jnp.int32, (8, half), 0)
    column = lax.broadcasted_iota(jnp.int32, (8, half), 1) + lax.axis_index("sub") * half
    live = jnp.where(column < counts_ref[0], 1.0, 0.0)
    table_ref[...] = jnp.where(line == 0, center_ref[0], jnp.where(line == 1, width_ref[0], live))


def band_parts(hop, pattern, counts, center, halfwidth, x, total_blocks):
    rows_dev, _, block, _ = hop.shape
    wide, tall, half = W * block, rows_dev * block, x.shape[1]
    return call(
        functools.partial(band_kernel, total_blocks),
        (
            jax.ShapeDtypeStruct((wide, wide), hop.dtype),
            jax.ShapeDtypeStruct((tall, tall), hop.dtype),
            jax.ShapeDtypeStruct((wide, wide), hop.dtype),
            jax.ShapeDtypeStruct((tall, half), jnp.float32),
            jax.ShapeDtypeStruct((8, half), jnp.float32),
        ),
        [SMEM] * 4 + [VMEM] * 2,
    )(pattern, counts, center, halfwidth, hop, x)


def step_kernel(at, table_ref, image_ref, low_ref, high_ref, halo_low_ref, halo_high_ref, x_ref, out_low_ref, out_high_ref):
    wide = low_ref.shape[0]
    shift, width = table_ref[0:1, at], table_ref[1:2, at]
    image = image_ref[:wide, at] + mm(low_ref[...], halo_low_ref[...])
    out_low_ref[...] = ((image - shift * x_ref[:wide, at].astype(jnp.float32)) / width).astype(jnp.bfloat16)
    image = image_ref[wide:, at] + mm(high_ref[...], halo_high_ref[...])
    out_high_ref[...] = ((image - shift * x_ref[wide:, at].astype(jnp.float32)) / width).astype(jnp.bfloat16)


def step(at, table, image, low, high, halo_low, halo_high, x):
    half = jax.ShapeDtypeStruct(halo_low.shape, jnp.bfloat16)
    return call(functools.partial(step_kernel, at), (half, half), [VMEM] * 7)(
        table, image, low, high, halo_low, halo_high, x)


def finish_kernel(at, table_ref, image_ref, low_ref, high_ref, halo_low_ref, halo_high_ref, s_low_ref, s_high_ref, x_ref, out_ref):
    wide = low_ref.shape[0]
    shift, width = table_ref[0:1, at], table_ref[1:2, at]
    live = table_ref[2:3, at] > 0.0

    def put(rows, image, s):
        value = 2.0 * (image - shift * s.astype(jnp.float32)) / width - x_ref[rows, at].astype(jnp.float32)
        out_ref[rows, :] = jnp.where(live, value, 0.0).astype(jnp.bfloat16)

    put(slice(0, wide), image_ref[:wide, :] + mm(low_ref[...], halo_low_ref[...]), s_low_ref[...])
    put(slice(wide, 2 * wide), image_ref[wide:, :] + mm(high_ref[...], halo_high_ref[...]), s_high_ref[...])


def finish(at, table, image, low, high, halo_low, halo_high, s_low, s_high, x):
    shape = jax.ShapeDtypeStruct(image.shape, jnp.bfloat16)
    return call(functools.partial(finish_kernel, at), shape, [VMEM] * 9)(
        table, image, low, high, halo_low, halo_high, s_low, s_high, x)


def early_kernel(*refs):
    *mine, out_ref = refs
    parts = [ref[...] for ref in mine]
    count = (len(parts) + 1) // 2
    own = jnp.concatenate(parts[:count], axis=1)
    out_ref[...] = tmm(own, jnp.concatenate(parts, axis=1))


def early_gram(parts):
    width = parts[0].shape[1]
    half = width * ((len(parts) + 1) // 2)
    shape = jax.ShapeDtypeStruct((half, width * len(parts)), jnp.float32)
    return call(early_kernel, shape, [VMEM] * len(parts))(*parts)


def code_kernel(share, early_ref, *refs):
    *mine, last_ref, out_ref = refs
    half = out_ref.shape[0]
    known = early_ref.shape[1]
    own = jnp.concatenate([ref[...] for ref in mine], axis=1)
    early = early_ref[...]
    late = tmm(own, last_ref[...])
    top = jnp.maximum(
        jnp.max(jnp.abs(early), axis=(0, 1), keepdims=True),
        jnp.max(jnp.abs(late), axis=(0, 1), keepdims=True),
    )
    e = jnp.clip(jnp.ceil(jnp.log2(jnp.maximum(top, 1e-36))) - 14.0, -100.0, 60.0)
    scale = jnp.exp2(-e)
    row = lax.broadcasted_iota(jnp.int32, (half, known), 0)
    col = lax.broadcasted_iota(jnp.int32, (half, known), 1)
    slot = (lax.rem(row, share) == 1) & (col == row - 1)
    out_ref[:, :known] = jnp.where(slot, e, early * scale)
    out_ref[:, known:] = late * scale


def code_terms(early, mine, last, share):
    half = early.shape[0]
    shape = jax.ShapeDtypeStruct((half, 2 * half), jnp.float32)
    return call(functools.partial(code_kernel, share), shape, [VMEM] * (2 + len(mine)))(
        early, *mine, last)


def read_code(value, slot):
    return jnp.sum(jnp.where(slot, value, 0.0), axis=(0, 1), keepdims=True)


def slots(head, half, start):
    row = lax.broadcasted_iota(jnp.int32, (head, half), 0)
    col = lax.broadcasted_iota(jnp.int32, (head, half), 1)
    return (row == 1) & (col == start), (row == 0) & (col == start + 1)


def pair_kernel(far, coded_ref, piece_ref, out_ref):
    share, half = out_ref.shape[0], out_ref.shape[1] // 2
    start = (lax.axis_index("row") ^ far) * share
    head = 8
    slot, _ = slots(head, half, start)
    here = coded_ref[pl.ds(pl.multiple_of(start, 8), share), :]
    there = piece_ref[...]
    e_here, e_there = read_code(here[:head, :half], slot), read_code(there[:head, :half], slot)
    e = jnp.maximum(e_here, e_there)
    total = here * jnp.exp2(e_here - e) + there * jnp.exp2(e_there - e)
    out_ref[...] = total
    out_ref[:head, :half] = jnp.where(slot, e, total[:head, :half])


def pair_terms(far, coded, piece):
    shape = jax.ShapeDtypeStruct(piece.shape, jnp.float32)
    return call(functools.partial(pair_kernel, far), shape, [VMEM] * 2)(coded, piece)


def sum_kernel(order_total, coded_ref, *refs):
    *pieces, out_ref = refs
    share, half = out_ref.shape[0], out_ref.shape[1] // 2
    me, sub = lax.axis_index("row"), lax.axis_index("sub")
    head = 8
    start = me * share
    slot, twin = slots(head, half, start)
    same = jnp.zeros((share, half), jnp.float32)
    cross = jnp.zeros((share, half), jnp.float32)
    here = coded_ref[pl.ds(pl.multiple_of(start, 8), share), :]
    for value in [here] + [ref[...] for ref in pieces]:
        scale = jnp.exp2(read_code(value[:head, :half], slot)) / order_total
        same += value[:, :half] * scale
        cross += value[:, half:] * scale
    lost = jnp.sum(jnp.where(twin, same[:head], 0.0), axis=(0, 1), keepdims=True)
    at = pl.ds(pl.multiple_of(sub * half, half), half)
    out_ref[:, at] = same
    out_ref[:head, at] = jnp.where(slot, lost, same[:head])
    out_ref[:, pl.ds(pl.multiple_of((1 - sub) * half, half), half)] = cross


def sum_terms(coded, pieces, order_total):
    shape = jax.ShapeDtypeStruct(pieces[0].shape, jnp.float32)
    return call(functools.partial(sum_kernel, order_total), shape, [VMEM] * (1 + len(pieces)))(coded, *pieces)


def gather_terms(coded, row_count, share):
    me = lax.axis_index("row")
    sent = coded.astype(jnp.float16)

    def send(piece, ring):
        return lax.ppermute(piece, "row", ring).astype(jnp.float32)

    def chunk(index):
        return lax.dynamic_slice_in_dim(sent, index * share, share, axis=0)

    if row_count != 4:
        return [
            send(chunk((me + shift) % row_count), [(i, (i + shift) % row_count) for i in range(row_count)])
            for shift in range(1, row_count)
        ]
    near = [(i, i ^ 1) for i in range(4)]
    onward = send(chunk(me ^ 3), near)
    kept = send(chunk(me ^ 1), near)
    pair = pair_terms(2, coded, onward)
    return [kept, send(pair.astype(jnp.float16), [(i, i ^ 2) for i in range(4)])]


def body(hop, pattern, vectors, counts, center, halfwidth):
    rows_dev = hop.shape[0]
    block = hop.shape[2]
    half = vectors.shape[2]
    row_count = lax.axis_size("row")
    total_blocks = rows_dev * row_count
    order_total = total_blocks * block
    wide = W * block
    piece = half // 2
    share = half // row_count
    forward = [(i, (i + 1) % row_count) for i in range(row_count)]
    backward = [(target, source) for source, target in forward]
    swap = [(0, 1), (1, 0)]
    sides = [slice(0, piece), slice(piece, half)]

    def from_sides(low, high):
        return lax.ppermute(high, "row", forward), lax.ppermute(low, "row", backward)

    x = vectors[0]
    halos = [from_sides(x[:wide, at], x[wide:, at]) for at in sides]
    low, own, high, image, table = band_parts(hop, pattern, counts, center, halfwidth, x, total_blocks)
    steps = [step(at, table, image, low, high, *halo, x) for at, halo in zip(sides, halos)]
    halos = [from_sides(*s) for s in steps]
    images = [mm(own[:, :wide], s[0]) + mm(own[:, wide:], s[1]) for s in steps]
    mine, other = [], []
    for at, second, halo, s in zip(sides, images, halos, steps):
        mine.append(finish(at, table, second, low, high, *halo, *s, x))
        other.append(lax.ppermute(mine[-1], "sub", swap))
    early = early_gram([*mine, other[0]])
    coded = code_terms(early, mine, other[1], share)
    margin = sum_terms(coded, gather_terms(coded, row_count, share), order_total)
    return margin.reshape(1, 1, share, 2 * half)


def solution(mesh):
    in_specs = (
        P(("groups", "row"), None, None, None),
        P(("groups", "row"), None),
        P("cuts", ("groups", "row"), "sub"),
        P(("groups", "cuts")),
        P(("groups", "cuts")),
        P(("groups", "cuts")),
    )
    out_specs = P(("groups", "cuts"), "sub", "row", None)
    return jax.shard_map(body, mesh=mesh, in_specs=in_specs, out_specs=out_specs, check_vma=False)
```

```python
import functools

import jax
import jax.numpy as jnp
from jax import lax
from jax.experimental import pallas as pl
from jax.experimental.pallas import tpu as pltpu
from jax.sharding import PartitionSpec as P

W = 3
LIMIT = 16 * 1024 * 1024
VMEM = pl.BlockSpec(memory_space=pltpu.VMEM)
SMEM = pl.BlockSpec(memory_space=pltpu.SMEM)


def call(kernel, out_shape, in_specs):
    return pl.pallas_call(
        kernel,
        out_shape=out_shape,
        in_specs=in_specs,
        out_specs=jax.tree.map(lambda _: VMEM, out_shape),
        compiler_params=pltpu.CompilerParams(vmem_limit_bytes=LIMIT),
        cost_estimate=pl.CostEstimate(flops=1000, bytes_accessed=1000, transcendentals=0),
    )


def mm(a, b):
    return jnp.dot(a, b, preferred_element_type=jnp.float32)


def tmm(a, b):
    return lax.dot_general(a, b, (((0,), (0,)), ((), ())), preferred_element_type=jnp.float32)


def side_of_low():
    return 1 - lax.rem(lax.axis_index("row"), 2)


def band_kernel(total_blocks, pattern_ref, counts_ref, center_ref, width_ref, hop_ref, xa_ref, xb_ref, halo_ref, own_ref, image_ref, table_ref):
    rows_dev, stored, block, _ = hop_ref.shape
    wide = W * block
    first_block = lax.axis_index("row") * rows_dev
    low = side_of_low()
    halo_ref[...] = jnp.zeros_like(halo_ref)
    own_ref[...] = jnp.zeros_like(own_ref)

    def place(r):
        side = jnp.where(r < W, low, 1 - low)
        return side * wide + jnp.where(r < W, r, r - W) * block

    for r in range(rows_dev):
        side = low if r < W else 1 - low
        inner = pl.ds((r % W) * block, block)
        outer = pl.ds(pl.multiple_of(side * wide + (r % W) * block, block), block)
        for k in range(stored):
            col = lax.rem(pattern_ref[r, k] - first_block + (W + total_blocks), total_blocks)
            tile = hop_ref[r, k]
            inside = (col >= W) & (col < W + rows_dev)

            @pl.when(inside)
            def _():
                own_ref[outer, pl.ds(pl.multiple_of(place(col - W), block), block)] = tile

            @pl.when(jnp.logical_not(inside))
            def _():
                at = jnp.where(col < W, col, col - W - rows_dev) * block
                halo_ref[side, inner, pl.ds(pl.multiple_of(at, block), block)] = tile

    image_ref[...] = mm(own_ref[:, :wide], xa_ref[...]) + mm(own_ref[:, wide:], xb_ref[...])
    half = xa_ref.shape[1]
    line = lax.broadcasted_iota(jnp.int32, (8, half), 0)
    column = lax.broadcasted_iota(jnp.int32, (8, half), 1) + lax.axis_index("sub") * half
    live = jnp.where(column < counts_ref[0], 1.0, 0.0)
    table_ref[...] = jnp.where(line == 0, center_ref[0], jnp.where(line == 1, width_ref[0], live))


def band_parts(hop, pattern, counts, center, halfwidth, xa, xb, total_blocks):
    rows_dev, _, block, _ = hop.shape
    wide, tall, half = W * block, rows_dev * block, xa.shape[1]
    return call(
        functools.partial(band_kernel, total_blocks),
        (
            jax.ShapeDtypeStruct((2, wide, wide), hop.dtype),
            jax.ShapeDtypeStruct((tall, tall), hop.dtype),
            jax.ShapeDtypeStruct((tall, half), jnp.float32),
            jax.ShapeDtypeStruct((8, half), jnp.float32),
        ),
        [SMEM] * 4 + [VMEM] * 3,
    )(pattern, counts, center, halfwidth, hop, xa, xb)


def step_kernel(side, table_ref, image_ref, band_ref, halo_ref, x_ref, out_ref):
    wide = x_ref.shape[0]
    shift, width = table_ref[0:1, :], table_ref[1:2, :]
    image = image_ref[side * wide:(side + 1) * wide, :] + mm(band_ref[side], halo_ref[...])
    out_ref[...] = ((image - shift * x_ref[...].astype(jnp.float32)) / width).astype(jnp.bfloat16)


def step(side, table, image, band, halo, x):
    shape = jax.ShapeDtypeStruct(x.shape, jnp.bfloat16)
    return call(functools.partial(step_kernel, side), shape, [VMEM] * 5)(table, image, band, halo, x)


def finish_kernel(side, table_ref, image_ref, band_ref, halo_ref, s_ref, x_ref, out_ref):
    wide = x_ref.shape[0]
    shift, width = table_ref[0:1, :], table_ref[1:2, :]
    live = table_ref[2:3, :] > 0.0
    image = image_ref[side * wide:(side + 1) * wide, :] + mm(band_ref[side], halo_ref[...])
    value = 2.0 * (image - shift * s_ref[...].astype(jnp.float32)) / width - x_ref[...].astype(jnp.float32)
    out_ref[...] = jnp.where(live, value, 0.0).astype(jnp.bfloat16)


def finish(side, table, image, band, halo, s, x):
    shape = jax.ShapeDtypeStruct(x.shape, jnp.bfloat16)
    return call(functools.partial(finish_kernel, side), shape, [VMEM] * 6)(table, image, band, halo, s, x)


def early_kernel(fa_ref, fb_ref, oa_ref, out_ref):
    half = fa_ref.shape[1]
    fa, fb = fa_ref[...], fb_ref[...]
    out_ref[:, :half] = tmm(fa, fa) + tmm(fb, fb)
    out_ref[:, half:] = tmm(fa, oa_ref[...])


def early_gram(fa, fb, oa):
    half = fa.shape[1]
    return call(early_kernel, jax.ShapeDtypeStruct((half, 2 * half), jnp.float32), [VMEM] * 3)(fa, fb, oa)


def code_kernel(share, early_ref, fb_ref, ob_ref, out_ref):
    half = fb_ref.shape[1]
    same = early_ref[:, :half]
    cross = early_ref[:, half:] + tmm(fb_ref[...], ob_ref[...])
    top = jnp.max(jnp.maximum(jnp.abs(same), jnp.abs(cross)), axis=(0, 1), keepdims=True)
    e = jnp.clip(jnp.ceil(jnp.log2(jnp.maximum(top, 1e-36))) - 14.0, -100.0, 60.0)
    scale = jnp.exp2(-e)
    row = lax.broadcasted_iota(jnp.int32, (half, half), 0)
    col = lax.broadcasted_iota(jnp.int32, (half, half), 1)
    slot = (lax.rem(row, share) == 1) & (col == row - 1)
    out_ref[:, :half] = jnp.where(slot, e, same * scale)
    out_ref[:, half:] = cross * scale


def code_terms(early, fb, ob, share):
    shape = jax.ShapeDtypeStruct(early.shape, jnp.float32)
    return call(functools.partial(code_kernel, share), shape, [VMEM] * 3)(early, fb, ob)


def read_code(value, slot):
    return jnp.sum(jnp.where(slot, value, 0.0), axis=(0, 1), keepdims=True)


def slots(head, half, start):
    row = lax.broadcasted_iota(jnp.int32, (head, half), 0)
    col = lax.broadcasted_iota(jnp.int32, (head, half), 1)
    return (row == 1) & (col == start), (row == 0) & (col == start + 1)


def sum_kernel(order_total, coded_ref, *refs):
    *pieces, out_ref = refs
    share, half = out_ref.shape[0], out_ref.shape[1] // 2
    me, sub = lax.axis_index("row"), lax.axis_index("sub")
    head = 8
    start = me * share
    slot, twin = slots(head, half, start)
    same = jnp.zeros((share, half), jnp.float32)
    cross = jnp.zeros((share, half), jnp.float32)
    here = coded_ref[pl.ds(pl.multiple_of(start, 8), share), :]
    for value in [here] + [ref[...] for ref in pieces]:
        scale = jnp.exp2(read_code(value[:head, :half], slot)) / order_total
        same += value[:, :half] * scale
        cross += value[:, half:] * scale
    lost = jnp.sum(jnp.where(twin, same[:head], 0.0), axis=(0, 1), keepdims=True)
    at = pl.ds(pl.multiple_of(sub * half, half), half)
    out_ref[:, at] = same
    out_ref[:head, at] = jnp.where(slot, lost, same[:head])
    out_ref[:, pl.ds(pl.multiple_of((1 - sub) * half, half), half)] = cross


def sum_terms(coded, pieces, order_total):
    shape = jax.ShapeDtypeStruct(pieces[0].shape, jnp.float32)
    return call(functools.partial(sum_kernel, order_total), shape, [VMEM] * (1 + len(pieces)))(coded, *pieces)


def gather_terms(coded, row_count, share):
    me = lax.axis_index("row")
    sent = coded.astype(jnp.float16)
    arrived = []
    for far in [*range(row_count // 2, row_count), *range(1, row_count // 2)]:
        piece = lax.dynamic_slice_in_dim(sent, (me ^ far) * share, share, axis=0)
        pairs = [(i, i ^ far) for i in range(row_count)]
        arrived.append(lax.ppermute(piece, "row", pairs).astype(jnp.float32))
    return arrived


def body(hop, pattern, vectors, counts, center, halfwidth):
    rows_dev = hop.shape[0]
    block = hop.shape[2]
    half = vectors.shape[2]
    row_count = lax.axis_size("row")
    total_blocks = rows_dev * row_count
    order_total = total_blocks * block
    wide = W * block
    share = half // row_count
    assert rows_dev == 2 * W and row_count & (row_count - 1) == 0
    next_door = [(i, i ^ 1) for i in range(row_count)]
    other_door = [(i, (i - 1 if i % 2 == 0 else i + 1) % row_count) for i in range(row_count)]
    swap = [(0, 1), (1, 0)]

    def exchange(a, b):
        return lax.ppermute(a, "row", next_door), lax.ppermute(b, "row", other_door)

    x = vectors[0]
    low = side_of_low()
    xa = lax.dynamic_slice_in_dim(x, low * wide, wide, axis=0)
    xb = lax.dynamic_slice_in_dim(x, (1 - low) * wide, wide, axis=0)
    halo_a, halo_b = exchange(xa, xb)
    band, own, image, table = band_parts(hop, pattern, counts, center, halfwidth, xa, xb, total_blocks)
    sa = step(0, table, image, band, halo_a, xa)
    sb = step(1, table, image, band, halo_b, xb)
    halo_a, halo_b = exchange(sa, sb)
    image = mm(own[:, :wide], sa) + mm(own[:, wide:], sb)
    fa = finish(0, table, image, band, halo_a, sa, xa)
    oa = lax.ppermute(fa, "sub", swap)
    fb = finish(1, table, image, band, halo_b, sb, xb)
    ob = lax.ppermute(fb, "sub", swap)
    coded = code_terms(early_gram(fa, fb, oa), fb, ob, share)
    margin = sum_terms(coded, gather_terms(coded, row_count, share), order_total)
    return margin.reshape(1, 1, share, 2 * half)


def solution(mesh):
    in_specs = (
        P(("groups", "row"), None, None, None),
        P(("groups", "row"), None),
        P("cuts", ("groups", "row"), "sub"),
        P(("groups", "cuts")),
        P(("groups", "cuts")),
        P(("groups", "cuts")),
    )
    out_specs = P(("groups", "cuts"), "sub", "row", None)
    return jax.shard_map(body, mesh=mesh, in_specs=in_specs, out_specs=out_specs, check_vma=False)
```

```python
import functools

import jax
import jax.numpy as jnp
from jax import lax
from jax.experimental import pallas as pl
from jax.experimental.pallas import tpu as pltpu
from jax.sharding import PartitionSpec as P

W = 3
TAIL = 8
LIMIT = 16 * 1024 * 1024
VMEM = pl.BlockSpec(memory_space=pltpu.VMEM)
SMEM = pl.BlockSpec(memory_space=pltpu.SMEM)


def call(kernel, out_shape, in_specs):
    return pl.pallas_call(
        kernel,
        out_shape=out_shape,
        in_specs=in_specs,
        out_specs=jax.tree.map(lambda _: VMEM, out_shape),
        compiler_params=pltpu.CompilerParams(vmem_limit_bytes=LIMIT),
        cost_estimate=pl.CostEstimate(flops=1000, bytes_accessed=1000, transcendentals=0),
    )


def mm(a, b):
    return jnp.dot(a, b, preferred_element_type=jnp.float32)


def tmm(a, b):
    return lax.dot_general(a, b, (((0,), (0,)), ((), ())), preferred_element_type=jnp.float32)


def side_of_low():
    return 1 - lax.rem(lax.axis_index("row"), 2)


def band_kernel(total_blocks, pattern_ref, counts_ref, center_ref, width_ref, hop_ref, xa_ref, xb_ref, halo_ref, own_ref, image_ref, table_ref):
    rows_dev, stored, block, _ = hop_ref.shape
    wide = W * block
    first_block = lax.axis_index("row") * rows_dev
    low = side_of_low()
    halo_ref[...] = jnp.zeros_like(halo_ref)
    own_ref[...] = jnp.zeros_like(own_ref)

    def place(r):
        side = jnp.where(r < W, low, 1 - low)
        return side * wide + jnp.where(r < W, r, r - W) * block

    for r in range(rows_dev):
        side = low if r < W else 1 - low
        inner = pl.ds((r % W) * block, block)
        outer = pl.ds(pl.multiple_of(side * wide + (r % W) * block, block), block)
        for k in range(stored):
            col = lax.rem(pattern_ref[r, k] - first_block + (W + total_blocks), total_blocks)
            tile = hop_ref[r, k]
            inside = (col >= W) & (col < W + rows_dev)

            @pl.when(inside)
            def _():
                own_ref[outer, pl.ds(pl.multiple_of(place(col - W), block), block)] = tile

            @pl.when(jnp.logical_not(inside))
            def _():
                at = jnp.where(col < W, col, col - W - rows_dev) * block
                halo_ref[side, inner, pl.ds(pl.multiple_of(at, block), block)] = tile

    image_ref[...] = mm(own_ref[:, :wide], xa_ref[...]) + mm(own_ref[:, wide:], xb_ref[...])
    half = xa_ref.shape[1]
    line = lax.broadcasted_iota(jnp.int32, (8, half), 0)
    column = lax.broadcasted_iota(jnp.int32, (8, half), 1) + lax.axis_index("sub") * half
    live = jnp.where(column < counts_ref[0], 1.0, 0.0)
    table_ref[...] = jnp.where(line == 0, center_ref[0], jnp.where(line == 1, width_ref[0], live))


def band_parts(hop, pattern, counts, center, halfwidth, xa, xb, total_blocks):
    rows_dev, _, block, _ = hop.shape
    wide, tall, half = W * block, rows_dev * block, xa.shape[1]
    return call(
        functools.partial(band_kernel, total_blocks),
        (
            jax.ShapeDtypeStruct((2, wide, wide), hop.dtype),
            jax.ShapeDtypeStruct((tall, tall), hop.dtype),
            jax.ShapeDtypeStruct((tall, half), jnp.float32),
            jax.ShapeDtypeStruct((8, half), jnp.float32),
        ),
        [SMEM] * 4 + [VMEM] * 3,
    )(pattern, counts, center, halfwidth, hop, xa, xb)


def step_kernel(side, table_ref, image_ref, band_ref, halo_ref, x_ref, out_ref):
    wide = x_ref.shape[0]
    shift, width = table_ref[0:1, :], table_ref[1:2, :]
    image = image_ref[side * wide:(side + 1) * wide, :] + mm(band_ref[side], halo_ref[...])
    out_ref[...] = ((image - shift * x_ref[...].astype(jnp.float32)) / width).astype(jnp.bfloat16)


def step(side, table, image, band, halo, x):
    shape = jax.ShapeDtypeStruct(x.shape, jnp.bfloat16)
    return call(functools.partial(step_kernel, side), shape, [VMEM] * 5)(table, image, band, halo, x)


def finish_kernel(side, table_ref, image_ref, band_ref, halo_ref, s_ref, x_ref, out_ref):
    wide = x_ref.shape[0]
    shift, width = table_ref[0:1, :], table_ref[1:2, :]
    live = table_ref[2:3, :] > 0.0
    image = image_ref[side * wide:(side + 1) * wide, :] + mm(band_ref[side], halo_ref[...])
    value = 2.0 * (image - shift * s_ref[...].astype(jnp.float32)) / width - x_ref[...].astype(jnp.float32)
    out_ref[...] = jnp.where(live, value, 0.0).astype(jnp.bfloat16)


def finish(side, table, image, band, halo, s, x):
    shape = jax.ShapeDtypeStruct(x.shape, jnp.bfloat16)
    return call(functools.partial(finish_kernel, side), shape, [VMEM] * 6)(table, image, band, halo, s, x)


def term_kernel(row_count, *refs):
    *mine, out_ref = refs
    count = len(mine) // 2
    total = sum(tmm(a[...], b[...]) for a, b in zip(mine[:count], mine[count:]))
    top = jnp.max(jnp.abs(total), axis=(0, 1), keepdims=True)
    e = jnp.clip(jnp.ceil(jnp.log2(jnp.maximum(top, 1e-36))) - 14.0, -100.0, 60.0)
    total = total * jnp.exp2(-e)
    half = total.shape[0]
    share = half // row_count
    bits = row_count.bit_length() - 1
    me = lax.axis_index("row")
    for r in range(row_count):
        at = 0
        for bit in range(bits):
            at = at + (((me >> bit) & 1) ^ ((r >> bit) & 1)) * (share << (bits - 1 - bit))
        out_ref[pl.ds(pl.multiple_of(at, 8), share), :] = total[r * share:(r + 1) * share, :]
    out_ref[half:, :] = jnp.broadcast_to(e, (TAIL, total.shape[1]))


def term(left, right, row_count):
    half = left[0].shape[1]
    shape = jax.ShapeDtypeStruct((half + TAIL, half), jnp.float32)
    return call(functools.partial(term_kernel, row_count), shape, [VMEM] * (2 * len(left)))(*left, *right)


def pair_kernel(here_ref, there_ref, out_ref):
    rows = out_ref.shape[0] - TAIL
    e_here = here_ref[2 * rows:2 * rows + 1, :]
    e_there = there_ref[rows:rows + 1, :]
    e = jnp.maximum(e_here, e_there)
    out_ref[:rows, :] = here_ref[:rows, :] * jnp.exp2(e_here - e) + there_ref[:rows, :] * jnp.exp2(e_there - e)
    out_ref[rows:, :] = jnp.broadcast_to(e, (TAIL, e.shape[1]))


def pair(here, there):
    return call(pair_kernel, jax.ShapeDtypeStruct(there.shape, jnp.float32), [VMEM] * 2)(here, there)


def last_kernel(order_total, *refs):
    *terms, out_ref = refs
    share, half = out_ref.shape[0], out_ref.shape[1] // 2
    sub = lax.axis_index("sub")
    for position, (here_ref, there_ref) in zip((sub, 1 - sub), (terms[:2], terms[2:])):
        total = here_ref[:share, :] * (jnp.exp2(here_ref[2 * share:2 * share + 1, :]) / order_total)
        total += there_ref[:share, :] * (jnp.exp2(there_ref[share:share + 1, :]) / order_total)
        out_ref[:, pl.ds(pl.multiple_of(position * half, half), half)] = total


def last(same, cross, order_total):
    rows, half = same[1].shape
    shape = jax.ShapeDtypeStruct((rows - TAIL, 2 * half), jnp.float32)
    return call(functools.partial(last_kernel, order_total), shape, [VMEM] * 4)(*same, *cross)


def after(value, other):
    return lax.optimization_barrier((value, other))[0]


def halving(same, cross_of, row_count):
    far = 1
    products = [same, None]
    while True:
        pairs = [(i, i ^ far) for i in range(row_count)]

        def send(coded):
            keep = (coded.shape[0] - TAIL) // 2
            return lax.ppermute(coded[keep:].astype(jnp.float16), "row", pairs)

        first = send(products[0])
        if far == 1:
            products[1] = cross_of()
        second = send(products[1])
        arrived = [after(first, products[1]).astype(jnp.float32), second.astype(jnp.float32)]
        far *= 2
        if far == row_count:
            return list(zip(products, arrived))
        products = [pair(here, there) for here, there in zip(products, arrived)]


def body(hop, pattern, vectors, counts, center, halfwidth):
    rows_dev = hop.shape[0]
    block = hop.shape[2]
    half = vectors.shape[2]
    row_count = lax.axis_size("row")
    total_blocks = rows_dev * row_count
    order_total = total_blocks * block
    wide = W * block
    share = half // row_count
    assert rows_dev == 2 * W and row_count & (row_count - 1) == 0
    next_door = [(i, i ^ 1) for i in range(row_count)]
    other_door = [(i, (i - 1 if i % 2 == 0 else i + 1) % row_count) for i in range(row_count)]
    swap = [(0, 1), (1, 0)]

    x = vectors[0]
    low = side_of_low()
    xa = lax.dynamic_slice_in_dim(x, low * wide, wide, axis=0)
    xb = lax.dynamic_slice_in_dim(x, (1 - low) * wide, wide, axis=0)
    halo_a = lax.ppermute(xa, "row", next_door)
    halo_b = lax.ppermute(xb, "row", other_door)
    band, own, image, table = band_parts(hop, pattern, counts, center, halfwidth, xa, xb, total_blocks)
    sa = step(0, table, image, band, halo_a, xa)
    next_a = lax.ppermute(sa, "row", next_door)
    sa, halo_b = lax.optimization_barrier((sa, halo_b))
    sb = step(1, table, image, band, halo_b, xb)
    next_b = lax.ppermute(sb, "row", other_door)
    image = mm(own[:, :wide], sa) + mm(own[:, wide:], sb)
    fa = finish(0, table, image, band, next_a, sa, xa)
    oa = lax.ppermute(fa, "sub", swap)
    fa, next_b = lax.optimization_barrier((fa, next_b))
    fb = finish(1, table, image, band, next_b, sb, xb)
    ob = lax.ppermute(fb, "sub", swap)
    same, cross = halving(
        term([fa, fb], [fa, fb], row_count), lambda: term([fa, fb], [oa, ob], row_count), row_count
    )
    margin = last(same, cross, order_total)
    return margin.reshape(1, 1, share, 2 * half)


def solution(mesh):
    in_specs = (
        P(("groups", "row"), None, None, None),
        P(("groups", "row"), None),
        P("cuts", ("groups", "row"), "sub"),
        P(("groups", "cuts")),
        P(("groups", "cuts")),
        P(("groups", "cuts")),
    )
    out_specs = P(("groups", "cuts"), "sub", "row", None)
    return jax.shard_map(body, mesh=mesh, in_specs=in_specs, out_specs=out_specs, check_vma=False)
```

```python
import functools

import jax
import jax.numpy as jnp
from jax import lax
from jax.experimental import pallas as pl
from jax.experimental.pallas import tpu as pltpu
from jax.sharding import PartitionSpec as P

W = 3
TAIL = 8
LIMIT = 16 * 1024 * 1024
COST = pl.CostEstimate(flops=1000, bytes_accessed=1000, transcendentals=0)
LONG = pl.CostEstimate(flops=20_000_000_000, bytes_accessed=1000, transcendentals=0)
VMEM = pl.BlockSpec(memory_space=pltpu.VMEM)
SMEM = pl.BlockSpec(memory_space=pltpu.SMEM)


def call(kernel, out_shape, in_specs, cost=COST):
    return pl.pallas_call(
        kernel,
        out_shape=out_shape,
        in_specs=in_specs,
        out_specs=jax.tree.map(lambda _: VMEM, out_shape),
        compiler_params=pltpu.CompilerParams(vmem_limit_bytes=LIMIT),
        cost_estimate=cost,
    )


def mm(a, b):
    return jnp.dot(a, b, preferred_element_type=jnp.float32)


def tmm(a, b):
    return lax.dot_general(a, b, (((0,), (0,)), ((), ())), preferred_element_type=jnp.float32)


def side_of_low():
    return 1 - lax.rem(lax.axis_index("row"), 2)


def band_kernel(total_blocks, counts_ref, center_ref, width_ref, pattern_ref, hop_ref, xa_ref, xb_ref, band_ref, image_ref, table_ref):
    rows_dev, stored, block, _ = hop_ref.shape
    wide = W * block
    first_block = lax.axis_index("row") * rows_dev
    low = side_of_low()
    band_ref[...] = jnp.zeros_like(band_ref)
    half = xa_ref.shape[1]
    line = lax.broadcasted_iota(jnp.int32, (8, half), 0)
    column = lax.broadcasted_iota(jnp.int32, (8, half), 1) + lax.axis_index("sub") * half
    live = jnp.where(column < counts_ref[0], 1.0, 0.0)
    table_ref[...] = jnp.where(line == 0, center_ref[0], jnp.where(line == 1, width_ref[0], live))
    for r in range(rows_dev):
        side = low if r < W else 1 - low
        rows = pl.ds(pl.multiple_of(side * wide + (r % W) * block, block), block)
        for k in range(stored):
            col = lax.rem(pattern_ref[r, k] - first_block + (W + total_blocks), total_blocks) - W
            in_low = jnp.logical_and(col >= 0, col < W)
            in_high = jnp.logical_and(col >= W, col < rows_dev)
            at = jnp.where(
                in_low, low * W + col,
                jnp.where(in_high, (1 - low) * W + col - W, 2 * W + jnp.where(col < 0, col + W, col - rows_dev)),
            )
            band_ref[rows, pl.ds(pl.multiple_of(at * block, block), block)] = hop_ref[r, k]
    image_ref[...] = mm(band_ref[:, :wide], xa_ref[...]) + mm(band_ref[:, wide:2 * wide], xb_ref[...])


def band_parts(hop, pattern, counts, center, halfwidth, xa, xb, total_blocks):
    rows_dev, _, block, _ = hop.shape
    wide, tall, half = W * block, rows_dev * block, xa.shape[1]
    return call(
        functools.partial(band_kernel, total_blocks),
        (
            jax.ShapeDtypeStruct((tall, 3 * wide), hop.dtype),
            jax.ShapeDtypeStruct((tall, half), jnp.float32),
            jax.ShapeDtypeStruct((8, half), jnp.float32),
        ),
        [SMEM] * 4 + [VMEM] * 3,
    )(counts, center, halfwidth, pattern, hop, xa, xb)


def halo_image(side, band_ref, image_ref, halo_ref):
    wide = halo_ref.shape[0]
    rows = slice(side * wide, (side + 1) * wide)
    return image_ref[rows, :] + mm(band_ref[rows, 2 * wide:], halo_ref[...])


def step_kernel(side, table_ref, image_ref, band_ref, halo_ref, x_ref, out_ref):
    shift, width = table_ref[0:1, :], table_ref[1:2, :]
    image = halo_image(side, band_ref, image_ref, halo_ref)
    out_ref[...] = ((image - shift * x_ref[...].astype(jnp.float32)) / width).astype(jnp.bfloat16)


def step(side, table, image, band, halo, x):
    shape = jax.ShapeDtypeStruct(x.shape, jnp.bfloat16)
    return call(functools.partial(step_kernel, side), shape, [VMEM] * 5)(table, image, band, halo, x)


def finish_kernel(side, table_ref, image_ref, band_ref, halo_ref, s_ref, x_ref, out_ref):
    shift, width = table_ref[0:1, :], table_ref[1:2, :]
    live = table_ref[2:3, :] > 0.0
    image = halo_image(side, band_ref, image_ref, halo_ref)
    value = 2.0 * (image - shift * s_ref[...].astype(jnp.float32)) / width - x_ref[...].astype(jnp.float32)
    out_ref[...] = jnp.where(live, value, 0.0).astype(jnp.bfloat16)


def finish(side, table, image, band, halo, s, x):
    shape = jax.ShapeDtypeStruct(x.shape, jnp.bfloat16)
    return call(functools.partial(finish_kernel, side), shape, [VMEM] * 6)(table, image, band, halo, s, x)


def exponent(*values):
    top = functools.reduce(jnp.maximum, [jnp.abs(value) for value in values])
    top = jnp.max(top, axis=(0, 1), keepdims=True)
    return jnp.clip(jnp.ceil(jnp.log2(jnp.maximum(top, 1e-36))) - 14.0, -100.0, 60.0)


def with_code(share, same, e):
    row = lax.broadcasted_iota(jnp.int32, same.shape, 0)
    col = lax.broadcasted_iota(jnp.int32, same.shape, 1)
    slot = (lax.rem(row, share) == 1) & (col == row - 1)
    return jnp.where(slot, e, same * jnp.exp2(-e))


def same_kernel(share, fa_ref, fb_ref, same_ref, coded_ref):
    fa, fb = fa_ref[...], fb_ref[...]
    same = tmm(fa, fa) + tmm(fb, fb)
    same_ref[...] = same
    coded_ref[...] = with_code(share, same, exponent(same))


def same_terms(fa, fb, share):
    half = fa.shape[1]
    shape = jax.ShapeDtypeStruct((half, half), jnp.float32)
    return call(functools.partial(same_kernel, share), (shape, shape), [VMEM] * 2)(fa, fb)


def both_kernel(share, same_ref, fa_ref, fb_ref, oa_ref, ob_ref, out_ref):
    half = fa_ref.shape[1]
    same = same_ref[...]
    cross = tmm(fa_ref[...], oa_ref[...]) + tmm(fb_ref[...], ob_ref[...])
    e = exponent(same, cross)
    out_ref[:half, :half] = with_code(share, same, e)
    out_ref[:half, half:] = cross * jnp.exp2(-e)
    out_ref[half:, :] = jnp.broadcast_to(e, (TAIL, 2 * half))


def both_terms(same, fa, fb, oa, ob, share):
    half = fa.shape[1]
    shape = jax.ShapeDtypeStruct((half + TAIL, 2 * half), jnp.float32)
    return call(functools.partial(both_kernel, share), shape, [VMEM] * 5)(same, fa, fb, oa, ob)


def slots(shape):
    start = lax.axis_index("row") * shape[0]
    row = lax.broadcasted_iota(jnp.int32, (8, shape[1]), 0)
    col = lax.broadcasted_iota(jnp.int32, (8, shape[1]), 1)
    return (row == 1) & (col == start), (row == 0) & (col == start + 1)


def slot_factor(ref, slot, order_total):
    e = jnp.sum(jnp.where(slot, ref[:8, :slot.shape[1]], 0.0), axis=(0, 1), keepdims=True)
    return jnp.exp2(e) / order_total


def first_sum_kernel(order_total, coded_ref, same_ref, cross_ref, out_ref):
    share, half = same_ref.shape
    slot, _ = slots((share, half))
    mine = pl.ds(pl.multiple_of(lax.axis_index("row") * share, 8), share)
    factor = jnp.exp2(coded_ref[half:half + 1, :half]) / order_total
    out_ref[:, :half] = coded_ref[mine, :half] * factor + same_ref[...] * slot_factor(same_ref, slot, order_total)
    there = cross_ref[:share, :] * (jnp.exp2(cross_ref[share:share + 1, :]) / order_total)
    out_ref[:, half:] = coded_ref[mine, half:] * factor + there


def first_sum(coded, same, cross, order_total):
    share, half = same.shape
    shape = jax.ShapeDtypeStruct((share, 2 * half), jnp.float32)
    return call(functools.partial(first_sum_kernel, order_total), shape, [VMEM] * 3, LONG)(coded, same, cross)


def sum_kernel(order_total, first_ref, *refs):
    *pieces, out_ref = refs
    share, half = out_ref.shape[0], out_ref.shape[1] // 2
    slot, twin = slots((share, half))
    same, cross = first_ref[:, :half], first_ref[:, half:]
    for ref in pieces:
        factor = slot_factor(ref, slot, order_total)
        same += ref[:, :half] * factor
        cross += ref[:, half:] * factor
    lost = jnp.sum(jnp.where(twin, same[:8], 0.0), axis=(0, 1), keepdims=True)
    sub = lax.axis_index("sub")
    at = pl.ds(pl.multiple_of(sub * half, half), half)
    out_ref[:, at] = same
    out_ref[:8, at] = jnp.where(slot, lost, same[:8])
    out_ref[:, pl.ds(pl.multiple_of((1 - sub) * half, half), half)] = cross


def sum_terms(first, pieces, order_total):
    shape = jax.ShapeDtypeStruct(first.shape, jnp.float32)
    return call(functools.partial(sum_kernel, order_total), shape, [VMEM] * (1 + len(pieces)))(first, *pieces)


def send(terms, far, row_count):
    pairs = [(i, i ^ far) for i in range(row_count)]
    return lax.ppermute(terms, "row", pairs)


def share_of(terms, far, share):
    at = (lax.axis_index("row") ^ far) * share
    return lax.dynamic_slice_in_dim(terms, at, share, axis=0)


def body(hop, pattern, vectors, counts, center, halfwidth):
    rows_dev = hop.shape[0]
    block = hop.shape[2]
    half = vectors.shape[2]
    row_count = lax.axis_size("row")
    total_blocks = rows_dev * row_count
    order_total = total_blocks * block
    wide = W * block
    share = half // row_count
    assert rows_dev == 2 * W and row_count & (row_count - 1) == 0
    next_door = [(i, i ^ 1) for i in range(row_count)]
    other_door = [(i, (i - 1 if i % 2 == 0 else i + 1) % row_count) for i in range(row_count)]
    swap = [(0, 1), (1, 0)]

    def exchange(a, b):
        return lax.ppermute(a, "row", next_door), lax.ppermute(b, "row", other_door)

    x = vectors[0]
    low = side_of_low()
    xa = lax.dynamic_slice_in_dim(x, low * wide, wide, axis=0)
    xb = lax.dynamic_slice_in_dim(x, (1 - low) * wide, wide, axis=0)
    halo_a, halo_b = exchange(xa, xb)
    band, image, table = band_parts(hop, pattern, counts, center, halfwidth, xa, xb, total_blocks)
    sa = step(0, table, image, band, halo_a, xa)
    sb = step(1, table, image, band, halo_b, xb)
    halo_a, halo_b = exchange(sa, sb)
    image = mm(band[:, :wide], sa) + mm(band[:, wide:2 * wide], sb)
    fa = finish(0, table, image, band, halo_a, sa, xa)
    oa = lax.ppermute(fa, "sub", swap)
    fb = finish(1, table, image, band, halo_b, sb, xb)
    ob = lax.ppermute(fb, "sub", swap)

    first, *others = [*range(row_count // 2, row_count), *range(1, row_count // 2)]
    same, coded = same_terms(fa, fb, share)
    same_there = send(share_of(coded.astype(jnp.float16), first, share), first, row_count)
    coded = both_terms(same, fa, fb, oa, ob, share)
    half_wide = coded.astype(jnp.float16)
    cross = jnp.concatenate([share_of(half_wide[:, half:], first, share), half_wide[half:, half:]], axis=0)
    cross_there = send(cross, first, row_count)
    pieces = [send(share_of(half_wide, far, share), far, row_count).astype(jnp.float32) for far in others]
    same_there, cross_there = lax.optimization_barrier((same_there, cross_there))
    same_there, cross_there = same_there.astype(jnp.float32), cross_there.astype(jnp.float32)
    margin = sum_terms(first_sum(coded, same_there, cross_there, order_total), pieces, order_total)
    return margin.reshape(1, 1, share, 2 * half)


def solution(mesh):
    in_specs = (
        P(("groups", "row"), None, None, None),
        P(("groups", "row"), None),
        P("cuts", ("groups", "row"), "sub"),
        P(("groups", "cuts")),
        P(("groups", "cuts")),
        P(("groups", "cuts")),
    )
    out_specs = P(("groups", "cuts"), "sub", "row", None)
    return jax.shard_map(body, mesh=mesh, in_specs=in_specs, out_specs=out_specs, check_vma=False)
```

```python
import functools

import jax
import jax.numpy as jnp
from jax import lax
from jax.experimental import pallas as pl
from jax.experimental.pallas import tpu as pltpu
from jax.sharding import PartitionSpec as P

W = 3
TAIL = 8
LIMIT = 16 * 1024 * 1024
COST = pl.CostEstimate(flops=1000, bytes_accessed=1000, transcendentals=0)
LONG = pl.CostEstimate(flops=20_000_000_000, bytes_accessed=1000, transcendentals=0)
VMEM = pl.BlockSpec(memory_space=pltpu.VMEM)
SMEM = pl.BlockSpec(memory_space=pltpu.SMEM)


def call(kernel, out_shape, in_specs, cost=COST):
    return pl.pallas_call(
        kernel,
        out_shape=out_shape,
        in_specs=in_specs,
        out_specs=jax.tree.map(lambda _: VMEM, out_shape),
        compiler_params=pltpu.CompilerParams(vmem_limit_bytes=LIMIT),
        cost_estimate=cost,
    )


def mm(a, b):
    return jnp.dot(a, b, preferred_element_type=jnp.float32)


def tmm(a, b):
    return lax.dot_general(a, b, (((0,), (0,)), ((), ())), preferred_element_type=jnp.float32)


def side_of_low():
    return 1 - lax.rem(lax.axis_index("row"), 2)


def band_kernel(total_blocks, counts_ref, center_ref, width_ref, pattern_ref, hop_ref, xa_ref, xb_ref, band_ref, image_ref, table_ref):
    rows_dev, stored, block, _ = hop_ref.shape
    wide = W * block
    first_block = lax.axis_index("row") * rows_dev
    low = side_of_low()
    band_ref[...] = jnp.zeros_like(band_ref)
    half = xa_ref.shape[1]
    line = lax.broadcasted_iota(jnp.int32, (8, half), 0)
    column = lax.broadcasted_iota(jnp.int32, (8, half), 1) + lax.axis_index("sub") * half
    live = jnp.where(column < counts_ref[0], 1.0, 0.0)
    table_ref[...] = jnp.where(line == 0, center_ref[0], jnp.where(line == 1, width_ref[0], live))
    for r in range(rows_dev):
        side = low if r < W else 1 - low
        rows = pl.ds(pl.multiple_of(side * wide + (r % W) * block, block), block)
        for k in range(stored):
            col = lax.rem(pattern_ref[r, k] - first_block + (W + total_blocks), total_blocks) - W
            in_low = jnp.logical_and(col >= 0, col < W)
            in_high = jnp.logical_and(col >= W, col < rows_dev)
            at = jnp.where(
                in_low, low * W + col,
                jnp.where(in_high, (1 - low) * W + col - W, 2 * W + jnp.where(col < 0, col + W, col - rows_dev)),
            )
            band_ref[rows, pl.ds(pl.multiple_of(at * block, block), block)] = hop_ref[r, k]
    image_ref[...] = mm(band_ref[:, :wide], xa_ref[...]) + mm(band_ref[:, wide:2 * wide], xb_ref[...])


def band_parts(hop, pattern, counts, center, halfwidth, xa, xb, total_blocks):
    rows_dev, _, block, _ = hop.shape
    wide, tall, half = W * block, rows_dev * block, xa.shape[1]
    return call(
        functools.partial(band_kernel, total_blocks),
        (
            jax.ShapeDtypeStruct((tall, 3 * wide), hop.dtype),
            jax.ShapeDtypeStruct((tall, half), jnp.float32),
            jax.ShapeDtypeStruct((8, half), jnp.float32),
        ),
        [SMEM] * 4 + [VMEM] * 3,
    )(counts, center, halfwidth, pattern, hop, xa, xb)


def halo_image(side, band_ref, image_ref, halo_ref):
    wide = halo_ref.shape[0]
    rows = slice(side * wide, (side + 1) * wide)
    return image_ref[rows, :] + mm(band_ref[rows, 2 * wide:], halo_ref[...])


def step_kernel(side, table_ref, image_ref, band_ref, halo_ref, x_ref, out_ref):
    shift, width = table_ref[0:1, :], table_ref[1:2, :]
    image = halo_image(side, band_ref, image_ref, halo_ref)
    out_ref[...] = ((image - shift * x_ref[...].astype(jnp.float32)) / width).astype(jnp.bfloat16)


def step(side, table, image, band, halo, x):
    shape = jax.ShapeDtypeStruct(x.shape, jnp.bfloat16)
    return call(functools.partial(step_kernel, side), shape, [VMEM] * 5)(table, image, band, halo, x)


def finish_kernel(side, table_ref, image_ref, band_ref, halo_ref, s_ref, x_ref, out_ref):
    shift, width = table_ref[0:1, :], table_ref[1:2, :]
    live = table_ref[2:3, :] > 0.0
    image = halo_image(side, band_ref, image_ref, halo_ref)
    value = 2.0 * (image - shift * s_ref[...].astype(jnp.float32)) / width - x_ref[...].astype(jnp.float32)
    out_ref[...] = jnp.where(live, value, 0.0).astype(jnp.bfloat16)


def finish(side, table, image, band, halo, s, x):
    shape = jax.ShapeDtypeStruct(x.shape, jnp.bfloat16)
    return call(functools.partial(finish_kernel, side), shape, [VMEM] * 6)(table, image, band, halo, s, x)


def exponent(*values):
    top = functools.reduce(jnp.maximum, [jnp.abs(value) for value in values])
    top = jnp.max(top, axis=(0, 1), keepdims=True)
    return jnp.clip(jnp.ceil(jnp.log2(jnp.maximum(top, 1e-36))) - 14.0, -100.0, 60.0)


def with_code(share, same, e):
    row = lax.broadcasted_iota(jnp.int32, same.shape, 0)
    col = lax.broadcasted_iota(jnp.int32, same.shape, 1)
    slot = (lax.rem(row, share) == 1) & (col == row - 1)
    return jnp.where(slot, e, same * jnp.exp2(-e))


def same_kernel(share, fa_ref, fb_ref, same_ref, coded_ref):
    fa, fb = fa_ref[...], fb_ref[...]
    same = tmm(fa, fa) + tmm(fb, fb)
    same_ref[...] = same
    coded_ref[...] = with_code(share, same, exponent(same))


def same_terms(fa, fb, share):
    half = fa.shape[1]
    shape = jax.ShapeDtypeStruct((half, half), jnp.float32)
    return call(functools.partial(same_kernel, share), (shape, shape), [VMEM] * 2)(fa, fb)


def both_kernel(share, same_ref, fa_ref, fb_ref, oa_ref, ob_ref, out_ref):
    half = fa_ref.shape[1]
    same = same_ref[...]
    cross = tmm(fa_ref[...], oa_ref[...]) + tmm(fb_ref[...], ob_ref[...])
    e = exponent(same, cross)
    out_ref[:half, :half] = with_code(share, same, e)
    out_ref[:half, half:] = cross * jnp.exp2(-e)
    out_ref[half:, :] = jnp.broadcast_to(e, (TAIL, 2 * half))


def both_terms(same, fa, fb, oa, ob, share):
    half = fa.shape[1]
    shape = jax.ShapeDtypeStruct((half + TAIL, 2 * half), jnp.float32)
    return call(functools.partial(both_kernel, share), shape, [VMEM] * 5)(same, fa, fb, oa, ob)


def slots(shape):
    start = lax.axis_index("row") * shape[0]
    row = lax.broadcasted_iota(jnp.int32, (8, shape[1]), 0)
    col = lax.broadcasted_iota(jnp.int32, (8, shape[1]), 1)
    return (row == 1) & (col == start), (row == 0) & (col == start + 1)


def slot_factor(ref, slot, order_total):
    e = jnp.sum(jnp.where(slot, ref[:8, :slot.shape[1]], 0.0), axis=(0, 1), keepdims=True)
    return jnp.exp2(e) / order_total


def first_sum_kernel(order_total, coded_ref, piece_ref, same_ref, out_ref):
    share, half = same_ref.shape
    slot, _ = slots((share, half))
    mine = pl.ds(pl.multiple_of(lax.axis_index("row") * share, 8), share)
    factor = jnp.exp2(coded_ref[half:half + 1, :half]) / order_total
    factor_there = slot_factor(piece_ref, slot, order_total)
    same = coded_ref[mine, :half] * factor + piece_ref[:, :half] * factor_there
    out_ref[:, :half] = same + same_ref[...] * slot_factor(same_ref, slot, order_total)
    out_ref[:, half:] = coded_ref[mine, half:] * factor + piece_ref[:, half:] * factor_there


def first_sum(coded, piece, same, order_total):
    shape = jax.ShapeDtypeStruct(piece.shape, jnp.float32)
    return call(functools.partial(first_sum_kernel, order_total), shape, [VMEM] * 3, LONG)(coded, piece, same)


def sum_kernel(order_total, first_ref, cross_ref, *refs):
    *pieces, out_ref = refs
    share, half = out_ref.shape[0], out_ref.shape[1] // 2
    slot, twin = slots((share, half))
    same, cross = first_ref[:, :half], first_ref[:, half:]
    cross += cross_ref[:share, :] * (jnp.exp2(cross_ref[share:share + 1, :]) / order_total)
    for ref in pieces:
        factor = slot_factor(ref, slot, order_total)
        same += ref[:, :half] * factor
        cross += ref[:, half:] * factor
    lost = jnp.sum(jnp.where(twin, same[:8], 0.0), axis=(0, 1), keepdims=True)
    sub = lax.axis_index("sub")
    at = pl.ds(pl.multiple_of(sub * half, half), half)
    out_ref[:, at] = same
    out_ref[:8, at] = jnp.where(slot, lost, same[:8])
    out_ref[:, pl.ds(pl.multiple_of((1 - sub) * half, half), half)] = cross


def sum_terms(first, cross, pieces, order_total):
    shape = jax.ShapeDtypeStruct(first.shape, jnp.float32)
    return call(functools.partial(sum_kernel, order_total), shape, [VMEM] * (2 + len(pieces)))(first, cross, *pieces)


def image_kernel(band_ref, sa_ref, sb_ref, out_ref):
    wide = sa_ref.shape[0]
    out_ref[...] = mm(band_ref[:, :wide], sa_ref[...]) + mm(band_ref[:, wide:2 * wide], sb_ref[...])


def own_image(band, sa, sb):
    shape = jax.ShapeDtypeStruct((band.shape[0], sa.shape[1]), jnp.float32)
    return call(image_kernel, shape, [VMEM] * 3)(band, sa, sb)


def send(terms, far, row_count):
    pairs = [(i, i ^ far) for i in range(row_count)]
    return lax.ppermute(terms, "row", pairs)


def share_of(terms, far, share):
    at = (lax.axis_index("row") ^ far) * share
    return lax.dynamic_slice_in_dim(terms, at, share, axis=0)


def body(hop, pattern, vectors, counts, center, halfwidth):
    rows_dev = hop.shape[0]
    block = hop.shape[2]
    half = vectors.shape[2]
    row_count = lax.axis_size("row")
    total_blocks = rows_dev * row_count
    order_total = total_blocks * block
    wide = W * block
    share = half // row_count
    assert rows_dev == 2 * W and row_count & (row_count - 1) == 0
    next_door = [(i, i ^ 1) for i in range(row_count)]
    other_door = [(i, (i - 1 if i % 2 == 0 else i + 1) % row_count) for i in range(row_count)]
    swap = [(0, 1), (1, 0)]

    def exchange(a, b):
        return lax.ppermute(a, "row", next_door), lax.ppermute(b, "row", other_door)

    x = vectors[0]
    low = side_of_low()
    xa = lax.dynamic_slice_in_dim(x, low * wide, wide, axis=0)
    xb = lax.dynamic_slice_in_dim(x, (1 - low) * wide, wide, axis=0)
    halo_a, halo_b = exchange(xa, xb)
    band, image, table = band_parts(hop, pattern, counts, center, halfwidth, xa, xb, total_blocks)
    sa = step(0, table, image, band, halo_a, xa)
    sb = step(1, table, image, band, halo_b, xb)
    halo_a, halo_b = exchange(sa, sb)
    image = own_image(band, sa, sb)
    fa = finish(0, table, image, band, halo_a, sa, xa)
    oa = lax.ppermute(fa, "sub", swap)
    fb = finish(1, table, image, band, halo_b, sb, xb)
    ob = lax.ppermute(fb, "sub", swap)

    first, *others = [*range(row_count // 2, row_count), *range(1, row_count // 2)]
    same, coded = same_terms(fa, fb, share)
    same_there = send(share_of(coded.astype(jnp.float16), first, share), first, row_count)
    coded = both_terms(same, fa, fb, oa, ob, share)
    half_wide = coded.astype(jnp.float16)
    cross = jnp.concatenate([share_of(half_wide[:, half:], first, share), half_wide[half:, half:]], axis=0)
    piece, *pieces = [send(share_of(half_wide, far, share), far, row_count) for far in others]
    cross_there = send(cross, first, row_count)
    same_there, piece = lax.optimization_barrier((same_there, piece))
    partial = first_sum(coded, piece.astype(jnp.float32), same_there.astype(jnp.float32), order_total)
    partial, cross_there, *pieces = lax.optimization_barrier((partial, cross_there, *pieces))
    margin = sum_terms(partial, cross_there.astype(jnp.float32), [p.astype(jnp.float32) for p in pieces], order_total)
    return margin.reshape(1, 1, share, 2 * half)


def solution(mesh):
    in_specs = (
        P(("groups", "row"), None, None, None),
        P(("groups", "row"), None),
        P("cuts", ("groups", "row"), "sub"),
        P(("groups", "cuts")),
        P(("groups", "cuts")),
        P(("groups", "cuts")),
    )
    out_specs = P(("groups", "cuts"), "sub", "row", None)
    return jax.shard_map(body, mesh=mesh, in_specs=in_specs, out_specs=out_specs, check_vma=False)
```

```python
import functools

import jax
import jax.numpy as jnp
from jax import lax
from jax.experimental import pallas as pl
from jax.experimental.pallas import tpu as pltpu
from jax.sharding import PartitionSpec as P

W = 3
TAIL = 8
LIMIT = 16 * 1024 * 1024
COST = pl.CostEstimate(flops=1000, bytes_accessed=1000, transcendentals=0)
LONG = pl.CostEstimate(flops=20_000_000_000, bytes_accessed=1000, transcendentals=0)
VMEM = pl.BlockSpec(memory_space=pltpu.VMEM)
SMEM = pl.BlockSpec(memory_space=pltpu.SMEM)


def call(kernel, out_shape, in_specs, cost=COST):
    return pl.pallas_call(
        kernel,
        out_shape=out_shape,
        in_specs=in_specs,
        out_specs=jax.tree.map(lambda _: VMEM, out_shape),
        compiler_params=pltpu.CompilerParams(vmem_limit_bytes=LIMIT),
        cost_estimate=cost,
    )


def mm(a, b):
    return jnp.dot(a, b, preferred_element_type=jnp.float32)


def tmm(a, b):
    return lax.dot_general(a, b, (((0,), (0,)), ((), ())), preferred_element_type=jnp.float32)


def side_of_low():
    return 1 - lax.rem(lax.axis_index("row"), 2)


def table_kernel(counts_ref, center_ref, width_ref, table_ref):
    half = table_ref.shape[1]
    line = lax.broadcasted_iota(jnp.int32, (8, half), 0)
    column = lax.broadcasted_iota(jnp.int32, (8, half), 1) + lax.axis_index("sub") * half
    live = jnp.where(column < counts_ref[0], 1.0, 0.0)
    table_ref[...] = jnp.where(line == 0, center_ref[0], jnp.where(line == 1, width_ref[0], live))


def table_of(counts, center, halfwidth, half):
    shape = jax.ShapeDtypeStruct((8, half), jnp.float32)
    return call(table_kernel, shape, [SMEM] * 3, LONG)(counts, center, halfwidth)


def band_kernel(total_blocks, table_ref, pattern_ref, hop_ref, *refs):
    *x_refs, band_ref, image_ref = refs
    rows_dev, stored, block, _ = hop_ref.shape
    wide = W * block
    first_block = lax.axis_index("row") * rows_dev
    low = side_of_low()
    band_ref[...] = jnp.zeros_like(band_ref)
    for r in range(rows_dev):
        side = low if r < W else 1 - low
        rows = pl.ds(pl.multiple_of(side * wide + (r % W) * block, block), block)
        for k in range(stored):
            col = lax.rem(pattern_ref[r, k] - first_block + (W + total_blocks), total_blocks) - W
            in_low = jnp.logical_and(col >= 0, col < W)
            in_high = jnp.logical_and(col >= W, col < rows_dev)
            at = jnp.where(
                in_low, low * W + col,
                jnp.where(in_high, (1 - low) * W + col - W, 2 * W + jnp.where(col < 0, col + W, col - rows_dev)),
            )
            band_ref[rows, pl.ds(pl.multiple_of(at * block, block), block)] = hop_ref[r, k]
    for p in range(len(x_refs) // 2):
        xa_ref, xb_ref = x_refs[2 * p:2 * p + 2]
        piece = xa_ref.shape[1]
        image_ref[:, p * piece:(p + 1) * piece] = (
            mm(band_ref[:, :wide], xa_ref[...]) + mm(band_ref[:, wide:2 * wide], xb_ref[...])
        )


def band_parts(table, hop, pattern, xs, total_blocks):
    rows_dev, _, block, _ = hop.shape
    wide, tall = W * block, rows_dev * block
    return call(
        functools.partial(band_kernel, total_blocks),
        (
            jax.ShapeDtypeStruct((tall, 3 * wide), hop.dtype),
            jax.ShapeDtypeStruct((tall, table.shape[1]), jnp.float32),
        ),
        [VMEM, SMEM] + [VMEM] * (1 + len(xs)),
    )(table, pattern, hop, *xs)


def step_kernel(side, at, table_ref, image_ref, band_ref, halo_ref, x_ref, out_ref):
    wide = halo_ref.shape[0]
    rows = slice(side * wide, (side + 1) * wide)
    shift, width = table_ref[0:1, at], table_ref[1:2, at]
    image = image_ref[rows, at] + mm(band_ref[rows, 2 * wide:], halo_ref[...])
    out_ref[...] = ((image - shift * x_ref[...].astype(jnp.float32)) / width).astype(jnp.bfloat16)


def step(side, at, table, image, band, halo, x):
    shape = jax.ShapeDtypeStruct(x.shape, jnp.bfloat16)
    return call(functools.partial(step_kernel, side, at), shape, [VMEM] * 5)(table, image, band, halo, x)


def finish_kernel(at, table_ref, image_ref, band_ref, *refs):
    *sides, out_ref = refs
    shift, width = table_ref[0:1, at], table_ref[1:2, at]
    live = table_ref[2:3, at] > 0.0
    for side in range(2):
        halo_ref, s_ref, x_ref = sides[3 * side:3 * side + 3]
        wide = halo_ref.shape[0]
        rows = slice(side * wide, (side + 1) * wide)
        image = image_ref[rows, :] + mm(band_ref[rows, 2 * wide:], halo_ref[...])
        value = 2.0 * (image - shift * s_ref[...].astype(jnp.float32)) / width - x_ref[...].astype(jnp.float32)
        out_ref[rows, :] = jnp.where(live, value, 0.0).astype(jnp.bfloat16)


def finish(at, table, image, band, side_a, side_b):
    shape = jax.ShapeDtypeStruct(image.shape, jnp.bfloat16)
    return call(functools.partial(finish_kernel, at), shape, [VMEM] * 9)(table, image, band, *side_a, *side_b)


def exponent(*values):
    top = functools.reduce(jnp.maximum, [jnp.abs(value) for value in values])
    top = jnp.max(top, axis=(0, 1), keepdims=True)
    return jnp.clip(jnp.ceil(jnp.log2(jnp.maximum(top, 1e-36))) - 14.0, -100.0, 60.0)


def with_code(share, same, e):
    row = lax.broadcasted_iota(jnp.int32, same.shape, 0)
    col = lax.broadcasted_iota(jnp.int32, same.shape, 1)
    slot = (lax.rem(row, share) == 1) & (col == row - 1)
    return jnp.where(slot, e, same * jnp.exp2(-e))


def joined(refs):
    return jnp.concatenate([ref[...] for ref in refs], axis=1)


def same_kernel(share, f0_ref, f1_ref, same_ref, coded_ref):
    own = joined([f0_ref, f1_ref])
    same = tmm(own, own)
    same_ref[...] = same
    coded_ref[...] = with_code(share, same, exponent(same))


def same_terms(f, share):
    half = 2 * f[0].shape[1]
    shape = jax.ShapeDtypeStruct((half, half), jnp.float32)
    return call(functools.partial(same_kernel, share), (shape, shape), [VMEM] * 2)(*f)


def both_kernel(share, same_ref, f0_ref, f1_ref, o0_ref, o1_ref, out_ref):
    same = same_ref[...]
    half = same.shape[0]
    cross = tmm(joined([f0_ref, f1_ref]), joined([o0_ref, o1_ref]))
    e = exponent(same, cross)
    out_ref[:half, :half] = with_code(share, same, e)
    out_ref[:half, half:] = cross * jnp.exp2(-e)
    out_ref[half:, :] = jnp.broadcast_to(e, (TAIL, 2 * half))


def both_terms(same, f, o, share):
    half = same.shape[0]
    shape = jax.ShapeDtypeStruct((half + TAIL, 2 * half), jnp.float32)
    return call(functools.partial(both_kernel, share), shape, [VMEM] * 5)(same, *f, *o)


def slots(shape):
    start = lax.axis_index("row") * shape[0]
    row = lax.broadcasted_iota(jnp.int32, (8, shape[1]), 0)
    col = lax.broadcasted_iota(jnp.int32, (8, shape[1]), 1)
    return (row == 1) & (col == start), (row == 0) & (col == start + 1)


def slot_factor(ref, slot, order_total):
    e = jnp.sum(jnp.where(slot, ref[:8, :slot.shape[1]], 0.0), axis=(0, 1), keepdims=True)
    return jnp.exp2(e) / order_total


def first_sum_kernel(order_total, coded_ref, piece_ref, same_ref, out_ref):
    share, half = same_ref.shape
    slot, _ = slots((share, half))
    mine = pl.ds(pl.multiple_of(lax.axis_index("row") * share, 8), share)
    factor = jnp.exp2(coded_ref[half:half + 1, :half]) / order_total
    factor_there = slot_factor(piece_ref, slot, order_total)
    same = coded_ref[mine, :half] * factor + piece_ref[:, :half] * factor_there
    out_ref[:, :half] = same + same_ref[...] * slot_factor(same_ref, slot, order_total)
    out_ref[:, half:] = coded_ref[mine, half:] * factor + piece_ref[:, half:] * factor_there


def first_sum(coded, piece, same, order_total):
    shape = jax.ShapeDtypeStruct(piece.shape, jnp.float32)
    return call(functools.partial(first_sum_kernel, order_total), shape, [VMEM] * 3, LONG)(coded, piece, same)


def sum_kernel(order_total, first_ref, cross_ref, *refs):
    *pieces, out_ref = refs
    share, half = out_ref.shape[0], out_ref.shape[1] // 2
    slot, twin = slots((share, half))
    same, cross = first_ref[:, :half], first_ref[:, half:]
    cross += cross_ref[:share, :] * (jnp.exp2(cross_ref[share:share + 1, :]) / order_total)
    for ref in pieces:
        factor = slot_factor(ref, slot, order_total)
        same += ref[:, :half] * factor
        cross += ref[:, half:] * factor
    lost = jnp.sum(jnp.where(twin, same[:8], 0.0), axis=(0, 1), keepdims=True)
    sub = lax.axis_index("sub")
    at = pl.ds(pl.multiple_of(sub * half, half), half)
    out_ref[:, at] = same
    out_ref[:8, at] = jnp.where(slot, lost, same[:8])
    out_ref[:, pl.ds(pl.multiple_of((1 - sub) * half, half), half)] = cross


def sum_terms(first, cross, pieces, order_total):
    shape = jax.ShapeDtypeStruct(first.shape, jnp.float32)
    return call(functools.partial(sum_kernel, order_total), shape, [VMEM] * (2 + len(pieces)))(first, cross, *pieces)


def image_kernel(band_ref, sa_ref, sb_ref, out_ref):
    wide = sa_ref.shape[0]
    out_ref[...] = mm(band_ref[:, :wide], sa_ref[...]) + mm(band_ref[:, wide:2 * wide], sb_ref[...])


def own_image(band, sa, sb):
    shape = jax.ShapeDtypeStruct((band.shape[0], sa.shape[1]), jnp.float32)
    return call(image_kernel, shape, [VMEM] * 3)(band, sa, sb)


def send(terms, far, row_count):
    pairs = [(i, i ^ far) for i in range(row_count)]
    return lax.ppermute(terms, "row", pairs)


def share_of(terms, far, share):
    at = (lax.axis_index("row") ^ far) * share
    return lax.dynamic_slice_in_dim(terms, at, share, axis=0)


def body(hop, pattern, vectors, counts, center, halfwidth):
    rows_dev = hop.shape[0]
    block = hop.shape[2]
    half = vectors.shape[2]
    row_count = lax.axis_size("row")
    total_blocks = rows_dev * row_count
    order_total = total_blocks * block
    wide = W * block
    share = half // row_count
    assert rows_dev == 2 * W and row_count & (row_count - 1) == 0
    next_door = [(i, i ^ 1) for i in range(row_count)]
    other_door = [(i, (i - 1 if i % 2 == 0 else i + 1) % row_count) for i in range(row_count)]
    swap = [(0, 1), (1, 0)]

    def exchange(a, b):
        return lax.ppermute(a, "row", next_door), lax.ppermute(b, "row", other_door)

    def after(value, other):
        return lax.optimization_barrier((value, other))[0]

    x = vectors[0]
    low = side_of_low()
    piece = half // 2
    columns = [slice(0, piece), slice(piece, half)]
    xs = [
        tuple(lax.dynamic_slice_in_dim(x[:, at], place * wide, wide, axis=0) for place in (low, 1 - low))
        for at in columns
    ]
    halos = [exchange(*pair) for pair in xs]
    table = table_of(counts, center, halfwidth, half)
    band, image = band_parts(table, hop, pattern, [v for pair in xs for v in pair], total_blocks)
    steps, nexts, last = [], [], None
    for at, (xa, xb), (halo_a, halo_b) in zip(columns, xs, halos):
        if last is not None:
            halo_b = after(halo_b, last)
        sb = step(1, at, table, image, band, halo_b, xb)
        sa = step(0, at, table, image, band, after(halo_a, sb), xa)
        last = sa
        steps.append((sa, sb))
        nexts.append(exchange(sa, sb))
    f, o = [], []
    for at, (xa, xb), (sa, sb), (halo_a, halo_b) in zip(columns, xs, steps, nexts):
        if f:
            halo_b = after(halo_b, f[0])
        second = own_image(band, sa, sb)
        f.append(finish(at, table, second, band, (halo_a, sa, xa), (halo_b, sb, xb)))
        o.append(lax.ppermute(f[-1], "sub", swap))

    first, *others = [*range(row_count // 2, row_count), *range(1, row_count // 2)]
    same, coded = same_terms(f, share)
    same_there = send(share_of(coded.astype(jnp.float16), first, share), first, row_count)
    coded = both_terms(same, f, o, share)
    half_wide = coded.astype(jnp.float16)
    cross = jnp.concatenate([share_of(half_wide[:, half:], first, share), half_wide[half:, half:]], axis=0)
    piece, *pieces = [send(share_of(half_wide, far, share), far, row_count) for far in others]
    cross_there = send(cross, first, row_count)
    same_there, piece = lax.optimization_barrier((same_there, piece))
    partial = first_sum(coded, piece.astype(jnp.float32), same_there.astype(jnp.float32), order_total)
    partial, cross_there, *pieces = lax.optimization_barrier((partial, cross_there, *pieces))
    margin = sum_terms(partial, cross_there.astype(jnp.float32), [p.astype(jnp.float32) for p in pieces], order_total)
    return margin.reshape(1, 1, share, 2 * half)


def solution(mesh):
    in_specs = (
        P(("groups", "row"), None, None, None),
        P(("groups", "row"), None),
        P("cuts", ("groups", "row"), "sub"),
        P(("groups", "cuts")),
        P(("groups", "cuts")),
        P(("groups", "cuts")),
    )
    out_specs = P(("groups", "cuts"), "sub", "row", None)
    return jax.shard_map(body, mesh=mesh, in_specs=in_specs, out_specs=out_specs, check_vma=False)
```

```python
import functools

import jax
import jax.numpy as jnp
from jax import lax
from jax.experimental import pallas as pl
from jax.experimental.pallas import tpu as pltpu
from jax.sharding import PartitionSpec as P

W = 3
TAIL = 8
LIMIT = 16 * 1024 * 1024
COST = pl.CostEstimate(flops=1000, bytes_accessed=1000, transcendentals=0)
LONG = pl.CostEstimate(flops=20_000_000_000, bytes_accessed=1000, transcendentals=0)
VMEM = pl.BlockSpec(memory_space=pltpu.VMEM)
SMEM = pl.BlockSpec(memory_space=pltpu.SMEM)


def call(kernel, out_shape, in_specs, cost=COST):
    return pl.pallas_call(
        kernel,
        out_shape=out_shape,
        in_specs=in_specs,
        out_specs=jax.tree.map(lambda _: VMEM, out_shape),
        compiler_params=pltpu.CompilerParams(vmem_limit_bytes=LIMIT),
        cost_estimate=cost,
    )


def mm(a, b):
    return jnp.dot(a, b, preferred_element_type=jnp.float32)


def tmm(a, b):
    return lax.dot_general(a, b, (((0,), (0,)), ((), ())), preferred_element_type=jnp.float32)


def side_of_low():
    return 1 - lax.rem(lax.axis_index("row"), 2)


def after(value, other):
    return lax.optimization_barrier((value, other))[0]


def ids_kernel(out_ref):
    out_ref[...] = lax.broadcasted_iota(jnp.int32, out_ref.shape, 1) + lax.axis_index("sub") * out_ref.shape[1]


def ids_of(half):
    return call(ids_kernel, jax.ShapeDtypeStruct((8, half), jnp.int32), [], LONG)()


def table_kernel(center_ref, width_ref, ids_ref, table_ref):
    line = lax.broadcasted_iota(jnp.int32, table_ref.shape, 0)
    table_ref[...] = jnp.where(line == 0, center_ref[0], width_ref[0])


def table_of(center, halfwidth, ids):
    shape = jax.ShapeDtypeStruct(ids.shape, jnp.float32)
    return call(table_kernel, shape, [SMEM] * 2 + [VMEM])(after(center, ids), after(halfwidth, ids), ids)


def live_kernel(counts_ref, ids_ref, live_ref):
    live_ref[...] = jnp.where(ids_ref[...] < counts_ref[0], 1.0, 0.0)


def live_of(counts, ids):
    return call(live_kernel, jax.ShapeDtypeStruct(ids.shape, jnp.float32), [SMEM, VMEM])(counts, ids)


def band_kernel(total_blocks, table_ref, pattern_ref, hop_ref, *refs):
    *x_refs, band_ref, image_ref = refs
    rows_dev, stored, block, _ = hop_ref.shape
    wide = W * block
    first_block = lax.axis_index("row") * rows_dev
    low = side_of_low()
    band_ref[...] = jnp.zeros_like(band_ref)
    for r in range(rows_dev):
        side = low if r < W else 1 - low
        rows = pl.ds(pl.multiple_of(side * wide + (r % W) * block, block), block)
        for k in range(stored):
            col = lax.rem(pattern_ref[r, k] - first_block + (W + total_blocks), total_blocks) - W
            in_low = jnp.logical_and(col >= 0, col < W)
            in_high = jnp.logical_and(col >= W, col < rows_dev)
            at = jnp.where(
                in_low, low * W + col,
                jnp.where(in_high, (1 - low) * W + col - W, 2 * W + jnp.where(col < 0, col + W, col - rows_dev)),
            )
            band_ref[rows, pl.ds(pl.multiple_of(at * block, block), block)] = hop_ref[r, k]
    for p in range(len(x_refs) // 2):
        xa_ref, xb_ref = x_refs[2 * p:2 * p + 2]
        piece = xa_ref.shape[1]
        image_ref[:, p * piece:(p + 1) * piece] = (
            mm(band_ref[:, :wide], xa_ref[...]) + mm(band_ref[:, wide:2 * wide], xb_ref[...])
        )


def band_parts(table, hop, pattern, xs, total_blocks):
    rows_dev, _, block, _ = hop.shape
    wide, tall = W * block, rows_dev * block
    return call(
        functools.partial(band_kernel, total_blocks),
        (
            jax.ShapeDtypeStruct((tall, 3 * wide), hop.dtype),
            jax.ShapeDtypeStruct((tall, table.shape[1]), jnp.float32),
        ),
        [VMEM, SMEM] + [VMEM] * (1 + len(xs)),
    )(table, pattern, hop, *xs)


def step_kernel(side, at, table_ref, image_ref, band_ref, halo_ref, x_ref, out_ref):
    wide = halo_ref.shape[0]
    rows = slice(side * wide, (side + 1) * wide)
    shift, width = table_ref[0:1, at], table_ref[1:2, at]
    image = image_ref[rows, at] + mm(band_ref[rows, 2 * wide:], halo_ref[...])
    out_ref[...] = ((image - shift * x_ref[...].astype(jnp.float32)) / width).astype(jnp.bfloat16)


def step(side, at, table, image, band, halo, x):
    shape = jax.ShapeDtypeStruct(x.shape, jnp.bfloat16)
    return call(functools.partial(step_kernel, side, at), shape, [VMEM] * 5)(table, image, band, halo, x)


def finish_kernel(at, table_ref, live_ref, image_ref, band_ref, *refs):
    *sides, out_ref = refs
    shift, width = table_ref[0:1, at], table_ref[1:2, at]
    live = live_ref[0:1, at] > 0.0
    for side in range(2):
        halo_ref, s_ref, x_ref = sides[3 * side:3 * side + 3]
        wide = halo_ref.shape[0]
        rows = slice(side * wide, (side + 1) * wide)
        image = image_ref[rows, :] + mm(band_ref[rows, 2 * wide:], halo_ref[...])
        value = 2.0 * (image - shift * s_ref[...].astype(jnp.float32)) / width - x_ref[...].astype(jnp.float32)
        out_ref[rows, :] = jnp.where(live, value, 0.0).astype(jnp.bfloat16)


def finish(at, table, live, image, band, side_a, side_b):
    shape = jax.ShapeDtypeStruct(image.shape, jnp.bfloat16)
    return call(functools.partial(finish_kernel, at), shape, [VMEM] * 10)(table, live, image, band, *side_a, *side_b)


def exponent(*values):
    top = functools.reduce(jnp.maximum, [jnp.abs(value) for value in values])
    top = jnp.max(top, axis=(0, 1), keepdims=True)
    return jnp.clip(jnp.ceil(jnp.log2(jnp.maximum(top, 1e-36))) - 14.0, -100.0, 60.0)


def with_code(share, same, e):
    row = lax.broadcasted_iota(jnp.int32, same.shape, 0)
    col = lax.broadcasted_iota(jnp.int32, same.shape, 1)
    slot = (lax.rem(row, share) == 1) & (col == row - 1)
    return jnp.where(slot, e, same * jnp.exp2(-e))


def joined(refs):
    return jnp.concatenate([ref[...] for ref in refs], axis=1)


def same_kernel(share, f0_ref, f1_ref, same_ref, coded_ref):
    own = joined([f0_ref, f1_ref])
    same = tmm(own, own)
    same_ref[...] = same
    coded_ref[...] = with_code(share, same, exponent(same))


def same_terms(f, share):
    half = 2 * f[0].shape[1]
    shape = jax.ShapeDtypeStruct((half, half), jnp.float32)
    return call(functools.partial(same_kernel, share), (shape, shape), [VMEM] * 2)(*f)


def both_kernel(share, same_ref, f0_ref, f1_ref, o0_ref, o1_ref, out_ref):
    same = same_ref[...]
    half = same.shape[0]
    cross = tmm(joined([f0_ref, f1_ref]), joined([o0_ref, o1_ref]))
    e = exponent(same, cross)
    out_ref[:half, :half] = with_code(share, same, e)
    out_ref[:half, half:] = cross * jnp.exp2(-e)
    out_ref[half:, :] = jnp.broadcast_to(e, (TAIL, 2 * half))


def both_terms(same, f, o, share):
    half = same.shape[0]
    shape = jax.ShapeDtypeStruct((half + TAIL, 2 * half), jnp.float32)
    return call(functools.partial(both_kernel, share), shape, [VMEM] * 5)(same, *f, *o)


def slots(shape):
    start = lax.axis_index("row") * shape[0]
    row = lax.broadcasted_iota(jnp.int32, (8, shape[1]), 0)
    col = lax.broadcasted_iota(jnp.int32, (8, shape[1]), 1)
    return (row == 1) & (col == start), (row == 0) & (col == start + 1)


def slot_factor(ref, slot, order_total):
    e = jnp.sum(jnp.where(slot, ref[:8, :slot.shape[1]], 0.0), axis=(0, 1), keepdims=True)
    return jnp.exp2(e) / order_total


def first_sum_kernel(order_total, coded_ref, piece_ref, same_ref, out_ref):
    share, half = same_ref.shape
    slot, _ = slots((share, half))
    mine = pl.ds(pl.multiple_of(lax.axis_index("row") * share, 8), share)
    factor = jnp.exp2(coded_ref[half:half + 1, :half]) / order_total
    factor_there = slot_factor(piece_ref, slot, order_total)
    same = coded_ref[mine, :half] * factor + piece_ref[:, :half] * factor_there
    out_ref[:, :half] = same + same_ref[...] * slot_factor(same_ref, slot, order_total)
    out_ref[:, half:] = coded_ref[mine, half:] * factor + piece_ref[:, half:] * factor_there


def first_sum(coded, piece, same, order_total):
    shape = jax.ShapeDtypeStruct(piece.shape, jnp.float32)
    return call(functools.partial(first_sum_kernel, order_total), shape, [VMEM] * 3, LONG)(coded, piece, same)


def sum_kernel(order_total, first_ref, cross_ref, *refs):
    *pieces, out_ref = refs
    share, half = out_ref.shape[0], out_ref.shape[1] // 2
    slot, twin = slots((share, half))
    same, cross = first_ref[:, :half], first_ref[:, half:]
    cross += cross_ref[:share, :] * (jnp.exp2(cross_ref[share:share + 1, :]) / order_total)
    for ref in pieces:
        factor = slot_factor(ref, slot, order_total)
        same += ref[:, :half] * factor
        cross += ref[:, half:] * factor
    lost = jnp.sum(jnp.where(twin, same[:8], 0.0), axis=(0, 1), keepdims=True)
    sub = lax.axis_index("sub")
    at = pl.ds(pl.multiple_of(sub * half, half), half)
    out_ref[:, at] = same
    out_ref[:8, at] = jnp.where(slot, lost, same[:8])
    out_ref[:, pl.ds(pl.multiple_of((1 - sub) * half, half), half)] = cross


def sum_terms(first, cross, pieces, order_total):
    shape = jax.ShapeDtypeStruct(first.shape, jnp.float32)
    return call(functools.partial(sum_kernel, order_total), shape, [VMEM] * (2 + len(pieces)))(first, cross, *pieces)


def image_kernel(band_ref, sa_ref, sb_ref, out_ref):
    wide = sa_ref.shape[0]
    out_ref[...] = mm(band_ref[:, :wide], sa_ref[...]) + mm(band_ref[:, wide:2 * wide], sb_ref[...])


def own_image(band, sa, sb):
    shape = jax.ShapeDtypeStruct((band.shape[0], sa.shape[1]), jnp.float32)
    return call(image_kernel, shape, [VMEM] * 3)(band, sa, sb)


def send(terms, far, row_count):
    pairs = [(i, i ^ far) for i in range(row_count)]
    return lax.ppermute(terms, "row", pairs)


def share_of(terms, far, share):
    at = (lax.axis_index("row") ^ far) * share
    return lax.dynamic_slice_in_dim(terms, at, share, axis=0)


def body(hop, pattern, vectors, counts, center, halfwidth):
    rows_dev = hop.shape[0]
    block = hop.shape[2]
    half = vectors.shape[2]
    row_count = lax.axis_size("row")
    total_blocks = rows_dev * row_count
    order_total = total_blocks * block
    wide = W * block
    share = half // row_count
    assert rows_dev == 2 * W and row_count & (row_count - 1) == 0
    next_door = [(i, i ^ 1) for i in range(row_count)]
    other_door = [(i, (i - 1 if i % 2 == 0 else i + 1) % row_count) for i in range(row_count)]
    swap = [(0, 1), (1, 0)]

    def exchange(a, b):
        return lax.ppermute(a, "row", next_door), lax.ppermute(b, "row", other_door)

    x = vectors[0]
    low = side_of_low()
    piece = half // 2
    columns = [slice(0, piece), slice(piece, half)]
    xs = [
        tuple(lax.dynamic_slice_in_dim(x[:, at], place * wide, wide, axis=0) for place in (low, 1 - low))
        for at in columns
    ]
    halos = [exchange(*pair) for pair in xs]
    ids = ids_of(half)
    table = table_of(center, halfwidth, ids)
    band, image = band_parts(table, hop, pattern, [v for pair in xs for v in pair], total_blocks)
    steps, nexts, last = [], [], None
    for at, (xa, xb), (halo_a, halo_b) in zip(columns, xs, halos):
        if last is not None:
            halo_b = after(halo_b, last)
        sb = step(1, at, table, image, band, halo_b, xb)
        sa = step(0, at, table, image, band, after(halo_a, sb), xa)
        last = sa
        steps.append((sa, sb))
        nexts.append(exchange(sa, sb))
    live = live_of(after(counts, steps[0][0]), ids)
    f, o = [], []
    for at, (xa, xb), (sa, sb), (halo_a, halo_b) in zip(columns, xs, steps, nexts):
        if f:
            halo_b = after(halo_b, f[0])
        second = own_image(band, sa, sb)
        f.append(finish(at, table, live, second, band, (halo_a, sa, xa), (halo_b, sb, xb)))
        o.append(lax.ppermute(f[-1], "sub", swap))

    first, *others = [*range(row_count // 2, row_count), *range(1, row_count // 2)]
    same, coded = same_terms(f, share)
    same_there = send(share_of(coded.astype(jnp.float16), first, share), first, row_count)
    coded = both_terms(same, f, o, share)
    half_wide = coded.astype(jnp.float16)
    cross = jnp.concatenate([share_of(half_wide[:, half:], first, share), half_wide[half:, half:]], axis=0)
    piece, *pieces = [send(share_of(half_wide, far, share), far, row_count) for far in others]
    cross_there = send(cross, first, row_count)
    same_there, piece = lax.optimization_barrier((same_there, piece))
    partial = first_sum(coded, piece.astype(jnp.float32), same_there.astype(jnp.float32), order_total)
    partial, cross_there, *pieces = lax.optimization_barrier((partial, cross_there, *pieces))
    margin = sum_terms(partial, cross_there.astype(jnp.float32), [p.astype(jnp.float32) for p in pieces], order_total)
    return margin.reshape(1, 1, share, 2 * half)


def solution(mesh):
    in_specs = (
        P(("groups", "row"), None, None, None),
        P(("groups", "row"), None),
        P("cuts", ("groups", "row"), "sub"),
        P(("groups", "cuts")),
        P(("groups", "cuts")),
        P(("groups", "cuts")),
    )
    out_specs = P(("groups", "cuts"), "sub", "row", None)
    return jax.shard_map(body, mesh=mesh, in_specs=in_specs, out_specs=out_specs, check_vma=False)
```

```python
import functools

import jax
import jax.numpy as jnp
from jax import lax
from jax.experimental import pallas as pl
from jax.experimental.pallas import tpu as pltpu
from jax.sharding import PartitionSpec as P

W = 3
TAIL = 8
LIMIT = 16 * 1024 * 1024
COST = pl.CostEstimate(flops=1000, bytes_accessed=1000, transcendentals=0)
LONG = pl.CostEstimate(flops=20_000_000_000, bytes_accessed=1000, transcendentals=0)
VMEM = pl.BlockSpec(memory_space=pltpu.VMEM)
SMEM = pl.BlockSpec(memory_space=pltpu.SMEM)


def call(kernel, out_shape, in_specs, cost=COST):
    return pl.pallas_call(
        kernel,
        out_shape=out_shape,
        in_specs=in_specs,
        out_specs=jax.tree.map(lambda _: VMEM, out_shape),
        compiler_params=pltpu.CompilerParams(vmem_limit_bytes=LIMIT),
        cost_estimate=cost,
    )


def mm(a, b):
    return jnp.dot(a, b, preferred_element_type=jnp.float32)


def tmm(a, b):
    return lax.dot_general(a, b, (((0,), (0,)), ((), ())), preferred_element_type=jnp.float32)


def side_of_low():
    return 1 - lax.rem(lax.axis_index("row"), 2)


def after(value, other):
    return lax.optimization_barrier((value, other))[0]


def ids_kernel(out_ref):
    out_ref[...] = lax.broadcasted_iota(jnp.int32, out_ref.shape, 1) + lax.axis_index("sub") * out_ref.shape[1]


def ids_of(half):
    return call(ids_kernel, jax.ShapeDtypeStruct((8, half), jnp.int32), [], LONG)()


def table_kernel(center_ref, width_ref, ids_ref, table_ref):
    line = lax.broadcasted_iota(jnp.int32, table_ref.shape, 0)
    table_ref[...] = jnp.where(line == 0, center_ref[0], width_ref[0])


def table_of(center, halfwidth, ids):
    shape = jax.ShapeDtypeStruct(ids.shape, jnp.float32)
    return call(table_kernel, shape, [SMEM] * 2 + [VMEM])(after(center, ids), after(halfwidth, ids), ids)


def live_kernel(counts_ref, ids_ref, live_ref):
    live_ref[...] = jnp.where(ids_ref[...] < counts_ref[0], 1.0, 0.0)


def live_of(counts, ids):
    return call(live_kernel, jax.ShapeDtypeStruct(ids.shape, jnp.float32), [SMEM, VMEM])(counts, ids)


def band_kernel(total_blocks, table_ref, pattern_ref, hop_ref, *refs):
    *x_refs, band_ref, image_ref = refs
    rows_dev, stored, block, _ = hop_ref.shape
    wide = W * block
    first_block = lax.axis_index("row") * rows_dev
    low = side_of_low()
    band_ref[...] = jnp.zeros_like(band_ref)
    for r in range(rows_dev):
        side = low if r < W else 1 - low
        rows = pl.ds(pl.multiple_of(side * wide + (r % W) * block, block), block)
        for k in range(stored):
            col = lax.rem(pattern_ref[r, k] - first_block + (W + total_blocks), total_blocks) - W
            in_low = jnp.logical_and(col >= 0, col < W)
            in_high = jnp.logical_and(col >= W, col < rows_dev)
            at = jnp.where(
                in_low, low * W + col,
                jnp.where(in_high, (1 - low) * W + col - W, 2 * W + jnp.where(col < 0, col + W, col - rows_dev)),
            )
            band_ref[rows, pl.ds(pl.multiple_of(at * block, block), block)] = hop_ref[r, k]
    for p in range(len(x_refs) // 2):
        xa_ref, xb_ref = x_refs[2 * p:2 * p + 2]
        piece = xa_ref.shape[1]
        image_ref[:, p * piece:(p + 1) * piece] = (
            mm(band_ref[:, :wide], xa_ref[...]) + mm(band_ref[:, wide:2 * wide], xb_ref[...])
        )


def band_parts(table, hop, pattern, xs, total_blocks):
    rows_dev, _, block, _ = hop.shape
    wide, tall = W * block, rows_dev * block
    return call(
        functools.partial(band_kernel, total_blocks),
        (
            jax.ShapeDtypeStruct((tall, 3 * wide), hop.dtype),
            jax.ShapeDtypeStruct((tall, table.shape[1]), jnp.float32),
        ),
        [VMEM, SMEM] + [VMEM] * (1 + len(xs)),
    )(table, pattern, hop, *xs)


def step_kernel(side, at, table_ref, image_ref, band_ref, halo_ref, x_ref, out_ref):
    wide = halo_ref.shape[0]
    rows = slice(side * wide, (side + 1) * wide)
    shift, width = table_ref[0:1, at], table_ref[1:2, at]
    image = image_ref[rows, at] + mm(band_ref[rows, 2 * wide:], halo_ref[...])
    out_ref[...] = ((image - shift * x_ref[...].astype(jnp.float32)) / width).astype(jnp.bfloat16)


def step(side, at, table, image, band, halo, x):
    shape = jax.ShapeDtypeStruct(x.shape, jnp.bfloat16)
    return call(functools.partial(step_kernel, side, at), shape, [VMEM] * 5)(table, image, band, halo, x)


def finish_kernel(at, table_ref, live_ref, image_ref, band_ref, *refs):
    *sides, out_ref = refs
    shift, width = table_ref[0:1, at], table_ref[1:2, at]
    live = live_ref[0:1, at] > 0.0
    for side in range(2):
        halo_ref, s_ref, x_ref = sides[3 * side:3 * side + 3]
        wide = halo_ref.shape[0]
        rows = slice(side * wide, (side + 1) * wide)
        image = image_ref[rows, :] + mm(band_ref[rows, 2 * wide:], halo_ref[...])
        value = 2.0 * (image - shift * s_ref[...].astype(jnp.float32)) / width - x_ref[...].astype(jnp.float32)
        out_ref[rows, :] = jnp.where(live, value, 0.0).astype(jnp.bfloat16)


def finish(at, table, live, image, band, side_a, side_b):
    shape = jax.ShapeDtypeStruct(image.shape, jnp.bfloat16)
    return call(functools.partial(finish_kernel, at), shape, [VMEM] * 10)(table, live, image, band, *side_a, *side_b)


def exponent(*values):
    top = functools.reduce(jnp.maximum, [jnp.abs(value) for value in values])
    top = jnp.max(top, axis=(0, 1), keepdims=True)
    return jnp.clip(jnp.ceil(jnp.log2(jnp.maximum(top, 1e-36))) - 14.0, -100.0, 60.0)


def with_code(share, same, e):
    row = lax.broadcasted_iota(jnp.int32, same.shape, 0)
    col = lax.broadcasted_iota(jnp.int32, same.shape, 1)
    slot = (lax.rem(row, share) == 1) & (col == row - 1)
    return jnp.where(slot, e, same * jnp.exp2(-e))


def joined(refs):
    return jnp.concatenate([ref[...] for ref in refs], axis=1)


def same_kernel(share, f0_ref, f1_ref, same_ref, coded_ref):
    own = joined([f0_ref, f1_ref])
    same = tmm(own, own)
    same_ref[...] = same
    coded_ref[...] = with_code(share, same, exponent(same))


def same_terms(f, share):
    half = 2 * f[0].shape[1]
    shape = jax.ShapeDtypeStruct((half, half), jnp.float32)
    return call(functools.partial(same_kernel, share), (shape, shape), [VMEM] * 2)(*f)


def both_kernel(share, same_ref, f0_ref, f1_ref, o0_ref, o1_ref, out_ref):
    same = same_ref[...]
    half = same.shape[0]
    cross = tmm(joined([f0_ref, f1_ref]), joined([o0_ref, o1_ref]))
    e = exponent(same, cross)
    out_ref[:half, :half] = with_code(share, same, e)
    out_ref[:half, half:] = cross * jnp.exp2(-e)
    out_ref[half:, :] = jnp.broadcast_to(e, (TAIL, 2 * half))


def both_terms(same, f, o, share):
    half = same.shape[0]
    shape = jax.ShapeDtypeStruct((half + TAIL, 2 * half), jnp.float32)
    return call(functools.partial(both_kernel, share), shape, [VMEM] * 5)(same, *f, *o)


def slots(shape):
    start = lax.axis_index("row") * shape[0]
    row = lax.broadcasted_iota(jnp.int32, (8, shape[1]), 0)
    col = lax.broadcasted_iota(jnp.int32, (8, shape[1]), 1)
    return (row == 1) & (col == start), (row == 0) & (col == start + 1)


def slot_factor(ref, slot, order_total):
    e = jnp.sum(jnp.where(slot, ref[:8, :slot.shape[1]], 0.0), axis=(0, 1), keepdims=True)
    return jnp.exp2(e) / order_total


def first_sum_kernel(order_total, coded_ref, piece_ref, same_ref, out_ref):
    share, half = same_ref.shape
    slot, _ = slots((share, half))
    mine = pl.ds(pl.multiple_of(lax.axis_index("row") * share, 8), share)
    factor = jnp.exp2(coded_ref[half:half + 1, :half]) / order_total
    factor_there = slot_factor(piece_ref, slot, order_total)
    same = coded_ref[mine, :half] * factor + piece_ref[:, :half] * factor_there
    out_ref[:, :half] = same + same_ref[...] * slot_factor(same_ref, slot, order_total)
    out_ref[:, half:] = coded_ref[mine, half:] * factor + piece_ref[:, half:] * factor_there


def first_sum(coded, piece, same, order_total):
    shape = jax.ShapeDtypeStruct(piece.shape, jnp.float32)
    return call(functools.partial(first_sum_kernel, order_total), shape, [VMEM] * 3, LONG)(coded, piece, same)


def sum_kernel(order_total, first_ref, cross_ref, *refs):
    *pieces, out_ref = refs
    share, half = out_ref.shape[0], out_ref.shape[1] // 2
    slot, twin = slots((share, half))
    same, cross = first_ref[:, :half], first_ref[:, half:]
    cross += cross_ref[:share, :] * (jnp.exp2(cross_ref[share:share + 1, :]) / order_total)
    for ref in pieces:
        factor = slot_factor(ref, slot, order_total)
        same += ref[:, :half] * factor
        cross += ref[:, half:] * factor
    lost = jnp.sum(jnp.where(twin, same[:8], 0.0), axis=(0, 1), keepdims=True)
    sub = lax.axis_index("sub")
    at = pl.ds(pl.multiple_of(sub * half, half), half)
    out_ref[:, at] = same
    out_ref[:8, at] = jnp.where(slot, lost, same[:8])
    out_ref[:, pl.ds(pl.multiple_of((1 - sub) * half, half), half)] = cross


def sum_terms(first, cross, pieces, order_total):
    shape = jax.ShapeDtypeStruct(first.shape, jnp.float32)
    return call(functools.partial(sum_kernel, order_total), shape, [VMEM] * (2 + len(pieces)))(first, cross, *pieces)


def image_kernel(sb_ref, sa_ref, band_ref, out_ref):
    wide = sa_ref.shape[0]
    out_ref[...] = mm(band_ref[:, :wide], sa_ref[...]) + mm(band_ref[:, wide:2 * wide], sb_ref[...])


def own_image(band, sa, sb):
    shape = jax.ShapeDtypeStruct((band.shape[0], sa.shape[1]), jnp.float32)
    return call(image_kernel, shape, [VMEM] * 3)(sb, sa, band)


def send(terms, far, row_count):
    pairs = [(i, i ^ far) for i in range(row_count)]
    return lax.ppermute(terms, "row", pairs)


def share_of(terms, far, share):
    at = (lax.axis_index("row") ^ far) * share
    return lax.dynamic_slice_in_dim(terms, at, share, axis=0)


def body(hop, pattern, vectors, counts, center, halfwidth):
    rows_dev = hop.shape[0]
    block = hop.shape[2]
    half = vectors.shape[2]
    row_count = lax.axis_size("row")
    total_blocks = rows_dev * row_count
    order_total = total_blocks * block
    wide = W * block
    share = half // row_count
    assert rows_dev == 2 * W and row_count & (row_count - 1) == 0
    next_door = [(i, i ^ 1) for i in range(row_count)]
    other_door = [(i, (i - 1 if i % 2 == 0 else i + 1) % row_count) for i in range(row_count)]
    swap = [(0, 1), (1, 0)]

    def exchange(a, b):
        return lax.ppermute(a, "row", next_door), lax.ppermute(b, "row", other_door)

    x = vectors[0]
    low = side_of_low()
    piece = half // 2
    columns = [slice(0, piece), slice(piece, half)]
    xs = [
        tuple(lax.dynamic_slice_in_dim(x[:, at], place * wide, wide, axis=0) for place in (low, 1 - low))
        for at in columns
    ]
    ids = ids_of(half)
    table = table_of(center, halfwidth, ids)
    halos = [exchange(after(xs[0][0], ids), xs[0][1]), exchange(*after(xs[1], table))]
    band, image = band_parts(table, hop, pattern, [v for pair in xs for v in pair], total_blocks)
    steps, nexts, last = [], [], None
    for at, (xa, xb), (halo_a, halo_b) in zip(columns, xs, halos):
        if last is not None:
            halo_b = after(halo_b, last)
        sb = step(1, at, table, image, band, halo_b, xb)
        sa = step(0, at, table, image, band, after(halo_a, sb), xa)
        last = sa
        steps.append((sa, sb))
        nexts.append(exchange(sa, sb))
    live = live_of(after(counts, steps[0][0]), ids)
    f, o = [], []
    for at, (xa, xb), (sa, sb), (halo_a, halo_b) in zip(columns, xs, steps, nexts):
        if f:
            halo_b = after(halo_b, f[0])
        second = own_image(band, sa, sb)
        f.append(finish(at, table, live, second, band, (halo_a, sa, xa), (halo_b, sb, xb)))
        o.append(lax.ppermute(f[-1], "sub", swap))

    first, *others = [*range(row_count // 2, row_count), *range(1, row_count // 2)]
    same, coded = same_terms(f, share)
    same_there = send(share_of(coded.astype(jnp.float16), first, share), first, row_count)
    coded = both_terms(same, f, o, share)
    half_wide = coded.astype(jnp.float16)
    cross = jnp.concatenate([share_of(half_wide[:, half:], first, share), half_wide[half:, half:]], axis=0)
    piece, *pieces = [send(share_of(half_wide, far, share), far, row_count) for far in others]
    cross_there = send(cross, first, row_count)
    same_there, piece = lax.optimization_barrier((same_there, piece))
    partial = first_sum(coded, piece.astype(jnp.float32), same_there.astype(jnp.float32), order_total)
    partial, cross_there, *pieces = lax.optimization_barrier((partial, cross_there, *pieces))
    margin = sum_terms(partial, cross_there.astype(jnp.float32), [p.astype(jnp.float32) for p in pieces], order_total)
    return margin.reshape(1, 1, share, 2 * half)


def solution(mesh):
    in_specs = (
        P(("groups", "row"), None, None, None),
        P(("groups", "row"), None),
        P("cuts", ("groups", "row"), "sub"),
        P(("groups", "cuts")),
        P(("groups", "cuts")),
        P(("groups", "cuts")),
    )
    out_specs = P(("groups", "cuts"), "sub", "row", None)
    return jax.shard_map(body, mesh=mesh, in_specs=in_specs, out_specs=out_specs, check_vma=False)
```

```python
import functools

import jax
import jax.numpy as jnp
from jax import lax
from jax.experimental import pallas as pl
from jax.experimental.pallas import tpu as pltpu
from jax.sharding import PartitionSpec as P

W = 3
TAIL = 8
LIMIT = 16 * 1024 * 1024
COST = pl.CostEstimate(flops=1000, bytes_accessed=1000, transcendentals=0)
LONG = pl.CostEstimate(flops=20_000_000_000, bytes_accessed=1000, transcendentals=0)
VMEM = pl.BlockSpec(memory_space=pltpu.VMEM)
SMEM = pl.BlockSpec(memory_space=pltpu.SMEM)


def call(kernel, out_shape, in_specs, cost=COST):
    return pl.pallas_call(
        kernel,
        out_shape=out_shape,
        in_specs=in_specs,
        out_specs=jax.tree.map(lambda _: VMEM, out_shape),
        compiler_params=pltpu.CompilerParams(vmem_limit_bytes=LIMIT),
        cost_estimate=cost,
    )


def mm(a, b):
    return jnp.dot(a, b, preferred_element_type=jnp.float32)


def tmm(a, b):
    return lax.dot_general(a, b, (((0,), (0,)), ((), ())), preferred_element_type=jnp.float32)


def side_of_low():
    return 1 - lax.rem(lax.axis_index("row"), 2)


def cut_kernel(x_any, xa_ref, xb_ref, sems):
    wide = xa_ref.shape[0]
    low = side_of_low()
    copies = [
        pltpu.make_async_copy(x_any.at[pl.ds(pl.multiple_of(place * wide, wide), wide)], ref, sems.at[i])
        for i, (place, ref) in enumerate([(1 - low, xb_ref), (low, xa_ref)])
    ]
    for copy in copies:
        copy.start()
    for copy in copies:
        copy.wait()


def cut_sides(x, wide):
    shape = jax.ShapeDtypeStruct((wide, x.shape[1]), x.dtype)
    return pl.pallas_call(
        cut_kernel,
        out_shape=(shape, shape),
        in_specs=[pl.BlockSpec(memory_space=pl.ANY)],
        out_specs=(VMEM, VMEM),
        scratch_shapes=[pltpu.SemaphoreType.DMA((2,))],
        cost_estimate=COST,
    )(x)


def band_kernel(total_blocks, counts_ref, center_ref, width_ref, pattern_ref, hop_ref, xa_ref, xb_ref, band_ref, image_ref, table_ref):
    rows_dev, stored, block, _ = hop_ref.shape
    wide = W * block
    first_block = lax.axis_index("row") * rows_dev
    low = side_of_low()
    band_ref[...] = jnp.zeros_like(band_ref)
    half = xa_ref.shape[1]
    line = lax.broadcasted_iota(jnp.int32, (8, half), 0)
    column = lax.broadcasted_iota(jnp.int32, (8, half), 1) + lax.axis_index("sub") * half
    live = jnp.where(column < counts_ref[0], 1.0, 0.0)
    table_ref[...] = jnp.where(line == 0, center_ref[0], jnp.where(line == 1, width_ref[0], live))
    for r in range(rows_dev):
        side = low if r < W else 1 - low
        rows = pl.ds(pl.multiple_of(side * wide + (r % W) * block, block), block)
        for k in range(stored):
            col = lax.rem(pattern_ref[r, k] - first_block + (W + total_blocks), total_blocks) - W
            in_low = jnp.logical_and(col >= 0, col < W)
            in_high = jnp.logical_and(col >= W, col < rows_dev)
            at = jnp.where(
                in_low, low * W + col,
                jnp.where(in_high, (1 - low) * W + col - W, 2 * W + jnp.where(col < 0, col + W, col - rows_dev)),
            )
            band_ref[rows, pl.ds(pl.multiple_of(at * block, block), block)] = hop_ref[r, k]
    image_ref[...] = mm(band_ref[:, :wide], xa_ref[...]) + mm(band_ref[:, wide:2 * wide], xb_ref[...])


def band_parts(hop, pattern, counts, center, halfwidth, xa, xb, total_blocks):
    rows_dev, _, block, _ = hop.shape
    wide, tall, half = W * block, rows_dev * block, xa.shape[1]
    return call(
        functools.partial(band_kernel, total_blocks),
        (
            jax.ShapeDtypeStruct((tall, 3 * wide), hop.dtype),
            jax.ShapeDtypeStruct((tall, half), jnp.float32),
            jax.ShapeDtypeStruct((8, half), jnp.float32),
        ),
        [SMEM] * 4 + [VMEM] * 3,
    )(counts, center, halfwidth, pattern, hop, xa, xb)


def halo_image(side, band_ref, image_ref, halo_ref):
    wide = halo_ref.shape[0]
    rows = slice(side * wide, (side + 1) * wide)
    return image_ref[rows, :] + mm(band_ref[rows, 2 * wide:], halo_ref[...])


def step_kernel(side, table_ref, image_ref, band_ref, halo_ref, x_ref, out_ref):
    shift, width = table_ref[0:1, :], table_ref[1:2, :]
    image = halo_image(side, band_ref, image_ref, halo_ref)
    out_ref[...] = ((image - shift * x_ref[...].astype(jnp.float32)) / width).astype(jnp.bfloat16)


def step(side, table, image, band, halo, x):
    shape = jax.ShapeDtypeStruct(x.shape, jnp.bfloat16)
    return call(functools.partial(step_kernel, side), shape, [VMEM] * 5)(table, image, band, halo, x)


def finish_kernel(side, table_ref, image_ref, band_ref, halo_ref, s_ref, x_ref, out_ref):
    shift, width = table_ref[0:1, :], table_ref[1:2, :]
    live = table_ref[2:3, :] > 0.0
    image = halo_image(side, band_ref, image_ref, halo_ref)
    value = 2.0 * (image - shift * s_ref[...].astype(jnp.float32)) / width - x_ref[...].astype(jnp.float32)
    out_ref[...] = jnp.where(live, value, 0.0).astype(jnp.bfloat16)


def finish(side, table, image, band, halo, s, x):
    shape = jax.ShapeDtypeStruct(x.shape, jnp.bfloat16)
    return call(functools.partial(finish_kernel, side), shape, [VMEM] * 6)(table, image, band, halo, s, x)


def exponent(*values):
    top = functools.reduce(jnp.maximum, [jnp.abs(value) for value in values])
    top = jnp.max(top, axis=(0, 1), keepdims=True)
    return jnp.clip(jnp.ceil(jnp.log2(jnp.maximum(top, 1e-36))) - 14.0, -100.0, 60.0)


def with_code(share, same, e):
    row = lax.broadcasted_iota(jnp.int32, same.shape, 0)
    col = lax.broadcasted_iota(jnp.int32, same.shape, 1)
    slot = (lax.rem(row, share) == 1) & (col == row - 1)
    return jnp.where(slot, e, same * jnp.exp2(-e))


def same_kernel(share, fa_ref, fb_ref, same_ref, coded_ref):
    fa, fb = fa_ref[...], fb_ref[...]
    same = tmm(fa, fa) + tmm(fb, fb)
    same_ref[...] = same
    coded_ref[...] = with_code(share, same, exponent(same))


def same_terms(fa, fb, share):
    half = fa.shape[1]
    shape = jax.ShapeDtypeStruct((half, half), jnp.float32)
    return call(functools.partial(same_kernel, share), (shape, shape), [VMEM] * 2)(fa, fb)


def both_kernel(share, same_ref, fa_ref, fb_ref, oa_ref, ob_ref, out_ref):
    half = fa_ref.shape[1]
    same = same_ref[...]
    cross = tmm(fa_ref[...], oa_ref[...]) + tmm(fb_ref[...], ob_ref[...])
    e = exponent(same, cross)
    out_ref[:half, :half] = with_code(share, same, e)
    out_ref[:half, half:] = cross * jnp.exp2(-e)
    out_ref[half:, :] = jnp.broadcast_to(e, (TAIL, 2 * half))


def both_terms(same, fa, fb, oa, ob, share):
    half = fa.shape[1]
    shape = jax.ShapeDtypeStruct((half + TAIL, 2 * half), jnp.float32)
    return call(functools.partial(both_kernel, share), shape, [VMEM] * 5)(same, fa, fb, oa, ob)


def slots(shape):
    start = lax.axis_index("row") * shape[0]
    row = lax.broadcasted_iota(jnp.int32, (8, shape[1]), 0)
    col = lax.broadcasted_iota(jnp.int32, (8, shape[1]), 1)
    return (row == 1) & (col == start), (row == 0) & (col == start + 1)


def slot_factor(ref, slot, order_total):
    e = jnp.sum(jnp.where(slot, ref[:8, :slot.shape[1]], 0.0), axis=(0, 1), keepdims=True)
    return jnp.exp2(e) / order_total


def first_sum_kernel(order_total, coded_ref, piece_ref, same_ref, out_ref):
    share, half = same_ref.shape
    slot, _ = slots((share, half))
    mine = pl.ds(pl.multiple_of(lax.axis_index("row") * share, 8), share)
    factor = jnp.exp2(coded_ref[half:half + 1, :half]) / order_total
    factor_there = slot_factor(piece_ref, slot, order_total)
    same = coded_ref[mine, :half] * factor + piece_ref[:, :half] * factor_there
    out_ref[:, :half] = same + same_ref[...] * slot_factor(same_ref, slot, order_total)
    out_ref[:, half:] = coded_ref[mine, half:] * factor + piece_ref[:, half:] * factor_there


def first_sum(coded, piece, same, order_total):
    shape = jax.ShapeDtypeStruct(piece.shape, jnp.float32)
    return call(functools.partial(first_sum_kernel, order_total), shape, [VMEM] * 3, LONG)(coded, piece, same)


def add_kernel(order_total, sum_ref, piece_ref, out_ref):
    share, columns = sum_ref.shape
    slot, _ = slots((share, columns // 2))
    out_ref[...] = sum_ref[...] + piece_ref[...] * slot_factor(piece_ref, slot, order_total)


def add_piece(total, piece, order_total):
    shape = jax.ShapeDtypeStruct(total.shape, jnp.float32)
    return call(functools.partial(add_kernel, order_total), shape, [VMEM] * 2, LONG)(total, piece)


def last_kernel(order_total, sum_ref, cross_ref, out_ref):
    share, half = out_ref.shape[0], out_ref.shape[1] // 2
    slot, twin = slots((share, half))
    sub = lax.axis_index("sub")
    at = pl.ds(pl.multiple_of(sub * half, half), half)
    out_ref[:, at] = sum_ref[:, :half]
    head = sum_ref[:8, :half]
    lost = jnp.sum(jnp.where(twin, head, 0.0), axis=(0, 1), keepdims=True)
    out_ref[:8, at] = jnp.where(slot, lost, head)
    factor = jnp.exp2(cross_ref[share:share + 1, :]) / order_total
    other = pl.ds(pl.multiple_of((1 - sub) * half, half), half)
    out_ref[:, other] = sum_ref[:, half:] + cross_ref[:share, :] * factor


def last_sum(total, cross, order_total):
    shape = jax.ShapeDtypeStruct(total.shape, jnp.float32)
    return call(functools.partial(last_kernel, order_total), shape, [VMEM] * 2)(total, cross)


def image_kernel(band_ref, sa_ref, sb_ref, out_ref):
    wide = sa_ref.shape[0]
    out_ref[...] = mm(band_ref[:, :wide], sa_ref[...]) + mm(band_ref[:, wide:2 * wide], sb_ref[...])


def own_image(band, sa, sb):
    shape = jax.ShapeDtypeStruct((band.shape[0], sa.shape[1]), jnp.float32)
    return call(image_kernel, shape, [VMEM] * 3)(band, sa, sb)


def send(terms, far, row_count):
    pairs = [(i, i ^ far) for i in range(row_count)]
    return lax.ppermute(terms, "row", pairs)


def share_of(terms, far, share):
    at = (lax.axis_index("row") ^ far) * share
    return lax.dynamic_slice_in_dim(terms, at, share, axis=0)


def body(hop, pattern, vectors, counts, center, halfwidth):
    rows_dev = hop.shape[0]
    block = hop.shape[2]
    half = vectors.shape[2]
    row_count = lax.axis_size("row")
    total_blocks = rows_dev * row_count
    order_total = total_blocks * block
    wide = W * block
    share = half // row_count
    assert rows_dev == 2 * W and row_count & (row_count - 1) == 0
    next_door = [(i, i ^ 1) for i in range(row_count)]
    other_door = [(i, (i - 1 if i % 2 == 0 else i + 1) % row_count) for i in range(row_count)]
    swap = [(0, 1), (1, 0)]

    def exchange(a, b):
        return lax.ppermute(a, "row", next_door), lax.ppermute(b, "row", other_door)

    x = vectors[0]
    xa, xb = cut_sides(x, wide)
    halo_a, halo_b = exchange(xa, xb)
    band, image, table = band_parts(hop, pattern, counts, center, halfwidth, xa, xb, total_blocks)
    sa = step(0, table, image, band, halo_a, xa)
    sb = step(1, table, image, band, halo_b, xb)
    halo_a, halo_b = exchange(sa, sb)
    image = own_image(band, sa, sb)
    fa = finish(0, table, image, band, halo_a, sa, xa)
    oa = lax.ppermute(fa, "sub", swap)
    fb = finish(1, table, image, band, halo_b, sb, xb)
    ob = lax.ppermute(fb, "sub", swap)

    first, *others = [1, *range(row_count - 1, 1, -1)]
    same, coded = same_terms(fa, fb, share)
    same_there = send(share_of(coded.astype(jnp.float16), first, share), first, row_count)
    coded = both_terms(same, fa, fb, oa, ob, share)
    half_wide = coded.astype(jnp.float16)
    cross = jnp.concatenate([share_of(half_wide[:, half:], first, share), half_wide[half:, half:]], axis=0)
    piece, *pieces = [send(share_of(half_wide, far, share), far, row_count) for far in others]
    cross_there = send(cross, first, row_count)
    same_there, piece = lax.optimization_barrier((same_there, piece))
    partial = first_sum(coded, piece.astype(jnp.float32), same_there.astype(jnp.float32), order_total)
    for piece in pieces:
        partial = add_piece(partial, piece.astype(jnp.float32), order_total)
    partial, cross_there = lax.optimization_barrier((partial, cross_there))
    margin = last_sum(partial, cross_there.astype(jnp.float32), order_total)
    return margin.reshape(1, 1, share, 2 * half)


def solution(mesh):
    in_specs = (
        P(("groups", "row"), None, None, None),
        P(("groups", "row"), None),
        P("cuts", ("groups", "row"), "sub"),
        P(("groups", "cuts")),
        P(("groups", "cuts")),
        P(("groups", "cuts")),
    )
    out_specs = P(("groups", "cuts"), "sub", "row", None)
    return jax.shard_map(body, mesh=mesh, in_specs=in_specs, out_specs=out_specs, check_vma=False)
```

```python
import functools

import jax
import jax.numpy as jnp
from jax import lax
from jax.experimental import pallas as pl
from jax.experimental.pallas import tpu as pltpu
from jax.sharding import PartitionSpec as P

W = 3
TAIL = 8
LIMIT = 16 * 1024 * 1024
COST = pl.CostEstimate(flops=1000, bytes_accessed=1000, transcendentals=0)
LONG = pl.CostEstimate(flops=20_000_000_000, bytes_accessed=1000, transcendentals=0)
VMEM = pl.BlockSpec(memory_space=pltpu.VMEM)
SMEM = pl.BlockSpec(memory_space=pltpu.SMEM)


def call(kernel, out_shape, in_specs, cost=COST):
    return pl.pallas_call(
        kernel,
        out_shape=out_shape,
        in_specs=in_specs,
        out_specs=jax.tree.map(lambda _: VMEM, out_shape),
        compiler_params=pltpu.CompilerParams(vmem_limit_bytes=LIMIT),
        cost_estimate=cost,
    )


def mm(a, b):
    return jnp.dot(a, b, preferred_element_type=jnp.float32)


def tmm(a, b):
    return lax.dot_general(a, b, (((0,), (0,)), ((), ())), preferred_element_type=jnp.float32)


def side_of_low():
    return 1 - lax.rem(lax.axis_index("row"), 2)


def band_kernel(total_blocks, counts_ref, center_ref, width_ref, pattern_ref, hop_ref, xa_ref, xb_ref, band_ref, image_ref, table_ref):
    rows_dev, stored, block, _ = hop_ref.shape
    wide = W * block
    first_block = lax.axis_index("row") * rows_dev
    low = side_of_low()
    band_ref[...] = jnp.zeros_like(band_ref)
    half = xa_ref.shape[1]
    line = lax.broadcasted_iota(jnp.int32, (8, half), 0)
    column = lax.broadcasted_iota(jnp.int32, (8, half), 1) + lax.axis_index("sub") * half
    live = jnp.where(column < counts_ref[0], 1.0, 0.0)
    table_ref[...] = jnp.where(line == 0, center_ref[0], jnp.where(line == 1, width_ref[0], live))
    for r in range(rows_dev):
        side = low if r < W else 1 - low
        rows = pl.ds(pl.multiple_of(side * wide + (r % W) * block, block), block)
        for k in range(stored):
            col = lax.rem(pattern_ref[r, k] - first_block + (W + total_blocks), total_blocks) - W
            in_low = jnp.logical_and(col >= 0, col < W)
            in_high = jnp.logical_and(col >= W, col < rows_dev)
            at = jnp.where(
                in_low, low * W + col,
                jnp.where(in_high, (1 - low) * W + col - W, 2 * W + jnp.where(col < 0, col + W, col - rows_dev)),
            )
            band_ref[rows, pl.ds(pl.multiple_of(at * block, block), block)] = hop_ref[r, k]
    image_ref[...] = mm(band_ref[:, :wide], xa_ref[...]) + mm(band_ref[:, wide:2 * wide], xb_ref[...])


def band_parts(hop, pattern, counts, center, halfwidth, xa, xb, total_blocks):
    rows_dev, _, block, _ = hop.shape
    wide, tall, half = W * block, rows_dev * block, xa.shape[1]
    return call(
        functools.partial(band_kernel, total_blocks),
        (
            jax.ShapeDtypeStruct((tall, 3 * wide), hop.dtype),
            jax.ShapeDtypeStruct((tall, half), jnp.float32),
            jax.ShapeDtypeStruct((8, half), jnp.float32),
        ),
        [SMEM] * 4 + [VMEM] * 3,
    )(counts, center, halfwidth, pattern, hop, xa, xb)


def halo_image(side, band_ref, image_ref, halo_ref):
    wide = halo_ref.shape[0]
    rows = slice(side * wide, (side + 1) * wide)
    return image_ref[rows, :] + mm(band_ref[rows, 2 * wide:], halo_ref[...])


def step_kernel(side, table_ref, image_ref, band_ref, halo_ref, x_ref, out_ref):
    shift, width = table_ref[0:1, :], table_ref[1:2, :]
    image = halo_image(side, band_ref, image_ref, halo_ref)
    out_ref[...] = ((image - shift * x_ref[...].astype(jnp.float32)) / width).astype(jnp.bfloat16)


def step(side, table, image, band, halo, x):
    shape = jax.ShapeDtypeStruct(x.shape, jnp.bfloat16)
    return call(functools.partial(step_kernel, side), shape, [VMEM] * 5)(table, image, band, halo, x)


def finish_kernel(side, table_ref, image_ref, band_ref, halo_ref, s_ref, x_ref, out_ref):
    shift, width = table_ref[0:1, :], table_ref[1:2, :]
    live = table_ref[2:3, :] > 0.0
    image = halo_image(side, band_ref, image_ref, halo_ref)
    value = 2.0 * (image - shift * s_ref[...].astype(jnp.float32)) / width - x_ref[...].astype(jnp.float32)
    out_ref[...] = jnp.where(live, value, 0.0).astype(jnp.bfloat16)


def finish(side, table, image, band, halo, s, x):
    shape = jax.ShapeDtypeStruct(x.shape, jnp.bfloat16)
    return call(functools.partial(finish_kernel, side), shape, [VMEM] * 6)(table, image, band, halo, s, x)


def exponent(*values):
    top = functools.reduce(jnp.maximum, [jnp.abs(value) for value in values])
    top = jnp.max(top, axis=(0, 1), keepdims=True)
    return jnp.clip(jnp.ceil(jnp.log2(jnp.maximum(top, 1e-36))) - 14.0, -100.0, 60.0)


def with_code(share, same, e):
    row = lax.broadcasted_iota(jnp.int32, same.shape, 0)
    col = lax.broadcasted_iota(jnp.int32, same.shape, 1)
    slot = (lax.rem(row, share) == 1) & (col == row - 1)
    return jnp.where(slot, e, same * jnp.exp2(-e))


def same_kernel(share, fa_ref, fb_ref, same_ref, coded_ref):
    fa, fb = fa_ref[...], fb_ref[...]
    same = tmm(fa, fa) + tmm(fb, fb)
    same_ref[...] = same
    coded_ref[...] = with_code(share, same, exponent(same))


def same_terms(fa, fb, share):
    half = fa.shape[1]
    shape = jax.ShapeDtypeStruct((half, half), jnp.float32)
    return call(functools.partial(same_kernel, share), (shape, shape), [VMEM] * 2)(fa, fb)


def both_kernel(share, same_ref, fa_ref, fb_ref, oa_ref, ob_ref, out_ref):
    half = fa_ref.shape[1]
    same = same_ref[...]
    cross = tmm(fa_ref[...], oa_ref[...]) + tmm(fb_ref[...], ob_ref[...])
    e = exponent(same, cross)
    same, cross = with_code(share, same, e), cross * jnp.exp2(-e)
    for r in range(half // share):
        rows, at = slice(r * share, (r + 1) * share), r * (share + TAIL)
        out_ref[at:at + share, :half] = same[rows]
        out_ref[at:at + share, half:] = cross[rows]
        out_ref[at + share:at + share + TAIL, :] = jnp.broadcast_to(e, (TAIL, 2 * half))


def both_terms(same, fa, fb, oa, ob, share):
    half = fa.shape[1]
    shape = jax.ShapeDtypeStruct((half // share * (share + TAIL), 2 * half), jnp.float32)
    return call(functools.partial(both_kernel, share), shape, [VMEM] * 5)(same, fa, fb, oa, ob)


def slots(shape):
    start = lax.axis_index("row") * shape[0]
    row = lax.broadcasted_iota(jnp.int32, (8, shape[1]), 0)
    col = lax.broadcasted_iota(jnp.int32, (8, shape[1]), 1)
    return (row == 1) & (col == start), (row == 0) & (col == start + 1)


def slot_factor(ref, slot, order_total):
    e = jnp.sum(jnp.where(slot, ref[:8, :slot.shape[1]], 0.0), axis=(0, 1), keepdims=True)
    return jnp.exp2(e) / order_total


def first_sum_kernel(order_total, coded_ref, piece_ref, same_ref, out_ref):
    share, half = same_ref.shape
    slot, _ = slots((share, half))
    mine = pl.ds(pl.multiple_of(lax.axis_index("row") * (share + TAIL), 8), share)
    factor = jnp.exp2(coded_ref[share:share + 1, :half]) / order_total
    factor_there = slot_factor(piece_ref, slot, order_total)
    same = coded_ref[mine, :half] * factor + piece_ref[:, :half] * factor_there
    out_ref[:, :half] = same + same_ref[...] * slot_factor(same_ref, slot, order_total)
    out_ref[:, half:] = coded_ref[mine, half:] * factor + piece_ref[:, half:] * factor_there


def first_sum(coded, piece, same, order_total):
    shape = jax.ShapeDtypeStruct(piece.shape, jnp.float32)
    return call(functools.partial(first_sum_kernel, order_total), shape, [VMEM] * 3, LONG)(coded, piece, same)


def add_kernel(order_total, sum_ref, piece_ref, out_ref):
    share, columns = sum_ref.shape
    slot, _ = slots((share, columns // 2))
    out_ref[...] = sum_ref[...] + piece_ref[...] * slot_factor(piece_ref, slot, order_total)


def add_piece(total, piece, order_total):
    shape = jax.ShapeDtypeStruct(total.shape, jnp.float32)
    return call(functools.partial(add_kernel, order_total), shape, [VMEM] * 2, LONG)(total, piece)


def last_kernel(order_total, sum_ref, cross_ref, out_ref):
    share, half = out_ref.shape[0], out_ref.shape[1] // 2
    slot, twin = slots((share, half))
    sub = lax.axis_index("sub")
    at = pl.ds(pl.multiple_of(sub * half, half), half)
    out_ref[:, at] = sum_ref[:, :half]
    head = sum_ref[:8, :half]
    lost = jnp.sum(jnp.where(twin, head, 0.0), axis=(0, 1), keepdims=True)
    out_ref[:8, at] = jnp.where(slot, lost, head)
    factor = jnp.exp2(cross_ref[share:share + 1, :]) / order_total
    other = pl.ds(pl.multiple_of((1 - sub) * half, half), half)
    out_ref[:, other] = sum_ref[:, half:] + cross_ref[:share, :] * factor


def last_sum(total, cross, order_total):
    shape = jax.ShapeDtypeStruct(total.shape, jnp.float32)
    return call(functools.partial(last_kernel, order_total), shape, [VMEM] * 2)(total, cross)


def image_kernel(band_ref, sa_ref, sb_ref, out_ref):
    wide = sa_ref.shape[0]
    out_ref[...] = mm(band_ref[:, :wide], sa_ref[...]) + mm(band_ref[:, wide:2 * wide], sb_ref[...])


def own_image(band, sa, sb):
    shape = jax.ShapeDtypeStruct((band.shape[0], sa.shape[1]), jnp.float32)
    return call(image_kernel, shape, [VMEM] * 3)(band, sa, sb)


def send(terms, far, row_count):
    pairs = [(i, i ^ far) for i in range(row_count)]
    return lax.ppermute(terms, "row", pairs)


def share_of(terms, far, rows, pitch):
    at = (lax.axis_index("row") ^ far) * pitch
    return lax.dynamic_slice_in_dim(terms, at, rows, axis=0)


def body(hop, pattern, vectors, counts, center, halfwidth):
    rows_dev = hop.shape[0]
    block = hop.shape[2]
    half = vectors.shape[2]
    row_count = lax.axis_size("row")
    total_blocks = rows_dev * row_count
    order_total = total_blocks * block
    wide = W * block
    share = half // row_count
    assert rows_dev == 2 * W and row_count & (row_count - 1) == 0
    next_door = [(i, i ^ 1) for i in range(row_count)]
    other_door = [(i, (i - 1 if i % 2 == 0 else i + 1) % row_count) for i in range(row_count)]
    swap = [(0, 1), (1, 0)]

    def exchange(a, b):
        return lax.ppermute(a, "row", next_door), lax.ppermute(b, "row", other_door)

    x = vectors[0]
    low = side_of_low()
    xa = lax.dynamic_slice_in_dim(x, low * wide, wide, axis=0)
    xb = lax.dynamic_slice_in_dim(x, (1 - low) * wide, wide, axis=0)
    halo_a, halo_b = exchange(xa, xb)
    band, image, table = band_parts(hop, pattern, counts, center, halfwidth, xa, xb, total_blocks)
    sa = step(0, table, image, band, halo_a, xa)
    sb = step(1, table, image, band, halo_b, xb)
    halo_a, halo_b = exchange(sa, sb)
    image = own_image(band, sa, sb)
    fa = finish(0, table, image, band, halo_a, sa, xa)
    oa = lax.ppermute(fa, "sub", swap)
    fb = finish(1, table, image, band, halo_b, sb, xb)
    ob = lax.ppermute(fb, "sub", swap)

    first, *others = [1, *range(row_count - 1, 1, -1)]
    same, coded = same_terms(fa, fb, share)
    same_there = send(share_of(coded.astype(jnp.float16), first, share, share), first, row_count)
    coded = both_terms(same, fa, fb, oa, ob, share)
    half_wide = coded.astype(jnp.float16)
    pitch = share + TAIL
    piece, *pieces = [send(share_of(half_wide, far, share, pitch), far, row_count) for far in others]
    cross_there = send(share_of(half_wide[:, half:], first, pitch, pitch), first, row_count)
    same_there, piece = lax.optimization_barrier((same_there, piece))
    partial = first_sum(coded, piece.astype(jnp.float32), same_there.astype(jnp.float32), order_total)
    for piece in pieces:
        partial = add_piece(partial, piece.astype(jnp.float32), order_total)
    partial, cross_there = lax.optimization_barrier((partial, cross_there))
    margin = last_sum(partial, cross_there.astype(jnp.float32), order_total)
    return margin.reshape(1, 1, share, 2 * half)


def solution(mesh):
    in_specs = (
        P(("groups", "row"), None, None, None),
        P(("groups", "row"), None),
        P("cuts", ("groups", "row"), "sub"),
        P(("groups", "cuts")),
        P(("groups", "cuts")),
        P(("groups", "cuts")),
    )
    out_specs = P(("groups", "cuts"), "sub", "row", None)
    return jax.shard_map(body, mesh=mesh, in_specs=in_specs, out_specs=out_specs, check_vma=False)
```

```python
import functools

import jax
import jax.numpy as jnp
from jax import lax
from jax.experimental import pallas as pl
from jax.experimental.pallas import tpu as pltpu
from jax.sharding import PartitionSpec as P

W = 3
LIMIT = 16 * 1024 * 1024
COST = pl.CostEstimate(flops=1000, bytes_accessed=1000, transcendentals=0)
LONG = pl.CostEstimate(flops=20_000_000_000, bytes_accessed=1000, transcendentals=0)
VMEM = pl.BlockSpec(memory_space=pltpu.VMEM)
SMEM = pl.BlockSpec(memory_space=pltpu.SMEM)


def call(kernel, out_shape, in_specs, cost=COST):
    return pl.pallas_call(
        kernel,
        out_shape=out_shape,
        in_specs=in_specs,
        out_specs=jax.tree.map(lambda _: VMEM, out_shape),
        compiler_params=pltpu.CompilerParams(vmem_limit_bytes=LIMIT),
        cost_estimate=cost,
    )


def mm(a, b):
    return jnp.dot(a, b, preferred_element_type=jnp.float32)


def tmm(a, b):
    return lax.dot_general(a, b, (((0,), (0,)), ((), ())), preferred_element_type=jnp.float32)


def side_of_low():
    return 1 - lax.rem(lax.axis_index("row"), 2)


def band_kernel(total_blocks, counts_ref, center_ref, width_ref, pattern_ref, hop_ref, xa_ref, xb_ref, band_ref, image_ref, table_ref):
    rows_dev, stored, block, _ = hop_ref.shape
    wide = W * block
    first_block = lax.axis_index("row") * rows_dev
    low = side_of_low()
    band_ref[...] = jnp.zeros_like(band_ref)
    half = xa_ref.shape[1]
    line = lax.broadcasted_iota(jnp.int32, (8, half), 0)
    column = lax.broadcasted_iota(jnp.int32, (8, half), 1) + lax.axis_index("sub") * half
    live = jnp.where(column < counts_ref[0], 1.0, 0.0)
    table_ref[...] = jnp.where(line == 0, center_ref[0], jnp.where(line == 1, width_ref[0], live))
    for r in range(rows_dev):
        side = low if r < W else 1 - low
        rows = pl.ds(pl.multiple_of(side * wide + (r % W) * block, block), block)
        for k in range(stored):
            col = lax.rem(pattern_ref[r, k] - first_block + (W + total_blocks), total_blocks) - W
            in_low = jnp.logical_and(col >= 0, col < W)
            in_high = jnp.logical_and(col >= W, col < rows_dev)
            at = jnp.where(
                in_low, low * W + col,
                jnp.where(in_high, (1 - low) * W + col - W, 2 * W + jnp.where(col < 0, col + W, col - rows_dev)),
            )
            band_ref[rows, pl.ds(pl.multiple_of(at * block, block), block)] = hop_ref[r, k]
    image_ref[...] = mm(band_ref[:, :wide], xa_ref[...]) + mm(band_ref[:, wide:2 * wide], xb_ref[...])


def band_parts(hop, pattern, counts, center, halfwidth, xa, xb, total_blocks):
    rows_dev, _, block, _ = hop.shape
    wide, tall, half = W * block, rows_dev * block, xa.shape[1]
    return call(
        functools.partial(band_kernel, total_blocks),
        (
            jax.ShapeDtypeStruct((tall, 3 * wide), hop.dtype),
            jax.ShapeDtypeStruct((tall, half), jnp.float32),
            jax.ShapeDtypeStruct((8, half), jnp.float32),
        ),
        [SMEM] * 4 + [VMEM] * 3,
    )(counts, center, halfwidth, pattern, hop, xa, xb)


def halo_image(side, band_ref, image_ref, halo_ref):
    wide = halo_ref.shape[0]
    rows = slice(side * wide, (side + 1) * wide)
    return image_ref[rows, :] + mm(band_ref[rows, 2 * wide:], halo_ref[...])


def step_kernel(side, table_ref, image_ref, band_ref, halo_ref, x_ref, out_ref):
    shift, width = table_ref[0:1, :], table_ref[1:2, :]
    image = halo_image(side, band_ref, image_ref, halo_ref)
    out_ref[...] = ((image - shift * x_ref[...].astype(jnp.float32)) / width).astype(jnp.bfloat16)


def step(side, table, image, band, halo, x):
    shape = jax.ShapeDtypeStruct(x.shape, jnp.bfloat16)
    return call(functools.partial(step_kernel, side), shape, [VMEM] * 5)(table, image, band, halo, x)


def finish_kernel(side, table_ref, image_ref, band_ref, halo_ref, s_ref, x_ref, out_ref):
    shift, width = table_ref[0:1, :], table_ref[1:2, :]
    live = table_ref[2:3, :] > 0.0
    image = halo_image(side, band_ref, image_ref, halo_ref)
    value = 2.0 * (image - shift * s_ref[...].astype(jnp.float32)) / width - x_ref[...].astype(jnp.float32)
    out_ref[...] = jnp.where(live, value, 0.0).astype(jnp.bfloat16)


def finish(side, table, image, band, halo, s, x):
    shape = jax.ShapeDtypeStruct(x.shape, jnp.bfloat16)
    return call(functools.partial(finish_kernel, side), shape, [VMEM] * 6)(table, image, band, halo, s, x)


def exponent(*values):
    top = functools.reduce(jnp.maximum, [jnp.abs(value) for value in values])
    top = jnp.max(top, axis=(0, 1), keepdims=True)
    return jnp.clip(jnp.ceil(jnp.log2(jnp.maximum(top, 1e-36))) - 14.0, -100.0, 60.0)


def with_code(share, same, e):
    row = lax.broadcasted_iota(jnp.int32, same.shape, 0)
    col = lax.broadcasted_iota(jnp.int32, same.shape, 1)
    slot = (lax.rem(row, share) == 1) & (col == row - 1)
    return jnp.where(slot, e, same * jnp.exp2(-e))


def same_kernel(fa_ref, fb_ref, out_ref):
    fa, fb = fa_ref[...], fb_ref[...]
    out_ref[...] = tmm(fa, fa) + tmm(fb, fb)


def same_terms(fa, fb):
    half = fa.shape[1]
    return call(same_kernel, jax.ShapeDtypeStruct((half, half), jnp.float32), [VMEM] * 2)(fa, fb)


def both_kernel(share, same_ref, fa_ref, fb_ref, oa_ref, ob_ref, out_ref):
    half = fa_ref.shape[1]
    same = same_ref[...]
    cross = tmm(fa_ref[...], oa_ref[...]) + tmm(fb_ref[...], ob_ref[...])
    e = exponent(same, cross)
    out_ref[:, :half] = with_code(share, same, e)
    out_ref[:, half:] = cross * jnp.exp2(-e)


def both_terms(same, fa, fb, oa, ob, share):
    half = fa.shape[1]
    shape = jax.ShapeDtypeStruct((half, 2 * half), jnp.float32)
    return call(functools.partial(both_kernel, share), shape, [VMEM] * 5)(same, fa, fb, oa, ob)


def slots(shape):
    start = lax.axis_index("row") * shape[0]
    row = lax.broadcasted_iota(jnp.int32, (8, shape[1]), 0)
    col = lax.broadcasted_iota(jnp.int32, (8, shape[1]), 1)
    return (row == 1) & (col == start), (row == 0) & (col == start + 1)


def slot_factor(ref, slot, order_total):
    e = jnp.sum(jnp.where(slot, ref[:8, :slot.shape[1]], 0.0), axis=(0, 1), keepdims=True)
    return jnp.exp2(e) / order_total


def first_sum_kernel(order_total, coded_ref, piece_ref, out_ref):
    share, half = out_ref.shape[0], out_ref.shape[1] // 2
    slot, _ = slots((share, half))
    mine = coded_ref.at[pl.ds(pl.multiple_of(lax.axis_index("row") * share, 8), share), :]
    total = mine[...] * slot_factor(mine, slot, order_total)
    out_ref[...] = total + piece_ref[...] * slot_factor(piece_ref, slot, order_total)


def first_sum(coded, piece, order_total):
    shape = jax.ShapeDtypeStruct(piece.shape, jnp.float32)
    return call(functools.partial(first_sum_kernel, order_total), shape, [VMEM] * 2, LONG)(coded, piece)


def add_kernel(order_total, sum_ref, piece_ref, out_ref):
    share, columns = sum_ref.shape
    slot, _ = slots((share, columns // 2))
    out_ref[...] = sum_ref[...] + piece_ref[...] * slot_factor(piece_ref, slot, order_total)


def add_piece(total, piece, order_total):
    shape = jax.ShapeDtypeStruct(total.shape, jnp.float32)
    return call(functools.partial(add_kernel, order_total), shape, [VMEM] * 2, LONG)(total, piece)


def last_kernel(order_total, sum_ref, piece_ref, out_ref):
    share, half = out_ref.shape[0], out_ref.shape[1] // 2
    slot, twin = slots((share, half))
    factor = slot_factor(piece_ref, slot, order_total)
    sub = lax.axis_index("sub")
    at = pl.ds(pl.multiple_of(sub * half, half), half)
    other = pl.ds(pl.multiple_of((1 - sub) * half, half), half)
    out_ref[:, other] = sum_ref[:, half:] + piece_ref[:, half:] * factor
    same = sum_ref[:, :half] + piece_ref[:, :half] * factor
    out_ref[:, at] = same
    lost = jnp.sum(jnp.where(twin, same[:8], 0.0), axis=(0, 1), keepdims=True)
    out_ref[:8, at] = jnp.where(slot, lost, same[:8])


def last_sum(total, piece, order_total):
    shape = jax.ShapeDtypeStruct(total.shape, jnp.float32)
    return call(functools.partial(last_kernel, order_total), shape, [VMEM] * 2)(total, piece)


def image_kernel(band_ref, sa_ref, sb_ref, out_ref):
    wide = sa_ref.shape[0]
    out_ref[...] = mm(band_ref[:, :wide], sa_ref[...]) + mm(band_ref[:, wide:2 * wide], sb_ref[...])


def own_image(band, sa, sb):
    shape = jax.ShapeDtypeStruct((band.shape[0], sa.shape[1]), jnp.float32)
    return call(image_kernel, shape, [VMEM] * 3)(band, sa, sb)


def send_shares(coded, row_count, share):
    me = lax.axis_index("row")
    arrived = []
    for shift in range(1, row_count):
        part = lax.dynamic_slice_in_dim(coded, (me + shift) % row_count * share, share, axis=0)
        ring = [(i, (i + shift) % row_count) for i in range(row_count)]
        arrived.append(lax.ppermute(part, "row", ring))
    return arrived


def body(hop, pattern, vectors, counts, center, halfwidth):
    rows_dev = hop.shape[0]
    block = hop.shape[2]
    half = vectors.shape[2]
    row_count = lax.axis_size("row")
    total_blocks = rows_dev * row_count
    order_total = total_blocks * block
    wide = W * block
    share = half // row_count
    assert rows_dev == 2 * W and row_count & (row_count - 1) == 0
    next_door = [(i, i ^ 1) for i in range(row_count)]
    other_door = [(i, (i - 1 if i % 2 == 0 else i + 1) % row_count) for i in range(row_count)]
    swap = [(0, 1), (1, 0)]

    def exchange(a, b):
        return lax.ppermute(a, "row", next_door), lax.ppermute(b, "row", other_door)

    x = vectors[0]
    low = side_of_low()
    xa = lax.dynamic_slice_in_dim(x, low * wide, wide, axis=0)
    xb = lax.dynamic_slice_in_dim(x, (1 - low) * wide, wide, axis=0)
    halo_a, halo_b = exchange(xa, xb)
    band, image, table = band_parts(hop, pattern, counts, center, halfwidth, xa, xb, total_blocks)
    sa = step(0, table, image, band, halo_a, xa)
    sb = step(1, table, image, band, halo_b, xb)
    halo_a, halo_b = exchange(sa, sb)
    image = own_image(band, sa, sb)
    fa = finish(0, table, image, band, halo_a, sa, xa)
    oa = lax.ppermute(fa, "sub", swap)
    fb = finish(1, table, image, band, halo_b, sb, xb)
    ob = lax.ppermute(fb, "sub", swap)

    coded = both_terms(same_terms(fa, fb), fa, fb, oa, ob, share)
    first, *middle, last = send_shares(coded.astype(jnp.float16), row_count, share)
    total = first_sum(coded, first.astype(jnp.float32), order_total)
    for piece in middle:
        total = add_piece(total, piece.astype(jnp.float32), order_total)
    total, last = lax.optimization_barrier((total, last))
    margin = last_sum(total, last.astype(jnp.float32), order_total)
    return margin.reshape(1, 1, share, 2 * half)


def solution(mesh):
    in_specs = (
        P(("groups", "row"), None, None, None),
        P(("groups", "row"), None),
        P("cuts", ("groups", "row"), "sub"),
        P(("groups", "cuts")),
        P(("groups", "cuts")),
        P(("groups", "cuts")),
    )
    out_specs = P(("groups", "cuts"), "sub", "row", None)
    return jax.shard_map(body, mesh=mesh, in_specs=in_specs, out_specs=out_specs, check_vma=False)
```

```python
import functools

import jax
import jax.numpy as jnp
from jax import lax
from jax.experimental import pallas as pl
from jax.experimental.pallas import tpu as pltpu
from jax.sharding import PartitionSpec as P

W = 3
LIMIT = 16 * 1024 * 1024
COST = pl.CostEstimate(flops=1000, bytes_accessed=1000, transcendentals=0)
LONG = pl.CostEstimate(flops=20_000_000_000, bytes_accessed=1000, transcendentals=0)
VMEM = pl.BlockSpec(memory_space=pltpu.VMEM)
SMEM = pl.BlockSpec(memory_space=pltpu.SMEM)


def call(kernel, out_shape, in_specs, cost=COST):
    return pl.pallas_call(
        kernel,
        out_shape=out_shape,
        in_specs=in_specs,
        out_specs=jax.tree.map(lambda _: VMEM, out_shape),
        compiler_params=pltpu.CompilerParams(vmem_limit_bytes=LIMIT),
        cost_estimate=cost,
    )


def mm(a, b):
    return jnp.dot(a, b, preferred_element_type=jnp.float32)


def tmm(a, b):
    return lax.dot_general(a, b, (((0,), (0,)), ((), ())), preferred_element_type=jnp.float32)


def side_of_low():
    return 1 - lax.rem(lax.axis_index("row"), 2)


def band_kernel(total_blocks, counts_ref, center_ref, width_ref, pattern_ref, hop_ref, xa_ref, xb_ref, band_ref, image_ref, table_ref):
    rows_dev, stored, block, _ = hop_ref.shape
    wide = W * block
    first_block = lax.axis_index("row") * rows_dev
    low = side_of_low()
    band_ref[...] = jnp.zeros_like(band_ref)
    half = xa_ref.shape[1]
    line = lax.broadcasted_iota(jnp.int32, (8, half), 0)
    column = lax.broadcasted_iota(jnp.int32, (8, half), 1) + lax.axis_index("sub") * half
    live = jnp.where(column < counts_ref[0], 1.0, 0.0)
    table_ref[...] = jnp.where(line == 0, center_ref[0], jnp.where(line == 1, width_ref[0], live))
    for r in range(rows_dev):
        side = low if r < W else 1 - low
        rows = pl.ds(pl.multiple_of(side * wide + (r % W) * block, block), block)
        for k in range(stored):
            col = lax.rem(pattern_ref[r, k] - first_block + (W + total_blocks), total_blocks) - W
            in_low = jnp.logical_and(col >= 0, col < W)
            in_high = jnp.logical_and(col >= W, col < rows_dev)
            at = jnp.where(
                in_low, low * W + col,
                jnp.where(in_high, (1 - low) * W + col - W, 2 * W + jnp.where(col < 0, col + W, col - rows_dev)),
            )
            band_ref[rows, pl.ds(pl.multiple_of(at * block, block), block)] = hop_ref[r, k]
    image_ref[...] = mm(band_ref[:, :wide], xa_ref[...]) + mm(band_ref[:, wide:2 * wide], xb_ref[...])


def band_parts(hop, pattern, counts, center, halfwidth, xa, xb, total_blocks):
    rows_dev, _, block, _ = hop.shape
    wide, tall, half = W * block, rows_dev * block, xa.shape[1]
    return call(
        functools.partial(band_kernel, total_blocks),
        (
            jax.ShapeDtypeStruct((tall, 3 * wide), hop.dtype),
            jax.ShapeDtypeStruct((tall, half), jnp.float32),
            jax.ShapeDtypeStruct((8, half), jnp.float32),
        ),
        [SMEM] * 4 + [VMEM] * 3,
    )(counts, center, halfwidth, pattern, hop, xa, xb)


def halo_image(side, band_ref, image_ref, halo_ref):
    wide = halo_ref.shape[0]
    rows = slice(side * wide, (side + 1) * wide)
    return image_ref[rows, :] + mm(band_ref[rows, 2 * wide:], halo_ref[...])


def step_kernel(side, table_ref, image_ref, band_ref, halo_ref, x_ref, out_ref):
    shift, width = table_ref[0:1, :], table_ref[1:2, :]
    image = halo_image(side, band_ref, image_ref, halo_ref)
    out_ref[...] = ((image - shift * x_ref[...].astype(jnp.float32)) / width).astype(jnp.bfloat16)


def step(side, table, image, band, halo, x):
    shape = jax.ShapeDtypeStruct(x.shape, jnp.bfloat16)
    return call(functools.partial(step_kernel, side), shape, [VMEM] * 5)(table, image, band, halo, x)


def finish_kernel(side, table_ref, image_ref, band_ref, halo_ref, s_ref, x_ref, out_ref):
    shift, width = table_ref[0:1, :], table_ref[1:2, :]
    live = table_ref[2:3, :] > 0.0
    image = halo_image(side, band_ref, image_ref, halo_ref)
    value = 2.0 * (image - shift * s_ref[...].astype(jnp.float32)) / width - x_ref[...].astype(jnp.float32)
    out_ref[...] = jnp.where(live, value, 0.0).astype(jnp.bfloat16)


def finish(side, table, image, band, halo, s, x):
    shape = jax.ShapeDtypeStruct(x.shape, jnp.bfloat16)
    return call(functools.partial(finish_kernel, side), shape, [VMEM] * 6)(table, image, band, halo, s, x)


def exponent(*values):
    top = functools.reduce(jnp.maximum, [jnp.abs(value) for value in values])
    top = jnp.max(top, axis=(0, 1), keepdims=True)
    return jnp.clip(jnp.ceil(jnp.log2(jnp.maximum(top, 1e-36))) - 14.0, -100.0, 60.0)


def with_code(share, same, e):
    row = lax.broadcasted_iota(jnp.int32, same.shape, 0)
    col = lax.broadcasted_iota(jnp.int32, same.shape, 1)
    slot = (lax.rem(row, share) == 1) & (col == row - 1)
    return jnp.where(slot, e, same * jnp.exp2(-e))


def early_kernel(fa_ref, fb_ref, ob_ref, out_ref):
    half = fa_ref.shape[1]
    fa, fb = fa_ref[...], fb_ref[...]
    out_ref[:, :half] = tmm(fa, fa) + tmm(fb, fb)
    out_ref[:, half:] = tmm(fb, ob_ref[...])


def early_terms(fa, fb, ob):
    half = fa.shape[1]
    shape = jax.ShapeDtypeStruct((half, 2 * half), jnp.float32)
    return call(early_kernel, shape, [VMEM] * 3)(fa, fb, ob)


def code_kernel(share, early_ref, fa_ref, oa_ref, out_ref):
    half = fa_ref.shape[1]
    same = early_ref[:, :half]
    cross = early_ref[:, half:] + tmm(fa_ref[...], oa_ref[...])
    e = exponent(same, cross)
    out_ref[:, :half] = with_code(share, same, e)
    out_ref[:, half:] = cross * jnp.exp2(-e)


def code_terms(early, fa, oa, share):
    shape = jax.ShapeDtypeStruct(early.shape, jnp.float32)
    return call(functools.partial(code_kernel, share), shape, [VMEM] * 3)(early, fa, oa)


def slots(shape):
    start = lax.axis_index("row") * shape[0]
    row = lax.broadcasted_iota(jnp.int32, (8, shape[1]), 0)
    col = lax.broadcasted_iota(jnp.int32, (8, shape[1]), 1)
    return (row == 1) & (col == start), (row == 0) & (col == start + 1)


def slot_factor(ref, slot, order_total):
    e = jnp.sum(jnp.where(slot, ref[:8, :slot.shape[1]], 0.0), axis=(0, 1), keepdims=True)
    return jnp.exp2(e) / order_total


def first_sum_kernel(order_total, coded_ref, piece_ref, out_ref):
    share, half = out_ref.shape[0], out_ref.shape[1] // 2
    slot, _ = slots((share, half))
    mine = coded_ref.at[pl.ds(pl.multiple_of(lax.axis_index("row") * share, 8), share), :]
    total = mine[...] * slot_factor(mine, slot, order_total)
    out_ref[...] = total + piece_ref[...] * slot_factor(piece_ref, slot, order_total)


def first_sum(coded, piece, order_total):
    shape = jax.ShapeDtypeStruct(piece.shape, jnp.float32)
    return call(functools.partial(first_sum_kernel, order_total), shape, [VMEM] * 2, LONG)(coded, piece)


def add_kernel(order_total, sum_ref, piece_ref, out_ref):
    share, columns = sum_ref.shape
    slot, _ = slots((share, columns // 2))
    out_ref[...] = sum_ref[...] + piece_ref[...] * slot_factor(piece_ref, slot, order_total)


def add_piece(total, piece, order_total):
    shape = jax.ShapeDtypeStruct(total.shape, jnp.float32)
    return call(functools.partial(add_kernel, order_total), shape, [VMEM] * 2, LONG)(total, piece)


def last_kernel(order_total, sum_ref, *refs):
    *pieces, out_ref = refs
    share, half = out_ref.shape[0], out_ref.shape[1] // 2
    slot, twin = slots((share, half))
    same, cross = sum_ref[:, :half], sum_ref[:, half:]
    for ref in pieces:
        factor = slot_factor(ref, slot, order_total)
        same += ref[:, :half] * factor
        cross += ref[:, half:] * factor
    sub = lax.axis_index("sub")
    at = pl.ds(pl.multiple_of(sub * half, half), half)
    out_ref[:, at] = same
    lost = jnp.sum(jnp.where(twin, same[:8], 0.0), axis=(0, 1), keepdims=True)
    out_ref[:8, at] = jnp.where(slot, lost, same[:8])
    out_ref[:, pl.ds(pl.multiple_of((1 - sub) * half, half), half)] = cross


def last_sum(total, pieces, order_total):
    shape = jax.ShapeDtypeStruct(total.shape, jnp.float32)
    return call(functools.partial(last_kernel, order_total), shape, [VMEM] * (1 + len(pieces)))(total, *pieces)


def image_kernel(band_ref, sa_ref, sb_ref, out_ref):
    wide = sa_ref.shape[0]
    out_ref[...] = mm(band_ref[:, :wide], sa_ref[...]) + mm(band_ref[:, wide:2 * wide], sb_ref[...])


def own_image(band, sa, sb):
    shape = jax.ShapeDtypeStruct((band.shape[0], sa.shape[1]), jnp.float32)
    return call(image_kernel, shape, [VMEM] * 3)(band, sa, sb)


def send_shares(coded, row_count, share):
    me = lax.axis_index("row")
    middle = row_count // 2
    arrived, late = [], []
    for shift in range(1, row_count):
        part = lax.dynamic_slice_in_dim(coded, (me + shift) % row_count * share, share, axis=0)
        ring = [(i, (i + shift) % row_count) for i in range(row_count)]
        if shift == middle:
            late = [pair for pair in ring if 0 < pair[1] < middle]
            half_part = part
            ring = [pair for pair in ring if pair not in late]
        arrived.append(lax.ppermute(part, "row", ring))
    return arrived, lax.ppermute(half_part, "row", late)


def body(hop, pattern, vectors, counts, center, halfwidth):
    rows_dev = hop.shape[0]
    block = hop.shape[2]
    half = vectors.shape[2]
    row_count = lax.axis_size("row")
    total_blocks = rows_dev * row_count
    order_total = total_blocks * block
    wide = W * block
    share = half // row_count
    assert rows_dev == 2 * W and row_count & (row_count - 1) == 0
    next_door = [(i, i ^ 1) for i in range(row_count)]
    other_door = [(i, (i - 1 if i % 2 == 0 else i + 1) % row_count) for i in range(row_count)]
    swap = [(0, 1), (1, 0)]

    def exchange(a, b):
        return lax.ppermute(a, "row", next_door), lax.ppermute(b, "row", other_door)

    x = vectors[0]
    low = side_of_low()
    xa = lax.dynamic_slice_in_dim(x, low * wide, wide, axis=0)
    xb = lax.dynamic_slice_in_dim(x, (1 - low) * wide, wide, axis=0)
    halo_a, halo_b = exchange(xa, xb)
    band, image, table = band_parts(hop, pattern, counts, center, halfwidth, xa, xb, total_blocks)
    sa = step(0, table, image, band, halo_a, xa)
    sb = step(1, table, image, band, halo_b, xb)
    halo_a, halo_b = exchange(sa, sb)
    image = own_image(band, sa, sb)
    fa = finish(0, table, image, band, halo_a, sa, xa)
    oa = lax.ppermute(fa, "sub", swap)
    fb = finish(1, table, image, band, halo_b, sb, xb)
    ob = lax.ppermute(fb, "sub", swap)

    coded = code_terms(early_terms(fa, fb, ob), fa, oa, share)
    (first, *middle, last), late = send_shares(coded.astype(jnp.float16), row_count, share)
    total = first_sum(coded, first.astype(jnp.float32), order_total)
    for piece in middle:
        total = add_piece(total, piece.astype(jnp.float32), order_total)
    total, last, late = lax.optimization_barrier((total, last, late))
    margin = last_sum(total, [last.astype(jnp.float32), late.astype(jnp.float32)], order_total)
    return margin.reshape(1, 1, share, 2 * half)


def solution(mesh):
    in_specs = (
        P(("groups", "row"), None, None, None),
        P(("groups", "row"), None),
        P("cuts", ("groups", "row"), "sub"),
        P(("groups", "cuts")),
        P(("groups", "cuts")),
        P(("groups", "cuts")),
    )
    out_specs = P(("groups", "cuts"), "sub", "row", None)
    return jax.shard_map(body, mesh=mesh, in_specs=in_specs, out_specs=out_specs, check_vma=False)
```

```python
import functools

import jax
import jax.numpy as jnp
from jax import lax
from jax.experimental import pallas as pl
from jax.experimental.pallas import tpu as pltpu
from jax.sharding import PartitionSpec as P

W = 3
LIMIT = 16 * 1024 * 1024
COST = pl.CostEstimate(flops=1000, bytes_accessed=1000, transcendentals=0)
LONG = pl.CostEstimate(flops=20_000_000_000, bytes_accessed=1000, transcendentals=0)
VMEM = pl.BlockSpec(memory_space=pltpu.VMEM)
SMEM = pl.BlockSpec(memory_space=pltpu.SMEM)


def call(kernel, out_shape, in_specs, cost=COST):
    return pl.pallas_call(
        kernel,
        out_shape=out_shape,
        in_specs=in_specs,
        out_specs=jax.tree.map(lambda _: VMEM, out_shape),
        compiler_params=pltpu.CompilerParams(vmem_limit_bytes=LIMIT),
        cost_estimate=cost,
    )


def mm(a, b):
    return jnp.dot(a, b, preferred_element_type=jnp.float32)


def tmm(a, b):
    return lax.dot_general(a, b, (((0,), (0,)), ((), ())), preferred_element_type=jnp.float32)


def band_kernel(total_blocks, counts_ref, center_ref, width_ref, pattern_ref, hop_ref, xa_ref, xb_ref, band_ref, image_ref, table_ref):
    rows_dev, stored, block, _ = hop_ref.shape
    wide = W * block
    first_block = lax.axis_index("row") * rows_dev
    band_ref[...] = jnp.zeros_like(band_ref)
    half = xa_ref.shape[1]
    line = lax.broadcasted_iota(jnp.int32, (8, half), 0)
    column = lax.broadcasted_iota(jnp.int32, (8, half), 1) + lax.axis_index("sub") * half
    live = jnp.where(column < counts_ref[0], 1.0, 0.0)
    table_ref[...] = jnp.where(line == 0, center_ref[0], jnp.where(line == 1, width_ref[0], live))
    for r in range(rows_dev):
        rows = slice(r * block, (r + 1) * block)
        for k in range(stored):
            col = lax.rem(pattern_ref[r, k] - first_block + (W + total_blocks), total_blocks) - W
            inside = jnp.logical_and(col >= 0, col < rows_dev)
            halo = 2 * W + jnp.where(col < 0, col + W, col - rows_dev)
            at = jnp.where(inside, col, halo)
            band_ref[rows, pl.ds(pl.multiple_of(at * block, block), block)] = hop_ref[r, k]
    image_ref[...] = mm(band_ref[:, :wide], xa_ref[...]) + mm(band_ref[:, wide:2 * wide], xb_ref[...])


def band_parts(hop, pattern, counts, center, halfwidth, xa, xb, total_blocks):
    rows_dev, _, block, _ = hop.shape
    wide, tall, half = W * block, rows_dev * block, xa.shape[1]
    return call(
        functools.partial(band_kernel, total_blocks),
        (
            jax.ShapeDtypeStruct((tall, 3 * wide), hop.dtype),
            jax.ShapeDtypeStruct((tall, half), jnp.float32),
            jax.ShapeDtypeStruct((8, half), jnp.float32),
        ),
        [SMEM] * 4 + [VMEM] * 3,
    )(counts, center, halfwidth, pattern, hop, xa, xb)


def halo_image(side, band_ref, image_ref, halo_ref):
    wide = halo_ref.shape[0]
    rows = slice(side * wide, (side + 1) * wide)
    return image_ref[rows, :] + mm(band_ref[rows, 2 * wide:], halo_ref[...])


def step_kernel(side, table_ref, image_ref, band_ref, halo_ref, x_ref, out_ref):
    shift, width = table_ref[0:1, :], table_ref[1:2, :]
    image = halo_image(side, band_ref, image_ref, halo_ref)
    out_ref[...] = ((image - shift * x_ref[...].astype(jnp.float32)) / width).astype(jnp.bfloat16)


def step(side, table, image, band, halo, x):
    shape = jax.ShapeDtypeStruct(x.shape, jnp.bfloat16)
    return call(functools.partial(step_kernel, side), shape, [VMEM] * 5)(table, image, band, halo, x)


def finish_kernel(side, table_ref, image_ref, band_ref, halo_ref, s_ref, x_ref, out_ref):
    shift, width = table_ref[0:1, :], table_ref[1:2, :]
    live = table_ref[2:3, :] > 0.0
    image = halo_image(side, band_ref, image_ref, halo_ref)
    value = 2.0 * (image - shift * s_ref[...].astype(jnp.float32)) / width - x_ref[...].astype(jnp.float32)
    out_ref[...] = jnp.where(live, value, 0.0).astype(jnp.bfloat16)


def finish(side, table, image, band, halo, s, x):
    shape = jax.ShapeDtypeStruct(x.shape, jnp.bfloat16)
    return call(functools.partial(finish_kernel, side), shape, [VMEM] * 6)(table, image, band, halo, s, x)


def exponent(*values):
    top = functools.reduce(jnp.maximum, [jnp.abs(value) for value in values])
    top = jnp.max(top, axis=(0, 1), keepdims=True)
    return jnp.clip(jnp.ceil(jnp.log2(jnp.maximum(top, 1e-36))) - 14.0, -100.0, 60.0)


def with_code(share, same, e):
    row = lax.broadcasted_iota(jnp.int32, same.shape, 0)
    col = lax.broadcasted_iota(jnp.int32, same.shape, 1)
    slot = (lax.rem(row, share) == 1) & (col == row - 1)
    return jnp.where(slot, e, same * jnp.exp2(-e))


def early_kernel(fa_ref, fb_ref, ob_ref, out_ref):
    half = fa_ref.shape[1]
    fa, fb = fa_ref[...], fb_ref[...]
    out_ref[:, :half] = tmm(fa, fa) + tmm(fb, fb)
    out_ref[:, half:] = tmm(fb, ob_ref[...])


def early_terms(fa, fb, ob):
    half = fa.shape[1]
    shape = jax.ShapeDtypeStruct((half, 2 * half), jnp.float32)
    return call(early_kernel, shape, [VMEM] * 3)(fa, fb, ob)


def code_kernel(share, early_ref, fa_ref, oa_ref, out_ref):
    half = fa_ref.shape[1]
    same = early_ref[:, :half]
    cross = early_ref[:, half:] + tmm(fa_ref[...], oa_ref[...])
    e = exponent(same, cross)
    out_ref[:, :half] = with_code(share, same, e)
    out_ref[:, half:] = cross * jnp.exp2(-e)


def code_terms(early, fa, oa, share):
    shape = jax.ShapeDtypeStruct(early.shape, jnp.float32)
    return call(functools.partial(code_kernel, share), shape, [VMEM] * 3)(early, fa, oa)


def slots(shape):
    start = lax.axis_index("row") * shape[0]
    row = lax.broadcasted_iota(jnp.int32, (8, shape[1]), 0)
    col = lax.broadcasted_iota(jnp.int32, (8, shape[1]), 1)
    return (row == 1) & (col == start), (row == 0) & (col == start + 1)


def slot_factor(ref, slot, order_total):
    e = jnp.sum(jnp.where(slot, ref[:8, :slot.shape[1]], 0.0), axis=(0, 1), keepdims=True)
    return jnp.exp2(e) / order_total


def first_sum_kernel(order_total, coded_ref, piece_ref, out_ref):
    share, half = out_ref.shape[0], out_ref.shape[1] // 2
    slot, _ = slots((share, half))
    mine = coded_ref.at[pl.ds(pl.multiple_of(lax.axis_index("row") * share, 8), share), :]
    total = mine[...] * slot_factor(mine, slot, order_total)
    out_ref[...] = total + piece_ref[...] * slot_factor(piece_ref, slot, order_total)


def first_sum(coded, piece, order_total):
    shape = jax.ShapeDtypeStruct(piece.shape, jnp.float32)
    return call(functools.partial(first_sum_kernel, order_total), shape, [VMEM] * 2, LONG)(coded, piece)


def add_kernel(order_total, sum_ref, piece_ref, out_ref):
    share, columns = sum_ref.shape
    slot, _ = slots((share, columns // 2))
    out_ref[...] = sum_ref[...] + piece_ref[...] * slot_factor(piece_ref, slot, order_total)


def add_piece(total, piece, order_total):
    shape = jax.ShapeDtypeStruct(total.shape, jnp.float32)
    return call(functools.partial(add_kernel, order_total), shape, [VMEM] * 2, LONG)(total, piece)


def last_kernel(order_total, sum_ref, piece_ref, out_ref):
    share, half = out_ref.shape[0], out_ref.shape[1] // 2
    slot, twin = slots((share, half))
    factor = slot_factor(piece_ref, slot, order_total)
    sub = lax.axis_index("sub")
    at = pl.ds(pl.multiple_of(sub * half, half), half)
    other = pl.ds(pl.multiple_of((1 - sub) * half, half), half)
    out_ref[:, other] = sum_ref[:, half:] + piece_ref[:, half:] * factor
    same = sum_ref[:, :half] + piece_ref[:, :half] * factor
    out_ref[:, at] = same
    lost = jnp.sum(jnp.where(twin, same[:8], 0.0), axis=(0, 1), keepdims=True)
    out_ref[:8, at] = jnp.where(slot, lost, same[:8])


def last_sum(total, piece, order_total):
    shape = jax.ShapeDtypeStruct(total.shape, jnp.float32)
    return call(functools.partial(last_kernel, order_total), shape, [VMEM] * 2)(total, piece)


def image_kernel(band_ref, sa_ref, sb_ref, out_ref):
    wide = sa_ref.shape[0]
    out_ref[...] = mm(band_ref[:, :wide], sa_ref[...]) + mm(band_ref[:, wide:2 * wide], sb_ref[...])


def own_image(band, sa, sb):
    shape = jax.ShapeDtypeStruct((band.shape[0], sa.shape[1]), jnp.float32)
    return call(image_kernel, shape, [VMEM] * 3)(band, sa, sb)


def send_shares(coded, row_count, share):
    me = lax.axis_index("row")
    arrived = []
    for shift in range(1, row_count):
        part = lax.dynamic_slice_in_dim(coded, (me + shift) % row_count * share, share, axis=0)
        ring = [(i, (i + shift) % row_count) for i in range(row_count)]
        arrived.append(lax.ppermute(part, "row", ring))
    return arrived


def body(hop, pattern, vectors, counts, center, halfwidth):
    rows_dev = hop.shape[0]
    block = hop.shape[2]
    half = vectors.shape[2]
    row_count = lax.axis_size("row")
    total_blocks = rows_dev * row_count
    order_total = total_blocks * block
    wide = W * block
    share = half // row_count
    assert rows_dev == 2 * W
    forward = [(i, (i + 1) % row_count) for i in range(row_count)]
    backward = [(target, source) for source, target in forward]
    swap = [(0, 1), (1, 0)]

    def halos_of(low, high):
        return lax.ppermute(high, "row", forward), lax.ppermute(low, "row", backward)

    x = vectors[0]
    xa, xb = x[:wide], x[wide:]
    halo_a, halo_b = halos_of(xa, xb)
    band, image, table = band_parts(hop, pattern, counts, center, halfwidth, xa, xb, total_blocks)
    sa = step(0, table, image, band, halo_a, xa)
    sb = step(1, table, image, band, halo_b, xb)
    halo_a, halo_b = halos_of(sa, sb)
    image = own_image(band, sa, sb)
    fa = finish(0, table, image, band, halo_a, sa, xa)
    oa = lax.ppermute(fa, "sub", swap)
    fb = finish(1, table, image, band, halo_b, sb, xb)
    ob = lax.ppermute(fb, "sub", swap)
    coded = code_terms(early_terms(fa, fb, ob), fa, oa, share)
    first, *middle, last = send_shares(coded.astype(jnp.float16), row_count, share)
    total = first_sum(coded, first.astype(jnp.float32), order_total)
    for piece in middle:
        total = add_piece(total, piece.astype(jnp.float32), order_total)
    total, last = lax.optimization_barrier((total, last))
    margin = last_sum(total, last.astype(jnp.float32), order_total)
    return margin.reshape(1, 1, share, 2 * half)


def solution(mesh):
    in_specs = (
        P(("groups", "row"), None, None, None),
        P(("groups", "row"), None),
        P("cuts", ("groups", "row"), "sub"),
        P(("groups", "cuts")),
        P(("groups", "cuts")),
        P(("groups", "cuts")),
    )
    out_specs = P(("groups", "cuts"), "sub", "row", None)
    return jax.shard_map(body, mesh=mesh, in_specs=in_specs, out_specs=out_specs, check_vma=False)
```

```python
import functools

import jax
import jax.numpy as jnp
from jax import lax
from jax.experimental import pallas as pl
from jax.experimental.pallas import tpu as pltpu
from jax.sharding import PartitionSpec as P

W = 3
LIMIT = 16 * 1024 * 1024
COST = pl.CostEstimate(flops=1000, bytes_accessed=1000, transcendentals=0)
LONG = pl.CostEstimate(flops=20_000_000_000, bytes_accessed=1000, transcendentals=0)
VMEM = pl.BlockSpec(memory_space=pltpu.VMEM)
SMEM = pl.BlockSpec(memory_space=pltpu.SMEM)


def call(kernel, out_shape, in_specs, cost=COST):
    return pl.pallas_call(
        kernel,
        out_shape=out_shape,
        in_specs=in_specs,
        out_specs=jax.tree.map(lambda _: VMEM, out_shape),
        compiler_params=pltpu.CompilerParams(vmem_limit_bytes=LIMIT),
        cost_estimate=cost,
    )


def mm(a, b):
    return jnp.dot(a, b, preferred_element_type=jnp.float32)


def tmm(a, b):
    return lax.dot_general(a, b, (((0,), (0,)), ((), ())), preferred_element_type=jnp.float32)


def band_kernel(total_blocks, counts_ref, center_ref, width_ref, pattern_ref, hop_ref, xa_ref, xb_ref, band_ref, image_ref, table_ref):
    rows_dev, stored, block, _ = hop_ref.shape
    wide = W * block
    first_block = lax.axis_index("row") * rows_dev
    band_ref[...] = jnp.zeros_like(band_ref)
    half = xa_ref.shape[1]
    line = lax.broadcasted_iota(jnp.int32, (8, half), 0)
    column = lax.broadcasted_iota(jnp.int32, (8, half), 1) + lax.axis_index("sub") * half
    live = jnp.where(column < counts_ref[0], 1.0, 0.0)
    table_ref[...] = jnp.where(line == 0, center_ref[0], jnp.where(line == 1, width_ref[0], live))
    for r in range(rows_dev):
        rows = slice(r * block, (r + 1) * block)
        for k in range(stored):
            col = lax.rem(pattern_ref[r, k] - first_block + (W + total_blocks), total_blocks) - W
            inside = jnp.logical_and(col >= 0, col < rows_dev)
            halo = 2 * W + jnp.where(col < 0, col + W, col - rows_dev)
            at = jnp.where(inside, col, halo)
            band_ref[rows, pl.ds(pl.multiple_of(at * block, block), block)] = hop_ref[r, k]
    image_ref[...] = mm(band_ref[:, :wide], xa_ref[...]) + mm(band_ref[:, wide:2 * wide], xb_ref[...])


def band_parts(hop, pattern, counts, center, halfwidth, xa, xb, total_blocks):
    rows_dev, _, block, _ = hop.shape
    wide, tall, half = W * block, rows_dev * block, xa.shape[1]
    return call(
        functools.partial(band_kernel, total_blocks),
        (
            jax.ShapeDtypeStruct((tall, 3 * wide), hop.dtype),
            jax.ShapeDtypeStruct((tall, half), jnp.float32),
            jax.ShapeDtypeStruct((8, half), jnp.float32),
        ),
        [SMEM] * 4 + [VMEM] * 3,
    )(counts, center, halfwidth, pattern, hop, xa, xb)


def halo_image(side, band_ref, image_ref, halo_ref):
    wide = halo_ref.shape[0]
    rows = slice(side * wide, (side + 1) * wide)
    return image_ref[rows, :] + mm(band_ref[rows, 2 * wide:], halo_ref[...])


def step_kernel(side, table_ref, image_ref, band_ref, halo_ref, x_ref, out_ref):
    shift, width = table_ref[0:1, :], table_ref[1:2, :]
    image = halo_image(side, band_ref, image_ref, halo_ref)
    out_ref[...] = ((image - shift * x_ref[...].astype(jnp.float32)) / width).astype(jnp.bfloat16)


def step(side, table, image, band, halo, x):
    shape = jax.ShapeDtypeStruct(x.shape, jnp.bfloat16)
    return call(functools.partial(step_kernel, side), shape, [VMEM] * 5)(table, image, band, halo, x)


def finish_kernel(side, table_ref, image_ref, band_ref, halo_ref, s_ref, x_ref, out_ref):
    shift, width = table_ref[0:1, :], table_ref[1:2, :]
    live = table_ref[2:3, :] > 0.0
    image = halo_image(side, band_ref, image_ref, halo_ref)
    value = 2.0 * (image - shift * s_ref[...].astype(jnp.float32)) / width - x_ref[...].astype(jnp.float32)
    out_ref[...] = jnp.where(live, value, 0.0).astype(jnp.bfloat16)


def finish(side, table, image, band, halo, s, x):
    shape = jax.ShapeDtypeStruct(x.shape, jnp.bfloat16)
    return call(functools.partial(finish_kernel, side), shape, [VMEM] * 6)(table, image, band, halo, s, x)


def exponent(*values):
    top = functools.reduce(jnp.maximum, [jnp.abs(value) for value in values])
    top = jnp.max(top, axis=(0, 1), keepdims=True)
    return jnp.clip(jnp.ceil(jnp.log2(jnp.maximum(top, 1e-36))) - 14.0, -100.0, 60.0)


def with_code(share, same, e):
    row = lax.broadcasted_iota(jnp.int32, same.shape, 0)
    col = lax.broadcasted_iota(jnp.int32, same.shape, 1)
    slot = (lax.rem(row, share) == 1) & (col == row - 1)
    return jnp.where(slot, e, same * jnp.exp2(-e))


def early_kernel(fa_ref, fb_ref, oa_ref, out_ref):
    half = fa_ref.shape[1]
    fa, fb = fa_ref[...], fb_ref[...]
    out_ref[:, :half] = tmm(fa, fa) + tmm(fb, fb)
    out_ref[:, half:] = tmm(fa, oa_ref[...])


def early_terms(fa, fb, oa):
    half = fa.shape[1]
    shape = jax.ShapeDtypeStruct((half, 2 * half), jnp.float32)
    return call(early_kernel, shape, [VMEM] * 3)(fa, fb, oa)


def code_kernel(share, early_ref, fb_ref, ob_ref, out_ref):
    half = fb_ref.shape[1]
    same = early_ref[:, :half]
    cross = early_ref[:, half:] + tmm(fb_ref[...], ob_ref[...])
    e = exponent(same, cross)
    out_ref[:, :half] = with_code(share, same, e)
    out_ref[:, half:] = cross * jnp.exp2(-e)


def code_terms(early, fb, ob, share):
    shape = jax.ShapeDtypeStruct(early.shape, jnp.float32)
    return call(functools.partial(code_kernel, share), shape, [VMEM] * 3)(early, fb, ob)


def slots(shape):
    start = lax.axis_index("row") * shape[0]
    row = lax.broadcasted_iota(jnp.int32, (8, shape[1]), 0)
    col = lax.broadcasted_iota(jnp.int32, (8, shape[1]), 1)
    return (row == 1) & (col == start), (row == 0) & (col == start + 1)


def slot_factor(ref, slot, order_total):
    e = jnp.sum(jnp.where(slot, ref[:8, :slot.shape[1]], 0.0), axis=(0, 1), keepdims=True)
    return jnp.exp2(e) / order_total


def first_sum_kernel(order_total, coded_ref, piece_ref, out_ref):
    share, half = out_ref.shape[0], out_ref.shape[1] // 2
    slot, _ = slots((share, half))
    mine = coded_ref.at[pl.ds(pl.multiple_of(lax.axis_index("row") * share, 8), share), :]
    total = mine[...] * slot_factor(mine, slot, order_total)
    out_ref[...] = total + piece_ref[...] * slot_factor(piece_ref, slot, order_total)


def first_sum(coded, piece, order_total):
    shape = jax.ShapeDtypeStruct(piece.shape, jnp.float32)
    return call(functools.partial(first_sum_kernel, order_total), shape, [VMEM] * 2, LONG)(coded, piece)


def add_kernel(order_total, sum_ref, piece_ref, out_ref):
    share, columns = sum_ref.shape
    slot, _ = slots((share, columns // 2))
    out_ref[...] = sum_ref[...] + piece_ref[...] * slot_factor(piece_ref, slot, order_total)


def add_piece(total, piece, order_total):
    shape = jax.ShapeDtypeStruct(total.shape, jnp.float32)
    return call(functools.partial(add_kernel, order_total), shape, [VMEM] * 2, LONG)(total, piece)


def last_kernel(order_total, sum_ref, piece_ref, out_ref):
    share, half = out_ref.shape[0], out_ref.shape[1] // 2
    slot, twin = slots((share, half))
    factor = slot_factor(piece_ref, slot, order_total)
    sub = lax.axis_index("sub")
    at = pl.ds(pl.multiple_of(sub * half, half), half)
    other = pl.ds(pl.multiple_of((1 - sub) * half, half), half)
    out_ref[:, other] = sum_ref[:, half:] + piece_ref[:, half:] * factor
    same = sum_ref[:, :half] + piece_ref[:, :half] * factor
    out_ref[:, at] = same
    lost = jnp.sum(jnp.where(twin, same[:8], 0.0), axis=(0, 1), keepdims=True)
    out_ref[:8, at] = jnp.where(slot, lost, same[:8])


def last_sum(total, piece, order_total):
    shape = jax.ShapeDtypeStruct(total.shape, jnp.float32)
    return call(functools.partial(last_kernel, order_total), shape, [VMEM] * 2)(total, piece)


def image_kernel(band_ref, sa_ref, sb_ref, out_ref):
    wide = sa_ref.shape[0]
    out_ref[...] = mm(band_ref[:, :wide], sa_ref[...]) + mm(band_ref[:, wide:2 * wide], sb_ref[...])


def own_image(band, sa, sb):
    shape = jax.ShapeDtypeStruct((band.shape[0], sa.shape[1]), jnp.float32)
    return call(image_kernel, shape, [VMEM] * 3)(band, sa, sb)


def send_shares(coded, row_count, share):
    me = lax.axis_index("row")
    arrived = []
    for shift in range(1, row_count):
        part = lax.dynamic_slice_in_dim(coded, (me + shift) % row_count * share, share, axis=0)
        ring = [(i, (i + shift) % row_count) for i in range(row_count)]
        arrived.append(lax.ppermute(part, "row", ring))
    return arrived


def body(hop, pattern, vectors, counts, center, halfwidth):
    rows_dev = hop.shape[0]
    block = hop.shape[2]
    half = vectors.shape[2]
    row_count = lax.axis_size("row")
    total_blocks = rows_dev * row_count
    order_total = total_blocks * block
    wide = W * block
    share = half // row_count
    assert rows_dev == 2 * W
    forward = [(i, (i + 1) % row_count) for i in range(row_count)]
    backward = [(target, source) for source, target in forward]
    swap = [(0, 1), (1, 0)]

    def halos_of(low, high):
        return lax.ppermute(high, "row", forward), lax.ppermute(low, "row", backward)

    x = vectors[0]
    xa, xb = x[:wide], x[wide:]
    halo_a, halo_b = halos_of(xa, xb)
    band, image, table = band_parts(hop, pattern, counts, center, halfwidth, xa, xb, total_blocks)
    halo_a, halo_b = lax.optimization_barrier((halo_a, halo_b))
    sb = step(1, table, image, band, halo_b, xb)
    sa = step(0, table, image, band, lax.optimization_barrier((halo_a, sb))[0], xa)
    halo_a, halo_b = halos_of(sa, sb)
    image = own_image(band, sa, sb)
    fa = finish(0, table, image, band, halo_a, sa, xa)
    oa = lax.ppermute(fa, "sub", swap)
    fb = finish(1, table, image, band, lax.optimization_barrier((halo_b, fa))[0], sb, xb)
    ob = lax.ppermute(fb, "sub", swap)
    coded = code_terms(early_terms(fa, fb, oa), fb, ob, share)
    first, *middle, last = send_shares(coded.astype(jnp.float16), row_count, share)
    total = first_sum(coded, first.astype(jnp.float32), order_total)
    for piece in middle:
        total = add_piece(total, piece.astype(jnp.float32), order_total)
    total, last = lax.optimization_barrier((total, last))
    margin = last_sum(total, last.astype(jnp.float32), order_total)
    return margin.reshape(1, 1, share, 2 * half)


def solution(mesh):
    in_specs = (
        P(("groups", "row"), None, None, None),
        P(("groups", "row"), None),
        P("cuts", ("groups", "row"), "sub"),
        P(("groups", "cuts")),
        P(("groups", "cuts")),
        P(("groups", "cuts")),
    )
    out_specs = P(("groups", "cuts"), "sub", "row", None)
    return jax.shard_map(body, mesh=mesh, in_specs=in_specs, out_specs=out_specs, check_vma=False)
```

```python
import functools

import jax
import jax.numpy as jnp
from jax import lax
from jax.experimental import pallas as pl
from jax.experimental.pallas import tpu as pltpu
from jax.sharding import PartitionSpec as P

W = 3
LIMIT = 16 * 1024 * 1024
COST = pl.CostEstimate(flops=1000, bytes_accessed=1000, transcendentals=0)
LONG = pl.CostEstimate(flops=20_000_000_000, bytes_accessed=1000, transcendentals=0)
VMEM = pl.BlockSpec(memory_space=pltpu.VMEM)
SMEM = pl.BlockSpec(memory_space=pltpu.SMEM)


def call(kernel, out_shape, in_specs, cost=COST):
    return pl.pallas_call(
        kernel,
        out_shape=out_shape,
        in_specs=in_specs,
        out_specs=jax.tree.map(lambda _: VMEM, out_shape),
        compiler_params=pltpu.CompilerParams(vmem_limit_bytes=LIMIT),
        cost_estimate=cost,
    )


def mm(a, b):
    return jnp.dot(a, b, preferred_element_type=jnp.float32)


def tmm(a, b):
    return lax.dot_general(a, b, (((0,), (0,)), ((), ())), preferred_element_type=jnp.float32)


def band_kernel(total_blocks, counts_ref, center_ref, width_ref, pattern_ref, hop_ref, xa_ref, xb_ref, band_ref, image_ref, table_ref):
    rows_dev, stored, block, _ = hop_ref.shape
    wide = W * block
    first_block = lax.axis_index("row") * rows_dev
    band_ref[...] = jnp.zeros_like(band_ref)
    half = xa_ref.shape[1]
    line = lax.broadcasted_iota(jnp.int32, (8, half), 0)
    column = lax.broadcasted_iota(jnp.int32, (8, half), 1) + lax.axis_index("sub") * half
    live = jnp.where(column < counts_ref[0], 1.0, 0.0)
    table_ref[...] = jnp.where(line == 0, center_ref[0], jnp.where(line == 1, width_ref[0], live))
    for r in range(rows_dev):
        rows = slice(r * block, (r + 1) * block)
        for k in range(stored):
            col = lax.rem(pattern_ref[r, k] - first_block + (W + total_blocks), total_blocks) - W
            inside = jnp.logical_and(col >= 0, col < rows_dev)
            halo = 2 * W + jnp.where(col < 0, col + W, col - rows_dev)
            at = jnp.where(inside, col, halo)
            band_ref[rows, pl.ds(pl.multiple_of(at * block, block), block)] = hop_ref[r, k]
    image_ref[...] = mm(band_ref[:, :wide], xa_ref[...]) + mm(band_ref[:, wide:2 * wide], xb_ref[...])


def band_parts(hop, pattern, counts, center, halfwidth, xa, xb, total_blocks):
    rows_dev, _, block, _ = hop.shape
    wide, tall, half = W * block, rows_dev * block, xa.shape[1]
    return call(
        functools.partial(band_kernel, total_blocks),
        (
            jax.ShapeDtypeStruct((tall, 3 * wide), hop.dtype),
            jax.ShapeDtypeStruct((tall, half), jnp.float32),
            jax.ShapeDtypeStruct((8, half), jnp.float32),
        ),
        [SMEM] * 4 + [VMEM] * 3,
    )(counts, center, halfwidth, pattern, hop, xa, xb)


def halo_image(side, band_ref, image_ref, halo_ref):
    wide = halo_ref.shape[0]
    rows = slice(side * wide, (side + 1) * wide)
    return image_ref[rows, :] + mm(band_ref[rows, 2 * wide:], halo_ref[...])


def step_kernel(side, table_ref, image_ref, band_ref, halo_ref, x_ref, out_ref):
    shift, width = table_ref[0:1, :], table_ref[1:2, :]
    image = halo_image(side, band_ref, image_ref, halo_ref)
    out_ref[...] = ((image - shift * x_ref[...].astype(jnp.float32)) / width).astype(jnp.bfloat16)


def step(side, table, image, band, halo, x):
    shape = jax.ShapeDtypeStruct(x.shape, jnp.bfloat16)
    return call(functools.partial(step_kernel, side), shape, [VMEM] * 5)(table, image, band, halo, x)


def finish_kernel(side, table_ref, image_ref, band_ref, halo_ref, s_ref, x_ref, out_ref):
    shift, width = table_ref[0:1, :], table_ref[1:2, :]
    live = table_ref[2:3, :] > 0.0
    image = halo_image(side, band_ref, image_ref, halo_ref)
    value = 2.0 * (image - shift * s_ref[...].astype(jnp.float32)) / width - x_ref[...].astype(jnp.float32)
    out_ref[...] = jnp.where(live, value, 0.0).astype(jnp.bfloat16)


def finish(side, table, image, band, halo, s, x):
    shape = jax.ShapeDtypeStruct(x.shape, jnp.bfloat16)
    return call(functools.partial(finish_kernel, side), shape, [VMEM] * 6)(table, image, band, halo, s, x)


def exponent(*values):
    top = functools.reduce(jnp.maximum, [jnp.abs(value) for value in values])
    top = jnp.max(top, axis=(0, 1), keepdims=True)
    return jnp.clip(jnp.ceil(jnp.log2(jnp.maximum(top, 1e-36))) - 14.0, -100.0, 60.0)


def with_code(share, same, e):
    row = lax.broadcasted_iota(jnp.int32, same.shape, 0)
    col = lax.broadcasted_iota(jnp.int32, same.shape, 1)
    slot = (lax.rem(row, share) == 1) & (col == row - 1)
    return jnp.where(slot, e, same * jnp.exp2(-e))


def early_kernel(fa_ref, fb_ref, oa_ref, out_ref):
    half = fa_ref.shape[1]
    fa, fb = fa_ref[...], fb_ref[...]
    out_ref[:, :half] = tmm(fa, fa) + tmm(fb, fb)
    out_ref[:, half:] = tmm(fa, oa_ref[...])


def early_terms(fa, fb, oa):
    half = fa.shape[1]
    shape = jax.ShapeDtypeStruct((half, 2 * half), jnp.float32)
    return call(early_kernel, shape, [VMEM] * 3)(fa, fb, oa)


def code_kernel(share, early_ref, fb_ref, ob_ref, out_ref):
    half = fb_ref.shape[1]
    same = early_ref[:, :half]
    cross = early_ref[:, half:] + tmm(fb_ref[...], ob_ref[...])
    e = exponent(same, cross)
    out_ref[:, :half] = with_code(share, same, e)
    out_ref[:, half:] = cross * jnp.exp2(-e)


def code_terms(early, fb, ob, share):
    shape = jax.ShapeDtypeStruct(early.shape, jnp.float32)
    return call(functools.partial(code_kernel, share), shape, [VMEM] * 3)(early, fb, ob)


def slots(shape):
    start = lax.axis_index("row") * shape[0]
    row = lax.broadcasted_iota(jnp.int32, (8, shape[1]), 0)
    col = lax.broadcasted_iota(jnp.int32, (8, shape[1]), 1)
    return (row == 1) & (col == start), (row == 0) & (col == start + 1)


def slot_factor(ref, slot, order_total):
    e = jnp.sum(jnp.where(slot, ref[:8, :slot.shape[1]], 0.0), axis=(0, 1), keepdims=True)
    return jnp.exp2(e) / order_total


def first_sum_kernel(order_total, coded_ref, piece_ref, out_ref):
    share, half = out_ref.shape[0], out_ref.shape[1] // 2
    slot, _ = slots((share, half))
    mine = coded_ref.at[pl.ds(pl.multiple_of(lax.axis_index("row") * share, 8), share), :]
    total = mine[...] * slot_factor(mine, slot, order_total)
    out_ref[...] = total + piece_ref[...] * slot_factor(piece_ref, slot, order_total)


def first_sum(coded, piece, order_total):
    shape = jax.ShapeDtypeStruct(piece.shape, jnp.float32)
    return call(functools.partial(first_sum_kernel, order_total), shape, [VMEM] * 2, LONG)(coded, piece)


def add_kernel(order_total, sum_ref, piece_ref, out_ref):
    share, columns = sum_ref.shape
    slot, _ = slots((share, columns // 2))
    out_ref[...] = sum_ref[...] + piece_ref[...] * slot_factor(piece_ref, slot, order_total)


def add_piece(total, piece, order_total):
    shape = jax.ShapeDtypeStruct(total.shape, jnp.float32)
    return call(functools.partial(add_kernel, order_total), shape, [VMEM] * 2, LONG)(total, piece)


def last_kernel(order_total, sum_ref, piece_ref, out_ref):
    share, half = out_ref.shape[0], out_ref.shape[1] // 2
    slot, twin = slots((share, half))
    factor = slot_factor(piece_ref, slot, order_total)
    sub = lax.axis_index("sub")
    at = pl.ds(pl.multiple_of(sub * half, half), half)
    other = pl.ds(pl.multiple_of((1 - sub) * half, half), half)
    out_ref[:, other] = sum_ref[:, half:] + piece_ref[:, half:] * factor
    same = sum_ref[:, :half] + piece_ref[:, :half] * factor
    out_ref[:, at] = same
    lost = jnp.sum(jnp.where(twin, same[:8], 0.0), axis=(0, 1), keepdims=True)
    out_ref[:8, at] = jnp.where(slot, lost, same[:8])


def last_sum(total, piece, order_total):
    shape = jax.ShapeDtypeStruct(total.shape, jnp.float32)
    return call(functools.partial(last_kernel, order_total), shape, [VMEM] * 2)(total, piece)


def image_kernel(band_ref, sa_ref, sb_ref, out_ref):
    wide = sa_ref.shape[0]
    out_ref[...] = mm(band_ref[:, :wide], sa_ref[...]) + mm(band_ref[:, wide:2 * wide], sb_ref[...])


def own_image(band, sa, sb):
    shape = jax.ShapeDtypeStruct((band.shape[0], sa.shape[1]), jnp.float32)
    return call(image_kernel, shape, [VMEM] * 3)(band, sa, sb)


def send_shares(coded, row_count, share):
    me = lax.axis_index("row")
    arrived = []
    for shift in range(1, row_count):
        part = lax.dynamic_slice_in_dim(coded, (me + shift) % row_count * share, share, axis=0)
        ring = [(i, (i + shift) % row_count) for i in range(row_count)]
        arrived.append(lax.ppermute(part, "row", ring))
    return arrived


def body(hop, pattern, vectors, counts, center, halfwidth):
    rows_dev = hop.shape[0]
    block = hop.shape[2]
    half = vectors.shape[2]
    row_count = lax.axis_size("row")
    total_blocks = rows_dev * row_count
    order_total = total_blocks * block
    wide = W * block
    share = half // row_count
    assert rows_dev == 2 * W
    forward = [(i, (i + 1) % row_count) for i in range(row_count)]
    backward = [(target, source) for source, target in forward]
    swap = [(0, 1), (1, 0)]

    def halos_of(low, high):
        return lax.ppermute(high, "row", forward), lax.ppermute(low, "row", backward)

    x = vectors[0]
    xa, xb = x[:wide], x[wide:]
    halo_a, halo_b = halos_of(xa, xb)
    band, image, table = band_parts(hop, pattern, counts, center, halfwidth, xa, xb, total_blocks)
    sb = step(1, table, image, band, halo_b, xb)
    sa = step(0, table, image, band, lax.optimization_barrier((halo_a, sb))[0], xa)
    halo_a, halo_b = halos_of(sa, sb)
    image = own_image(band, sa, sb)
    fa = finish(0, table, image, band, halo_a, sa, xa)
    oa = lax.ppermute(fa, "sub", swap)
    fb = finish(1, table, image, band, lax.optimization_barrier((halo_b, fa))[0], sb, xb)
    ob = lax.ppermute(fb, "sub", swap)
    coded = code_terms(early_terms(fa, fb, oa), fb, ob, share)
    first, *middle, last = send_shares(coded.astype(jnp.float16), row_count, share)
    total = first_sum(coded, first.astype(jnp.float32), order_total)
    for piece in middle:
        total = add_piece(total, piece.astype(jnp.float32), order_total)
    total, last = lax.optimization_barrier((total, last))
    margin = last_sum(total, last.astype(jnp.float32), order_total)
    return margin.reshape(1, 1, share, 2 * half)


def solution(mesh):
    in_specs = (
        P(("groups", "row"), None, None, None),
        P(("groups", "row"), None),
        P("cuts", ("groups", "row"), "sub"),
        P(("groups", "cuts")),
        P(("groups", "cuts")),
        P(("groups", "cuts")),
    )
    out_specs = P(("groups", "cuts"), "sub", "row", None)
    return jax.shard_map(body, mesh=mesh, in_specs=in_specs, out_specs=out_specs, check_vma=False)
```

```python
import functools

import jax
import jax.numpy as jnp
from jax import lax
from jax.experimental import pallas as pl
from jax.experimental.pallas import tpu as pltpu
from jax.sharding import PartitionSpec as P

W = 3
LIMIT = 16 * 1024 * 1024
COST = pl.CostEstimate(flops=1000, bytes_accessed=1000, transcendentals=0)
LONG = pl.CostEstimate(flops=20_000_000_000, bytes_accessed=1000, transcendentals=0)
VMEM = pl.BlockSpec(memory_space=pltpu.VMEM)
SMEM = pl.BlockSpec(memory_space=pltpu.SMEM)


def call(kernel, out_shape, in_specs, cost=COST):
    return pl.pallas_call(
        kernel,
        out_shape=out_shape,
        in_specs=in_specs,
        out_specs=jax.tree.map(lambda _: VMEM, out_shape),
        compiler_params=pltpu.CompilerParams(vmem_limit_bytes=LIMIT),
        cost_estimate=cost,
    )


def mm(a, b):
    return jnp.dot(a, b, preferred_element_type=jnp.float32)


def tmm(a, b):
    return lax.dot_general(a, b, (((0,), (0,)), ((), ())), preferred_element_type=jnp.float32)


def table_kernel(counts_ref, center_ref, width_ref, table_ref):
    half = table_ref.shape[1]
    line = lax.broadcasted_iota(jnp.int32, (8, half), 0)
    column = lax.broadcasted_iota(jnp.int32, (8, half), 1) + lax.axis_index("sub") * half
    live = jnp.where(column < counts_ref[0], 1.0, 0.0)
    table_ref[...] = jnp.where(line == 0, center_ref[0], jnp.where(line == 1, width_ref[0], live))


def table_of(counts, center, halfwidth, half):
    shape = jax.ShapeDtypeStruct((8, half), jnp.float32)
    return call(table_kernel, shape, [SMEM] * 3, LONG)(counts, center, halfwidth)


def band_kernel(total_blocks, pattern_ref, hop_ref, xa_ref, xb_ref, band_ref, image_ref):
    rows_dev, stored, block, _ = hop_ref.shape
    wide = W * block
    first_block = lax.axis_index("row") * rows_dev
    band_ref[...] = jnp.zeros_like(band_ref)
    for r in range(rows_dev):
        rows = slice(r * block, (r + 1) * block)
        for k in range(stored):
            col = lax.rem(pattern_ref[r, k] - first_block + (W + total_blocks), total_blocks) - W
            inside = jnp.logical_and(col >= 0, col < rows_dev)
            halo = 2 * W + jnp.where(col < 0, col + W, col - rows_dev)
            at = jnp.where(inside, col, halo)
            band_ref[rows, pl.ds(pl.multiple_of(at * block, block), block)] = hop_ref[r, k]
    image_ref[...] = mm(band_ref[:, :wide], xa_ref[...]) + mm(band_ref[:, wide:2 * wide], xb_ref[...])


def band_parts(hop, pattern, xa, xb, total_blocks):
    rows_dev, _, block, _ = hop.shape
    wide, tall, half = W * block, rows_dev * block, xa.shape[1]
    return call(
        functools.partial(band_kernel, total_blocks),
        (
            jax.ShapeDtypeStruct((tall, 3 * wide), hop.dtype),
            jax.ShapeDtypeStruct((tall, half), jnp.float32),
        ),
        [SMEM] + [VMEM] * 3,
    )(pattern, hop, xa, xb)


def halo_image(side, band_ref, image_ref, halo_ref):
    wide = halo_ref.shape[0]
    rows = slice(side * wide, (side + 1) * wide)
    return image_ref[rows, :] + mm(band_ref[rows, 2 * wide:], halo_ref[...])


def step_kernel(side, table_ref, image_ref, band_ref, halo_ref, x_ref, out_ref):
    shift, width = table_ref[0:1, :], table_ref[1:2, :]
    image = halo_image(side, band_ref, image_ref, halo_ref)
    out_ref[...] = ((image - shift * x_ref[...].astype(jnp.float32)) / width).astype(jnp.bfloat16)


def step(side, table, image, band, halo, x):
    shape = jax.ShapeDtypeStruct(x.shape, jnp.bfloat16)
    return call(functools.partial(step_kernel, side), shape, [VMEM] * 5)(table, image, band, halo, x)


def finish_kernel(side, table_ref, image_ref, band_ref, halo_ref, s_ref, x_ref, out_ref):
    shift, width = table_ref[0:1, :], table_ref[1:2, :]
    live = table_ref[2:3, :] > 0.0
    image = halo_image(side, band_ref, image_ref, halo_ref)
    value = 2.0 * (image - shift * s_ref[...].astype(jnp.float32)) / width - x_ref[...].astype(jnp.float32)
    out_ref[...] = jnp.where(live, value, 0.0).astype(jnp.bfloat16)


def finish(side, table, image, band, halo, s, x):
    shape = jax.ShapeDtypeStruct(x.shape, jnp.bfloat16)
    return call(functools.partial(finish_kernel, side), shape, [VMEM] * 6)(table, image, band, halo, s, x)


def exponent(*values):
    top = functools.reduce(jnp.maximum, [jnp.abs(value) for value in values])
    top = jnp.max(top, axis=(0, 1), keepdims=True)
    return jnp.clip(jnp.ceil(jnp.log2(jnp.maximum(top, 1e-36))) - 14.0, -100.0, 60.0)


def with_code(share, same, e):
    row = lax.broadcasted_iota(jnp.int32, same.shape, 0)
    col = lax.broadcasted_iota(jnp.int32, same.shape, 1)
    slot = (lax.rem(row, share) == 1) & (col == row - 1)
    return jnp.where(slot, e, same * jnp.exp2(-e))


def early_kernel(fa_ref, fb_ref, ob_ref, out_ref):
    half = fa_ref.shape[1]
    fa, fb = fa_ref[...], fb_ref[...]
    out_ref[:, :half] = tmm(fa, fa) + tmm(fb, fb)
    out_ref[:, half:] = tmm(fb, ob_ref[...])


def early_terms(fa, fb, ob):
    half = fa.shape[1]
    shape = jax.ShapeDtypeStruct((half, 2 * half), jnp.float32)
    return call(early_kernel, shape, [VMEM] * 3)(fa, fb, ob)


def code_kernel(share, early_ref, fa_ref, oa_ref, out_ref):
    half = fa_ref.shape[1]
    same = early_ref[:, :half]
    cross = early_ref[:, half:] + tmm(fa_ref[...], oa_ref[...])
    e = exponent(same, cross)
    out_ref[:, :half] = with_code(share, same, e)
    out_ref[:, half:] = cross * jnp.exp2(-e)


def code_terms(early, fa, oa, share):
    shape = jax.ShapeDtypeStruct(early.shape, jnp.float32)
    return call(functools.partial(code_kernel, share), shape, [VMEM] * 3)(early, fa, oa)


def slots(shape):
    start = lax.axis_index("row") * shape[0]
    row = lax.broadcasted_iota(jnp.int32, (8, shape[1]), 0)
    col = lax.broadcasted_iota(jnp.int32, (8, shape[1]), 1)
    return (row == 1) & (col == start), (row == 0) & (col == start + 1)


def slot_factor(ref, slot, order_total):
    e = jnp.sum(jnp.where(slot, ref[:8, :slot.shape[1]], 0.0), axis=(0, 1), keepdims=True)
    return jnp.exp2(e) / order_total


def first_sum_kernel(order_total, coded_ref, piece_ref, out_ref):
    share, half = out_ref.shape[0], out_ref.shape[1] // 2
    slot, _ = slots((share, half))
    mine = coded_ref.at[pl.ds(pl.multiple_of(lax.axis_index("row") * share, 8), share), :]
    total = mine[...] * slot_factor(mine, slot, order_total)
    out_ref[...] = total + piece_ref[...] * slot_factor(piece_ref, slot, order_total)


def first_sum(coded, piece, order_total):
    shape = jax.ShapeDtypeStruct(piece.shape, jnp.float32)
    return call(functools.partial(first_sum_kernel, order_total), shape, [VMEM] * 2, LONG)(coded, piece)


def add_kernel(order_total, sum_ref, piece_ref, out_ref):
    share, columns = sum_ref.shape
    slot, _ = slots((share, columns // 2))
    out_ref[...] = sum_ref[...] + piece_ref[...] * slot_factor(piece_ref, slot, order_total)


def add_piece(total, piece, order_total):
    shape = jax.ShapeDtypeStruct(total.shape, jnp.float32)
    return call(functools.partial(add_kernel, order_total), shape, [VMEM] * 2, LONG)(total, piece)


def last_kernel(order_total, sum_ref, piece_ref, out_ref):
    share, half = out_ref.shape[0], out_ref.shape[1] // 2
    slot, twin = slots((share, half))
    factor = slot_factor(piece_ref, slot, order_total)
    sub = lax.axis_index("sub")
    at = pl.ds(pl.multiple_of(sub * half, half), half)
    other = pl.ds(pl.multiple_of((1 - sub) * half, half), half)
    out_ref[:, other] = sum_ref[:, half:] + piece_ref[:, half:] * factor
    same = sum_ref[:, :half] + piece_ref[:, :half] * factor
    out_ref[:, at] = same
    lost = jnp.sum(jnp.where(twin, same[:8], 0.0), axis=(0, 1), keepdims=True)
    out_ref[:8, at] = jnp.where(slot, lost, same[:8])


def last_sum(total, piece, order_total):
    shape = jax.ShapeDtypeStruct(total.shape, jnp.float32)
    return call(functools.partial(last_kernel, order_total), shape, [VMEM] * 2)(total, piece)


def image_kernel(band_ref, sa_ref, sb_ref, out_ref):
    wide = sa_ref.shape[0]
    out_ref[...] = mm(band_ref[:, :wide], sa_ref[...]) + mm(band_ref[:, wide:2 * wide], sb_ref[...])


def own_image(band, sa, sb):
    shape = jax.ShapeDtypeStruct((band.shape[0], sa.shape[1]), jnp.float32)
    return call(image_kernel, shape, [VMEM] * 3)(band, sa, sb)


def send_shares(coded, row_count, share):
    me = lax.axis_index("row")
    arrived = []
    for shift in range(1, row_count):
        part = lax.dynamic_slice_in_dim(coded, (me + shift) % row_count * share, share, axis=0)
        ring = [(i, (i + shift) % row_count) for i in range(row_count)]
        arrived.append(lax.ppermute(part, "row", ring))
    return arrived


def body(hop, pattern, vectors, counts, center, halfwidth):
    rows_dev = hop.shape[0]
    block = hop.shape[2]
    half = vectors.shape[2]
    row_count = lax.axis_size("row")
    total_blocks = rows_dev * row_count
    order_total = total_blocks * block
    wide = W * block
    share = half // row_count
    assert rows_dev == 2 * W
    forward = [(i, (i + 1) % row_count) for i in range(row_count)]
    backward = [(target, source) for source, target in forward]
    swap = [(0, 1), (1, 0)]

    def halos_of(low, high):
        return lax.ppermute(high, "row", forward), lax.ppermute(low, "row", backward)

    x = vectors[0]
    xa, xb = x[:wide], x[wide:]
    table = table_of(counts, center, halfwidth, half)
    halo_a, halo_b = halos_of(lax.optimization_barrier((xa, table))[0], xb)
    band, image = band_parts(hop, pattern, xa, xb, total_blocks)
    sa = step(0, table, image, band, halo_a, xa)
    sb = step(1, table, image, band, halo_b, xb)
    halo_a, halo_b = halos_of(sa, sb)
    image = own_image(band, sa, sb)
    fa = finish(0, table, image, band, halo_a, sa, xa)
    oa = lax.ppermute(fa, "sub", swap)
    fb = finish(1, table, image, band, halo_b, sb, xb)
    ob = lax.ppermute(fb, "sub", swap)
    coded = code_terms(early_terms(fa, fb, ob), fa, oa, share)
    first, *middle, last = send_shares(coded.astype(jnp.float16), row_count, share)
    total = first_sum(coded, first.astype(jnp.float32), order_total)
    for piece in middle:
        total = add_piece(total, piece.astype(jnp.float32), order_total)
    total, last = lax.optimization_barrier((total, last))
    margin = last_sum(total, last.astype(jnp.float32), order_total)
    return margin.reshape(1, 1, share, 2 * half)


def solution(mesh):
    in_specs = (
        P(("groups", "row"), None, None, None),
        P(("groups", "row"), None),
        P("cuts", ("groups", "row"), "sub"),
        P(("groups", "cuts")),
        P(("groups", "cuts")),
        P(("groups", "cuts")),
    )
    out_specs = P(("groups", "cuts"), "sub", "row", None)
    return jax.shard_map(body, mesh=mesh, in_specs=in_specs, out_specs=out_specs, check_vma=False)
```

```python
import functools

import jax
import jax.numpy as jnp
from jax import lax
from jax.experimental import pallas as pl
from jax.experimental.pallas import tpu as pltpu
from jax.sharding import PartitionSpec as P

W = 3
LIMIT = 16 * 1024 * 1024
COST = pl.CostEstimate(flops=1000, bytes_accessed=1000, transcendentals=0)
LONG = pl.CostEstimate(flops=20_000_000_000, bytes_accessed=1000, transcendentals=0)
VMEM = pl.BlockSpec(memory_space=pltpu.VMEM)
SMEM = pl.BlockSpec(memory_space=pltpu.SMEM)


def call(kernel, out_shape, in_specs, cost=COST):
    return pl.pallas_call(
        kernel,
        out_shape=out_shape,
        in_specs=in_specs,
        out_specs=jax.tree.map(lambda _: VMEM, out_shape),
        compiler_params=pltpu.CompilerParams(vmem_limit_bytes=LIMIT),
        cost_estimate=cost,
    )


def mm(a, b):
    return jnp.dot(a, b, preferred_element_type=jnp.float32)


def tmm(a, b):
    return lax.dot_general(a, b, (((0,), (0,)), ((), ())), preferred_element_type=jnp.float32)


def side_of_low():
    return 1 - lax.axis_index("sub")


def band_kernel(total_blocks, counts_ref, center_ref, width_ref, pattern_ref, hop_ref, xa_ref, xb_ref, band_ref, image_ref, table_ref):
    rows_dev, stored, block, _ = hop_ref.shape
    wide = W * block
    first_block = lax.axis_index("row") * rows_dev
    low = side_of_low()
    band_ref[...] = jnp.zeros_like(band_ref)
    half = xa_ref.shape[1]
    line = lax.broadcasted_iota(jnp.int32, (8, half), 0)
    column = lax.broadcasted_iota(jnp.int32, (8, half), 1) + lax.axis_index("sub") * half
    live = jnp.where(column < counts_ref[0], 1.0, 0.0)
    table_ref[...] = jnp.where(line == 0, center_ref[0], jnp.where(line == 1, width_ref[0], live))
    for r in range(rows_dev):
        side = low if r < W else 1 - low
        rows = pl.ds(pl.multiple_of(side * wide + (r % W) * block, block), block)
        for k in range(stored):
            col = lax.rem(pattern_ref[r, k] - first_block + (W + total_blocks), total_blocks) - W
            in_low = jnp.logical_and(col >= 0, col < W)
            in_high = jnp.logical_and(col >= W, col < rows_dev)
            at = jnp.where(
                in_low, low * W + col,
                jnp.where(in_high, (1 - low) * W + col - W, 2 * W + jnp.where(col < 0, col + W, col - rows_dev)),
            )
            band_ref[rows, pl.ds(pl.multiple_of(at * block, block), block)] = hop_ref[r, k]
    image_ref[...] = mm(band_ref[:, :wide], xa_ref[...]) + mm(band_ref[:, wide:2 * wide], xb_ref[...])


def band_parts(hop, pattern, counts, center, halfwidth, xa, xb, total_blocks):
    rows_dev, _, block, _ = hop.shape
    wide, tall, half = W * block, rows_dev * block, xa.shape[1]
    return call(
        functools.partial(band_kernel, total_blocks),
        (
            jax.ShapeDtypeStruct((tall, 3 * wide), hop.dtype),
            jax.ShapeDtypeStruct((tall, half), jnp.float32),
            jax.ShapeDtypeStruct((8, half), jnp.float32),
        ),
        [SMEM] * 4 + [VMEM] * 3,
    )(counts, center, halfwidth, pattern, hop, xa, xb)


def halo_image(side, band_ref, image_ref, halo_ref):
    wide = halo_ref.shape[0]
    rows = slice(side * wide, (side + 1) * wide)
    return image_ref[rows, :] + mm(band_ref[rows, 2 * wide:], halo_ref[...])


def step_kernel(side, table_ref, image_ref, band_ref, halo_ref, x_ref, out_ref):
    shift, width = table_ref[0:1, :], table_ref[1:2, :]
    image = halo_image(side, band_ref, image_ref, halo_ref)
    out_ref[...] = ((image - shift * x_ref[...].astype(jnp.float32)) / width).astype(jnp.bfloat16)


def step(side, table, image, band, halo, x):
    shape = jax.ShapeDtypeStruct(x.shape, jnp.bfloat16)
    return call(functools.partial(step_kernel, side), shape, [VMEM] * 5)(table, image, band, halo, x)


def finish_kernel(side, table_ref, image_ref, band_ref, halo_ref, s_ref, x_ref, out_ref):
    shift, width = table_ref[0:1, :], table_ref[1:2, :]
    live = table_ref[2:3, :] > 0.0
    image = halo_image(side, band_ref, image_ref, halo_ref)
    value = 2.0 * (image - shift * s_ref[...].astype(jnp.float32)) / width - x_ref[...].astype(jnp.float32)
    out_ref[...] = jnp.where(live, value, 0.0).astype(jnp.bfloat16)


def finish(side, table, image, band, halo, s, x):
    shape = jax.ShapeDtypeStruct(x.shape, jnp.bfloat16)
    return call(functools.partial(finish_kernel, side), shape, [VMEM] * 6)(table, image, band, halo, s, x)


def exponent(*values):
    top = functools.reduce(jnp.maximum, [jnp.abs(value) for value in values])
    top = jnp.max(top, axis=(0, 1), keepdims=True)
    return jnp.clip(jnp.ceil(jnp.log2(jnp.maximum(top, 1e-36))) - 14.0, -100.0, 60.0)


def with_code(share, same, e):
    row = lax.broadcasted_iota(jnp.int32, same.shape, 0)
    col = lax.broadcasted_iota(jnp.int32, same.shape, 1)
    slot = (lax.rem(row, share) == 1) & (col == row - 1)
    return jnp.where(slot, e, same * jnp.exp2(-e))


def early_kernel(fa_ref, fb_ref, ob_ref, out_ref):
    half = fa_ref.shape[1]
    fa, fb = fa_ref[...], fb_ref[...]
    out_ref[:, :half] = tmm(fa, fa) + tmm(fb, fb)
    out_ref[:, half:] = tmm(fa, ob_ref[...])


def early_terms(fa, fb, ob):
    half = fa.shape[1]
    shape = jax.ShapeDtypeStruct((half, 2 * half), jnp.float32)
    return call(early_kernel, shape, [VMEM] * 3)(fa, fb, ob)


def code_kernel(share, early_ref, fb_ref, oa_ref, out_ref):
    half = fb_ref.shape[1]
    same = early_ref[:, :half]
    cross = early_ref[:, half:] + tmm(fb_ref[...], oa_ref[...])
    e = exponent(same, cross)
    out_ref[:, :half] = with_code(share, same, e)
    out_ref[:, half:] = cross * jnp.exp2(-e)


def code_terms(early, fb, oa, share):
    shape = jax.ShapeDtypeStruct(early.shape, jnp.float32)
    return call(functools.partial(code_kernel, share), shape, [VMEM] * 3)(early, fb, oa)


def slots(shape):
    start = lax.axis_index("row") * shape[0]
    row = lax.broadcasted_iota(jnp.int32, (8, shape[1]), 0)
    col = lax.broadcasted_iota(jnp.int32, (8, shape[1]), 1)
    return (row == 1) & (col == start), (row == 0) & (col == start + 1)


def slot_factor(ref, slot, order_total):
    e = jnp.sum(jnp.where(slot, ref[:8, :slot.shape[1]], 0.0), axis=(0, 1), keepdims=True)
    return jnp.exp2(e) / order_total


def first_sum_kernel(order_total, coded_ref, piece_ref, out_ref):
    share, half = out_ref.shape[0], out_ref.shape[1] // 2
    slot, _ = slots((share, half))
    mine = coded_ref.at[pl.ds(pl.multiple_of(lax.axis_index("row") * share, 8), share), :]
    total = mine[...] * slot_factor(mine, slot, order_total)
    out_ref[...] = total + piece_ref[...] * slot_factor(piece_ref, slot, order_total)


def first_sum(coded, piece, order_total):
    shape = jax.ShapeDtypeStruct(piece.shape, jnp.float32)
    return call(functools.partial(first_sum_kernel, order_total), shape, [VMEM] * 2, LONG)(coded, piece)


def add_kernel(order_total, sum_ref, piece_ref, out_ref):
    share, columns = sum_ref.shape
    slot, _ = slots((share, columns // 2))
    out_ref[...] = sum_ref[...] + piece_ref[...] * slot_factor(piece_ref, slot, order_total)


def add_piece(total, piece, order_total):
    shape = jax.ShapeDtypeStruct(total.shape, jnp.float32)
    return call(functools.partial(add_kernel, order_total), shape, [VMEM] * 2, LONG)(total, piece)


def last_kernel(order_total, sum_ref, piece_ref, out_ref):
    share, half = out_ref.shape[0], out_ref.shape[1] // 2
    slot, twin = slots((share, half))
    factor = slot_factor(piece_ref, slot, order_total)
    sub = lax.axis_index("sub")
    at = pl.ds(pl.multiple_of(sub * half, half), half)
    other = pl.ds(pl.multiple_of((1 - sub) * half, half), half)
    out_ref[:, other] = sum_ref[:, half:] + piece_ref[:, half:] * factor
    same = sum_ref[:, :half] + piece_ref[:, :half] * factor
    out_ref[:, at] = same
    lost = jnp.sum(jnp.where(twin, same[:8], 0.0), axis=(0, 1), keepdims=True)
    out_ref[:8, at] = jnp.where(slot, lost, same[:8])


def last_sum(total, piece, order_total):
    shape = jax.ShapeDtypeStruct(total.shape, jnp.float32)
    return call(functools.partial(last_kernel, order_total), shape, [VMEM] * 2)(total, piece)


def image_kernel(band_ref, sa_ref, sb_ref, out_ref):
    wide = sa_ref.shape[0]
    out_ref[...] = mm(band_ref[:, :wide], sa_ref[...]) + mm(band_ref[:, wide:2 * wide], sb_ref[...])


def own_image(band, sa, sb):
    shape = jax.ShapeDtypeStruct((band.shape[0], sa.shape[1]), jnp.float32)
    return call(image_kernel, shape, [VMEM] * 3)(band, sa, sb)


def send_shares(coded, row_count, share):
    me = lax.axis_index("row")
    arrived = []
    for shift in range(1, row_count):
        part = lax.dynamic_slice_in_dim(coded, (me + shift) % row_count * share, share, axis=0)
        ring = [(i, (i + shift) % row_count) for i in range(row_count)]
        arrived.append(lax.ppermute(part, "row", ring))
    return arrived


def body(hop, pattern, vectors, counts, center, halfwidth):
    rows_dev = hop.shape[0]
    block = hop.shape[2]
    half = vectors.shape[2]
    row_count = lax.axis_size("row")
    total_blocks = rows_dev * row_count
    order_total = total_blocks * block
    wide = W * block
    share = half // row_count
    assert rows_dev == 2 * W
    up = [(i, (i + 1) % row_count) for i in range(row_count)]
    down = [(target, source) for source, target in up]
    to_a = [(2 * i, 2 * j) for i, j in down] + [(2 * i + 1, 2 * j + 1) for i, j in up]
    to_b = [(target, source) for source, target in to_a]
    swap = [(0, 1), (1, 0)]

    def exchange(a, b):
        return lax.ppermute(b, ("row", "sub"), to_a), lax.ppermute(a, ("row", "sub"), to_b)

    x = vectors[0]
    low = side_of_low()
    xa = lax.dynamic_slice_in_dim(x, low * wide, wide, axis=0)
    xb = lax.dynamic_slice_in_dim(x, (1 - low) * wide, wide, axis=0)
    halo_a, halo_b = exchange(xa, xb)
    band, image, table = band_parts(hop, pattern, counts, center, halfwidth, xa, xb, total_blocks)
    sa = step(0, table, image, band, halo_a, xa)
    sb = step(1, table, image, band, halo_b, xb)
    halo_a, halo_b = exchange(sa, sb)
    image = own_image(band, sa, sb)
    fa = finish(0, table, image, band, halo_a, sa, xa)
    oa = lax.ppermute(fa, "sub", swap)
    fb = finish(1, table, image, band, halo_b, sb, xb)
    ob = lax.ppermute(fb, "sub", swap)

    coded = code_terms(early_terms(fa, fb, ob), fb, oa, share)
    first, *middle, last = send_shares(coded.astype(jnp.float16), row_count, share)
    total = first_sum(coded, first.astype(jnp.float32), order_total)
    for piece in middle:
        total = add_piece(total, piece.astype(jnp.float32), order_total)
    total, last = lax.optimization_barrier((total, last))
    margin = last_sum(total, last.astype(jnp.float32), order_total)
    return margin.reshape(1, 1, share, 2 * half)


def solution(mesh):
    in_specs = (
        P(("groups", "row"), None, None, None),
        P(("groups", "row"), None),
        P("cuts", ("groups", "row"), "sub"),
        P(("groups", "cuts")),
        P(("groups", "cuts")),
        P(("groups", "cuts")),
    )
    out_specs = P(("groups", "cuts"), "sub", "row", None)
    return jax.shard_map(body, mesh=mesh, in_specs=in_specs, out_specs=out_specs, check_vma=False)
```

```python
import functools

import jax
import jax.numpy as jnp
from jax import lax
from jax.experimental import pallas as pl
from jax.experimental.pallas import tpu as pltpu
from jax.sharding import PartitionSpec as P

W = 3
TAIL = 8
LIMIT = 16 * 1024 * 1024
COST = pl.CostEstimate(flops=1000, bytes_accessed=1000, transcendentals=0)
LONG = pl.CostEstimate(flops=20_000_000_000, bytes_accessed=1000, transcendentals=0)
VMEM = pl.BlockSpec(memory_space=pltpu.VMEM)
SMEM = pl.BlockSpec(memory_space=pltpu.SMEM)


def call(kernel, out_shape, in_specs, cost=COST):
    return pl.pallas_call(
        kernel,
        out_shape=out_shape,
        in_specs=in_specs,
        out_specs=jax.tree.map(lambda _: VMEM, out_shape),
        compiler_params=pltpu.CompilerParams(vmem_limit_bytes=LIMIT),
        cost_estimate=cost,
    )


def mm(a, b):
    return jnp.dot(a, b, preferred_element_type=jnp.float32)


def tmm(a, b):
    return lax.dot_general(a, b, (((0,), (0,)), ((), ())), preferred_element_type=jnp.float32)


def band_kernel(total_blocks, counts_ref, center_ref, width_ref, pattern_ref, hop_ref, xa_ref, xb_ref, band_ref, image_ref, table_ref):
    rows_dev, stored, block, _ = hop_ref.shape
    wide = W * block
    first_block = lax.axis_index("row") * rows_dev
    band_ref[...] = jnp.zeros_like(band_ref)
    half = xa_ref.shape[1]
    line = lax.broadcasted_iota(jnp.int32, (8, half), 0)
    column = lax.broadcasted_iota(jnp.int32, (8, half), 1) + lax.axis_index("sub") * half
    live = jnp.where(column < counts_ref[0], 1.0, 0.0)
    table_ref[...] = jnp.where(line == 0, center_ref[0], jnp.where(line == 1, width_ref[0], live))
    for r in range(rows_dev):
        rows = slice(r * block, (r + 1) * block)
        for k in range(stored):
            col = lax.rem(pattern_ref[r, k] - first_block + (W + total_blocks), total_blocks) - W
            inside = jnp.logical_and(col >= 0, col < rows_dev)
            halo = 2 * W + jnp.where(col < 0, col + W, col - rows_dev)
            at = jnp.where(inside, col, halo)
            band_ref[rows, pl.ds(pl.multiple_of(at * block, block), block)] = hop_ref[r, k]
    image_ref[...] = mm(band_ref[:, :wide], xa_ref[...]) + mm(band_ref[:, wide:2 * wide], xb_ref[...])


def band_parts(hop, pattern, counts, center, halfwidth, xa, xb, total_blocks):
    rows_dev, _, block, _ = hop.shape
    wide, tall, half = W * block, rows_dev * block, xa.shape[1]
    return call(
        functools.partial(band_kernel, total_blocks),
        (
            jax.ShapeDtypeStruct((tall, 3 * wide), hop.dtype),
            jax.ShapeDtypeStruct((tall, half), jnp.float32),
            jax.ShapeDtypeStruct((8, half), jnp.float32),
        ),
        [SMEM] * 4 + [VMEM] * 3,
    )(counts, center, halfwidth, pattern, hop, xa, xb)


def halo_image(side, band_ref, image_ref, halo_ref):
    wide = halo_ref.shape[0]
    rows = slice(side * wide, (side + 1) * wide)
    return image_ref[rows, :] + mm(band_ref[rows, 2 * wide:], halo_ref[...])


def step_kernel(side, table_ref, image_ref, band_ref, halo_ref, x_ref, out_ref):
    shift, width = table_ref[0:1, :], table_ref[1:2, :]
    image = halo_image(side, band_ref, image_ref, halo_ref)
    out_ref[...] = ((image - shift * x_ref[...].astype(jnp.float32)) / width).astype(jnp.bfloat16)


def step(side, table, image, band, halo, x):
    shape = jax.ShapeDtypeStruct(x.shape, jnp.bfloat16)
    return call(functools.partial(step_kernel, side), shape, [VMEM] * 5)(table, image, band, halo, x)


def finish_kernel(side, table_ref, image_ref, band_ref, halo_ref, s_ref, x_ref, out_ref):
    shift, width = table_ref[0:1, :], table_ref[1:2, :]
    live = table_ref[2:3, :] > 0.0
    image = halo_image(side, band_ref, image_ref, halo_ref)
    value = 2.0 * (image - shift * s_ref[...].astype(jnp.float32)) / width - x_ref[...].astype(jnp.float32)
    out_ref[...] = jnp.where(live, value, 0.0).astype(jnp.bfloat16)


def finish(side, table, image, band, halo, s, x):
    shape = jax.ShapeDtypeStruct(x.shape, jnp.bfloat16)
    return call(functools.partial(finish_kernel, side), shape, [VMEM] * 6)(table, image, band, halo, s, x)


def exponent(*values):
    top = functools.reduce(jnp.maximum, [jnp.abs(value) for value in values])
    top = jnp.max(top, axis=(0, 1), keepdims=True)
    return jnp.clip(jnp.ceil(jnp.log2(jnp.maximum(top, 1e-36))) - 14.0, -100.0, 60.0)


def with_code(share, same, e):
    row = lax.broadcasted_iota(jnp.int32, same.shape, 0)
    col = lax.broadcasted_iota(jnp.int32, same.shape, 1)
    slot = (lax.rem(row, share) == 1) & (col == row - 1)
    return jnp.where(slot, e, same * jnp.exp2(-e))


def same_kernel(share, fa_ref, fb_ref, out_ref, coded_ref):
    fa, fb = fa_ref[...], fb_ref[...]
    same = tmm(fa, fa) + tmm(fb, fb)
    out_ref[...] = same
    coded_ref[...] = with_code(share, same, exponent(same))


def same_terms(fa, fb, share):
    half = fa.shape[1]
    shape = jax.ShapeDtypeStruct((half, half), jnp.float32)
    return call(functools.partial(same_kernel, share), (shape, shape), [VMEM] * 2)(fa, fb)


def code_kernel(share, same_ref, fa_ref, fb_ref, oa_ref, ob_ref, out_ref):
    half = fb_ref.shape[1]
    same = same_ref[...]
    cross = tmm(fa_ref[...], oa_ref[...]) + tmm(fb_ref[...], ob_ref[...])
    e = exponent(same, cross)
    same, cross = with_code(share, same, e), cross * jnp.exp2(-e)
    for r in range(half // share):
        rows, at = slice(r * share, (r + 1) * share), r * (share + TAIL)
        out_ref[at:at + share, :half] = same[rows]
        out_ref[at:at + share, half:] = cross[rows]
        out_ref[at + share:at + share + TAIL, :] = jnp.broadcast_to(e, (TAIL, 2 * half))


def code_terms(same, fa, fb, oa, ob, share):
    half = fb.shape[1]
    shape = jax.ShapeDtypeStruct((half // share * (share + TAIL), 2 * half), jnp.float32)
    return call(functools.partial(code_kernel, share), shape, [VMEM] * 5)(same, fa, fb, oa, ob)


def slots(shape):
    start = lax.axis_index("row") * shape[0]
    row = lax.broadcasted_iota(jnp.int32, (8, shape[1]), 0)
    col = lax.broadcasted_iota(jnp.int32, (8, shape[1]), 1)
    return (row == 1) & (col == start), (row == 0) & (col == start + 1)


def slot_factor(ref, slot, order_total):
    e = jnp.sum(jnp.where(slot, ref[:8, :slot.shape[1]], 0.0), axis=(0, 1), keepdims=True)
    return jnp.exp2(e) / order_total


def first_sum_kernel(order_total, coded_ref, same_ref, cross_ref, out_ref):
    share, half = same_ref.shape
    slot, _ = slots((share, half))
    mine = pl.ds(pl.multiple_of(lax.axis_index("row") * (share + TAIL), 8), share)
    factor = jnp.exp2(coded_ref[share:share + 1, :half]) / order_total
    out_ref[:, :half] = coded_ref[mine, :half] * factor + same_ref[...] * slot_factor(same_ref, slot, order_total)
    there = jnp.exp2(cross_ref[share:share + 1, :]) / order_total
    out_ref[:, half:] = coded_ref[mine, half:] * factor + cross_ref[:share, :] * there


def first_sum(coded, same, cross, order_total):
    share, half = same.shape
    shape = jax.ShapeDtypeStruct((share, 2 * half), jnp.float32)
    return call(functools.partial(first_sum_kernel, order_total), shape, [VMEM] * 3, LONG)(coded, same, cross)


def add_kernel(order_total, sum_ref, piece_ref, out_ref):
    share, columns = sum_ref.shape
    slot, _ = slots((share, columns // 2))
    out_ref[...] = sum_ref[...] + piece_ref[...] * slot_factor(piece_ref, slot, order_total)


def add_piece(total, piece, order_total):
    shape = jax.ShapeDtypeStruct(total.shape, jnp.float32)
    return call(functools.partial(add_kernel, order_total), shape, [VMEM] * 2, LONG)(total, piece)


def last_kernel(order_total, sum_ref, piece_ref, out_ref):
    share, half = out_ref.shape[0], out_ref.shape[1] // 2
    slot, twin = slots((share, half))
    factor = slot_factor(piece_ref, slot, order_total)
    sub = lax.axis_index("sub")
    at = pl.ds(pl.multiple_of(sub * half, half), half)
    other = pl.ds(pl.multiple_of((1 - sub) * half, half), half)
    out_ref[:, other] = sum_ref[:, half:] + piece_ref[:, half:] * factor
    same = sum_ref[:, :half] + piece_ref[:, :half] * factor
    out_ref[:, at] = same
    lost = jnp.sum(jnp.where(twin, same[:8], 0.0), axis=(0, 1), keepdims=True)
    out_ref[:8, at] = jnp.where(slot, lost, same[:8])


def last_sum(total, piece, order_total):
    shape = jax.ShapeDtypeStruct(total.shape, jnp.float32)
    return call(functools.partial(last_kernel, order_total), shape, [VMEM] * 2)(total, piece)


def image_kernel(band_ref, sa_ref, sb_ref, out_ref):
    wide = sa_ref.shape[0]
    out_ref[...] = mm(band_ref[:, :wide], sa_ref[...]) + mm(band_ref[:, wide:2 * wide], sb_ref[...])


def own_image(band, sa, sb):
    shape = jax.ShapeDtypeStruct((band.shape[0], sa.shape[1]), jnp.float32)
    return call(image_kernel, shape, [VMEM] * 3)(band, sa, sb)


def send(terms, shift, row_count, rows, pitch):
    at = (lax.axis_index("row") + shift) % row_count * pitch
    ring = [(i, (i + shift) % row_count) for i in range(row_count)]
    return lax.ppermute(lax.dynamic_slice_in_dim(terms, at, rows, axis=0), "row", ring)


def body(hop, pattern, vectors, counts, center, halfwidth):
    rows_dev = hop.shape[0]
    block = hop.shape[2]
    half = vectors.shape[2]
    row_count = lax.axis_size("row")
    total_blocks = rows_dev * row_count
    order_total = total_blocks * block
    wide = W * block
    share = half // row_count
    assert rows_dev == 2 * W
    forward = [(i, (i + 1) % row_count) for i in range(row_count)]
    backward = [(target, source) for source, target in forward]
    swap = [(0, 1), (1, 0)]

    def halos_of(low, high):
        return lax.ppermute(high, "row", forward), lax.ppermute(low, "row", backward)

    x = vectors[0]
    xa, xb = x[:wide], x[wide:]
    halo_a, halo_b = halos_of(xa, xb)
    band, image, table = band_parts(hop, pattern, counts, center, halfwidth, xa, xb, total_blocks)
    sb = step(1, table, image, band, halo_b, xb)
    sa = step(0, table, image, band, lax.optimization_barrier((halo_a, sb))[0], xa)
    halo_a, halo_b = halos_of(sa, sb)
    image = own_image(band, sa, sb)
    fa = finish(0, table, image, band, halo_a, sa, xa)
    oa = lax.ppermute(fa, "sub", swap)
    fb = finish(1, table, image, band, lax.optimization_barrier((halo_b, fa))[0], sb, xb)
    ob = lax.ppermute(fb, "sub", swap)
    same, coded = same_terms(fa, fb, share)
    coded, same = (
        code_terms(same, fa, fb, oa, ob, share),
        send(coded.astype(jnp.float16), 1, row_count, share, share),
    )
    terms, pitch = coded.astype(jnp.float16), share + TAIL
    cross = send(terms[:, half:], 1, row_count, pitch, pitch)
    *middle, last = [send(terms, shift, row_count, share, pitch) for shift in range(2, row_count)]
    same, cross = lax.optimization_barrier((same, cross))
    total = first_sum(coded, same.astype(jnp.float32), cross.astype(jnp.float32), order_total)
    for piece in middle:
        total = add_piece(total, piece.astype(jnp.float32), order_total)
    total, last = lax.optimization_barrier((total, last))
    margin = last_sum(total, last.astype(jnp.float32), order_total)
    return margin.reshape(1, 1, share, 2 * half)


def solution(mesh):
    in_specs = (
        P(("groups", "row"), None, None, None),
        P(("groups", "row"), None),
        P("cuts", ("groups", "row"), "sub"),
        P(("groups", "cuts")),
        P(("groups", "cuts")),
        P(("groups", "cuts")),
    )
    out_specs = P(("groups", "cuts"), "sub", "row", None)
    return jax.shard_map(body, mesh=mesh, in_specs=in_specs, out_specs=out_specs, check_vma=False)
```

```python
import functools

import jax
import jax.numpy as jnp
from jax import lax
from jax.experimental import pallas as pl
from jax.experimental.pallas import tpu as pltpu
from jax.sharding import PartitionSpec as P

W = 3
LIMIT = 16 * 1024 * 1024
COST = pl.CostEstimate(flops=1000, bytes_accessed=1000, transcendentals=0)
LONG = pl.CostEstimate(flops=20_000_000_000, bytes_accessed=1000, transcendentals=0)
VMEM = pl.BlockSpec(memory_space=pltpu.VMEM)
SMEM = pl.BlockSpec(memory_space=pltpu.SMEM)


def call(kernel, out_shape, in_specs, cost=COST):
    return pl.pallas_call(
        kernel,
        out_shape=out_shape,
        in_specs=in_specs,
        out_specs=jax.tree.map(lambda _: VMEM, out_shape),
        compiler_params=pltpu.CompilerParams(vmem_limit_bytes=LIMIT),
        cost_estimate=cost,
    )


def mm(a, b):
    return jnp.dot(a, b, preferred_element_type=jnp.float32)


def tmm(a, b):
    return lax.dot_general(a, b, (((0,), (0,)), ((), ())), preferred_element_type=jnp.float32)


def after(value, other):
    return lax.optimization_barrier((value, other))[0]


def ids_kernel(out_ref):
    out_ref[...] = lax.broadcasted_iota(jnp.int32, out_ref.shape, 1) + lax.axis_index("sub") * out_ref.shape[1]


def ids_of(half):
    return call(ids_kernel, jax.ShapeDtypeStruct((8, half), jnp.int32), [], LONG)()


def table_kernel(center_ref, width_ref, ids_ref, table_ref):
    line = lax.broadcasted_iota(jnp.int32, table_ref.shape, 0)
    table_ref[...] = jnp.where(line == 0, center_ref[0], width_ref[0])


def table_of(center, halfwidth, ids):
    shape = jax.ShapeDtypeStruct(ids.shape, jnp.float32)
    return call(table_kernel, shape, [SMEM] * 2 + [VMEM])(after(center, ids), after(halfwidth, ids), ids)


def live_kernel(counts_ref, ids_ref, live_ref):
    live_ref[...] = jnp.where(ids_ref[...] < counts_ref[0], 1.0, 0.0)


def live_of(counts, ids):
    return call(live_kernel, jax.ShapeDtypeStruct(ids.shape, jnp.float32), [SMEM, VMEM])(counts, ids)


def band_kernel(total_blocks, table_ref, pattern_ref, hop_ref, xa_ref, xb_ref, band_ref, image_ref):
    rows_dev, stored, block, _ = hop_ref.shape
    wide = W * block
    first_block = lax.axis_index("row") * rows_dev
    band_ref[...] = jnp.zeros_like(band_ref)
    for r in range(rows_dev):
        rows = slice(r * block, (r + 1) * block)
        for k in range(stored):
            col = lax.rem(pattern_ref[r, k] - first_block + (W + total_blocks), total_blocks) - W
            inside = jnp.logical_and(col >= 0, col < rows_dev)
            halo = 2 * W + jnp.where(col < 0, col + W, col - rows_dev)
            at = jnp.where(inside, col, halo)
            band_ref[rows, pl.ds(pl.multiple_of(at * block, block), block)] = hop_ref[r, k]
    image_ref[...] = mm(band_ref[:, :wide], xa_ref[...]) + mm(band_ref[:, wide:2 * wide], xb_ref[...])


def band_parts(table, hop, pattern, xa, xb, total_blocks):
    rows_dev, _, block, _ = hop.shape
    wide, tall, half = W * block, rows_dev * block, xa.shape[1]
    return call(
        functools.partial(band_kernel, total_blocks),
        (
            jax.ShapeDtypeStruct((tall, 3 * wide), hop.dtype),
            jax.ShapeDtypeStruct((tall, half), jnp.float32),
        ),
        [VMEM, SMEM] + [VMEM] * 3,
    )(table, pattern, hop, xa, xb)


def halo_image(side, band_ref, image_ref, halo_ref):
    wide = halo_ref.shape[0]
    rows = slice(side * wide, (side + 1) * wide)
    return image_ref[rows, :] + mm(band_ref[rows, 2 * wide:], halo_ref[...])


def step_kernel(side, table_ref, image_ref, band_ref, halo_ref, x_ref, out_ref):
    shift, width = table_ref[0:1, :], table_ref[1:2, :]
    image = halo_image(side, band_ref, image_ref, halo_ref)
    out_ref[...] = ((image - shift * x_ref[...].astype(jnp.float32)) / width).astype(jnp.bfloat16)


def step(side, table, image, band, halo, x):
    shape = jax.ShapeDtypeStruct(x.shape, jnp.bfloat16)
    return call(functools.partial(step_kernel, side), shape, [VMEM] * 5)(table, image, band, halo, x)


def finish_kernel(side, table_ref, live_ref, image_ref, band_ref, halo_ref, s_ref, x_ref, out_ref):
    shift, width = table_ref[0:1, :], table_ref[1:2, :]
    live = live_ref[0:1, :] > 0.0
    image = halo_image(side, band_ref, image_ref, halo_ref)
    value = 2.0 * (image - shift * s_ref[...].astype(jnp.float32)) / width - x_ref[...].astype(jnp.float32)
    out_ref[...] = jnp.where(live, value, 0.0).astype(jnp.bfloat16)


def finish(side, table, live, image, band, halo, s, x):
    shape = jax.ShapeDtypeStruct(x.shape, jnp.bfloat16)
    return call(functools.partial(finish_kernel, side), shape, [VMEM] * 7)(table, live, image, band, halo, s, x)


def exponent(*values):
    top = functools.reduce(jnp.maximum, [jnp.abs(value) for value in values])
    top = jnp.max(top, axis=(0, 1), keepdims=True)
    return jnp.clip(jnp.ceil(jnp.log2(jnp.maximum(top, 1e-36))) - 14.0, -100.0, 60.0)


def with_code(share, same, e):
    row = lax.broadcasted_iota(jnp.int32, same.shape, 0)
    col = lax.broadcasted_iota(jnp.int32, same.shape, 1)
    slot = (lax.rem(row, share) == 1) & (col == row - 1)
    return jnp.where(slot, e, same * jnp.exp2(-e))


def early_kernel(fa_ref, fb_ref, oa_ref, out_ref):
    half = fa_ref.shape[1]
    fa, fb = fa_ref[...], fb_ref[...]
    out_ref[:, :half] = tmm(fa, fa) + tmm(fb, fb)
    out_ref[:, half:] = tmm(fa, oa_ref[...])


def early_terms(fa, fb, oa):
    half = fa.shape[1]
    shape = jax.ShapeDtypeStruct((half, 2 * half), jnp.float32)
    return call(early_kernel, shape, [VMEM] * 3)(fa, fb, oa)


def code_kernel(share, early_ref, fb_ref, ob_ref, out_ref):
    half = fb_ref.shape[1]
    same = early_ref[:, :half]
    cross = early_ref[:, half:] + tmm(fb_ref[...], ob_ref[...])
    e = exponent(same, cross)
    out_ref[:, :half] = with_code(share, same, e)
    out_ref[:, half:] = cross * jnp.exp2(-e)


def code_terms(early, fb, ob, share):
    shape = jax.ShapeDtypeStruct(early.shape, jnp.float32)
    return call(functools.partial(code_kernel, share), shape, [VMEM] * 3)(early, fb, ob)


def slots(shape):
    start = lax.axis_index("row") * shape[0]
    row = lax.broadcasted_iota(jnp.int32, (8, shape[1]), 0)
    col = lax.broadcasted_iota(jnp.int32, (8, shape[1]), 1)
    return (row == 1) & (col == start), (row == 0) & (col == start + 1)


def slot_factor(ref, slot, order_total):
    e = jnp.sum(jnp.where(slot, ref[:8, :slot.shape[1]], 0.0), axis=(0, 1), keepdims=True)
    return jnp.exp2(e) / order_total


def first_sum_kernel(order_total, coded_ref, piece_ref, out_ref):
    share, half = out_ref.shape[0], out_ref.shape[1] // 2
    slot, _ = slots((share, half))
    mine = coded_ref.at[pl.ds(pl.multiple_of(lax.axis_index("row") * share, 8), share), :]
    total = mine[...] * slot_factor(mine, slot, order_total)
    out_ref[...] = total + piece_ref[...] * slot_factor(piece_ref, slot, order_total)


def first_sum(coded, piece, order_total):
    shape = jax.ShapeDtypeStruct(piece.shape, jnp.float32)
    return call(functools.partial(first_sum_kernel, order_total), shape, [VMEM] * 2, LONG)(coded, piece)


def add_kernel(order_total, sum_ref, piece_ref, out_ref):
    share, columns = sum_ref.shape
    slot, _ = slots((share, columns // 2))
    out_ref[...] = sum_ref[...] + piece_ref[...] * slot_factor(piece_ref, slot, order_total)


def add_piece(total, piece, order_total):
    shape = jax.ShapeDtypeStruct(total.shape, jnp.float32)
    return call(functools.partial(add_kernel, order_total), shape, [VMEM] * 2, LONG)(total, piece)


def last_kernel(order_total, sum_ref, piece_ref, out_ref):
    share, half = out_ref.shape[0], out_ref.shape[1] // 2
    slot, twin = slots((share, half))
    factor = slot_factor(piece_ref, slot, order_total)
    sub = lax.axis_index("sub")
    at = pl.ds(pl.multiple_of(sub * half, half), half)
    other = pl.ds(pl.multiple_of((1 - sub) * half, half), half)
    out_ref[:, other] = sum_ref[:, half:] + piece_ref[:, half:] * factor
    same = sum_ref[:, :half] + piece_ref[:, :half] * factor
    out_ref[:, at] = same
    lost = jnp.sum(jnp.where(twin, same[:8], 0.0), axis=(0, 1), keepdims=True)
    out_ref[:8, at] = jnp.where(slot, lost, same[:8])


def last_sum(total, piece, order_total):
    shape = jax.ShapeDtypeStruct(total.shape, jnp.float32)
    return call(functools.partial(last_kernel, order_total), shape, [VMEM] * 2)(total, piece)


def image_kernel(band_ref, sa_ref, sb_ref, out_ref):
    wide = sa_ref.shape[0]
    out_ref[...] = mm(band_ref[:, :wide], sa_ref[...]) + mm(band_ref[:, wide:2 * wide], sb_ref[...])


def own_image(band, sa, sb):
    shape = jax.ShapeDtypeStruct((band.shape[0], sa.shape[1]), jnp.float32)
    return call(image_kernel, shape, [VMEM] * 3)(band, sa, sb)


def send_shares(coded, row_count, share):
    me = lax.axis_index("row")
    arrived = []
    for shift in range(1, row_count):
        part = lax.dynamic_slice_in_dim(coded, (me + shift) % row_count * share, share, axis=0)
        ring = [(i, (i + shift) % row_count) for i in range(row_count)]
        arrived.append(lax.ppermute(part, "row", ring))
    return arrived


def body(hop, pattern, vectors, counts, center, halfwidth):
    rows_dev = hop.shape[0]
    block = hop.shape[2]
    half = vectors.shape[2]
    row_count = lax.axis_size("row")
    total_blocks = rows_dev * row_count
    order_total = total_blocks * block
    wide = W * block
    share = half // row_count
    assert rows_dev == 2 * W
    forward = [(i, (i + 1) % row_count) for i in range(row_count)]
    backward = [(target, source) for source, target in forward]
    swap = [(0, 1), (1, 0)]

    def halos_of(low, high):
        return lax.ppermute(high, "row", forward), lax.ppermute(low, "row", backward)

    x = vectors[0]
    xa, xb = x[:wide], x[wide:]
    halo_a, halo_b = halos_of(xa, xb)
    ids = ids_of(half)
    table = table_of(center, halfwidth, ids)
    band, image = band_parts(table, hop, pattern, xa, xb, total_blocks)
    sb = step(1, table, image, band, halo_b, xb)
    sa = step(0, table, image, band, lax.optimization_barrier((halo_a, sb))[0], xa)
    halo_a, halo_b = halos_of(sa, sb)
    image = own_image(band, sa, sb)
    live = live_of(after(counts, sa), ids)
    fa = finish(0, table, live, image, band, halo_a, sa, xa)
    oa = lax.ppermute(fa, "sub", swap)
    fb = finish(1, table, live, image, band, lax.optimization_barrier((halo_b, fa))[0], sb, xb)
    ob = lax.ppermute(fb, "sub", swap)
    coded = code_terms(early_terms(fa, fb, oa), fb, ob, share)
    first, *middle, last = send_shares(coded.astype(jnp.float16), row_count, share)
    total = first_sum(coded, first.astype(jnp.float32), order_total)
    for piece in middle:
        total = add_piece(total, piece.astype(jnp.float32), order_total)
    total, last = lax.optimization_barrier((total, last))
    margin = last_sum(total, last.astype(jnp.float32), order_total)
    return margin.reshape(1, 1, share, 2 * half)


def solution(mesh):
    in_specs = (
        P(("groups", "row"), None, None, None),
        P(("groups", "row"), None),
        P("cuts", ("groups", "row"), "sub"),
        P(("groups", "cuts")),
        P(("groups", "cuts")),
        P(("groups", "cuts")),
    )
    out_specs = P(("groups", "cuts"), "sub", "row", None)
    return jax.shard_map(body, mesh=mesh, in_specs=in_specs, out_specs=out_specs, check_vma=False)
```

```python
import functools

import jax
import jax.numpy as jnp
from jax import lax
from jax.experimental import pallas as pl
from jax.experimental.pallas import tpu as pltpu
from jax.sharding import PartitionSpec as P

W = 3
LIMIT = 16 * 1024 * 1024
COST = pl.CostEstimate(flops=1000, bytes_accessed=1000, transcendentals=0)
LONG = pl.CostEstimate(flops=20_000_000_000, bytes_accessed=1000, transcendentals=0)
VMEM = pl.BlockSpec(memory_space=pltpu.VMEM)
SMEM = pl.BlockSpec(memory_space=pltpu.SMEM)


def call(kernel, out_shape, in_specs, cost=COST):
    return pl.pallas_call(
        kernel,
        out_shape=out_shape,
        in_specs=in_specs,
        out_specs=jax.tree.map(lambda _: VMEM, out_shape),
        compiler_params=pltpu.CompilerParams(vmem_limit_bytes=LIMIT),
        cost_estimate=cost,
    )


def mm(a, b):
    return jnp.dot(a, b, preferred_element_type=jnp.float32)


def tmm(a, b):
    return lax.dot_general(a, b, (((0,), (0,)), ((), ())), preferred_element_type=jnp.float32)


def after(value, other):
    return lax.optimization_barrier((value, other))[0]


def ids_kernel(out_ref):
    out_ref[...] = lax.broadcasted_iota(jnp.int32, out_ref.shape, 1) + lax.axis_index("sub") * out_ref.shape[1]


def ids_of(half):
    return call(ids_kernel, jax.ShapeDtypeStruct((8, half), jnp.int32), [], LONG)()


def table_kernel(center_ref, width_ref, ids_ref, table_ref):
    line = lax.broadcasted_iota(jnp.int32, table_ref.shape, 0)
    table_ref[...] = jnp.where(line == 0, center_ref[0], width_ref[0])


def table_of(center, halfwidth, ids):
    shape = jax.ShapeDtypeStruct(ids.shape, jnp.float32)
    return call(table_kernel, shape, [SMEM] * 2 + [VMEM])(after(center, ids), after(halfwidth, ids), ids)


def live_kernel(counts_ref, ids_ref, live_ref):
    live_ref[...] = jnp.where(ids_ref[...] < counts_ref[0], 1.0, 0.0)


def live_of(counts, ids):
    return call(live_kernel, jax.ShapeDtypeStruct(ids.shape, jnp.float32), [SMEM, VMEM])(counts, ids)


def band_kernel(total_blocks, table_ref, pattern_ref, hop_ref, xa_ref, xb_ref, band_ref, image_ref):
    rows_dev, stored, block, _ = hop_ref.shape
    wide = W * block
    first_block = lax.axis_index("row") * rows_dev
    band_ref[...] = jnp.zeros_like(band_ref)
    for r in range(rows_dev):
        rows = slice(r * block, (r + 1) * block)
        for k in range(stored):
            col = lax.rem(pattern_ref[r, k] - first_block + (W + total_blocks), total_blocks) - W
            inside = jnp.logical_and(col >= 0, col < rows_dev)
            halo = 2 * W + jnp.where(col < 0, col + W, col - rows_dev)
            at = jnp.where(inside, col, halo)
            band_ref[rows, pl.ds(pl.multiple_of(at * block, block), block)] = hop_ref[r, k]
    image_ref[...] = mm(band_ref[:, :wide], xa_ref[...]) + mm(band_ref[:, wide:2 * wide], xb_ref[...])


def band_parts(table, hop, pattern, xa, xb, total_blocks):
    rows_dev, _, block, _ = hop.shape
    wide, tall, half = W * block, rows_dev * block, xa.shape[1]
    return call(
        functools.partial(band_kernel, total_blocks),
        (
            jax.ShapeDtypeStruct((tall, 3 * wide), hop.dtype),
            jax.ShapeDtypeStruct((tall, half), jnp.float32),
        ),
        [VMEM, SMEM] + [VMEM] * 3,
    )(table, pattern, hop, xa, xb)


def halo_image(side, band_ref, image_ref, halo_ref):
    wide = halo_ref.shape[0]
    rows = slice(side * wide, (side + 1) * wide)
    return image_ref[rows, :] + mm(band_ref[rows, 2 * wide:], halo_ref[...])


def step_kernel(side, table_ref, image_ref, band_ref, halo_ref, x_ref, out_ref):
    shift, width = table_ref[0:1, :], table_ref[1:2, :]
    image = halo_image(side, band_ref, image_ref, halo_ref)
    out_ref[...] = ((image - shift * x_ref[...].astype(jnp.float32)) / width).astype(jnp.bfloat16)


def step(side, table, image, band, halo, x):
    shape = jax.ShapeDtypeStruct(x.shape, jnp.bfloat16)
    return call(functools.partial(step_kernel, side), shape, [VMEM] * 5)(table, image, band, halo, x)


def finish_kernel(side, table_ref, live_ref, image_ref, band_ref, halo_ref, s_ref, x_ref, out_ref):
    shift, width = table_ref[0:1, :], table_ref[1:2, :]
    live = live_ref[0:1, :] > 0.0
    image = halo_image(side, band_ref, image_ref, halo_ref)
    value = 2.0 * (image - shift * s_ref[...].astype(jnp.float32)) / width - x_ref[...].astype(jnp.float32)
    out_ref[...] = jnp.where(live, value, 0.0).astype(jnp.bfloat16)


def finish(side, table, live, image, band, halo, s, x):
    shape = jax.ShapeDtypeStruct(x.shape, jnp.bfloat16)
    return call(functools.partial(finish_kernel, side), shape, [VMEM] * 7)(table, live, image, band, halo, s, x)


def exponent(value):
    top = jnp.max(jnp.abs(value), axis=(0, 1), keepdims=True)
    return jnp.clip(jnp.ceil(jnp.log2(jnp.maximum(top, 1e-36))) - 14.0, -100.0, 60.0)


def with_code(share, line, same, e):
    row = lax.broadcasted_iota(jnp.int32, same.shape, 0)
    col = lax.broadcasted_iota(jnp.int32, same.shape, 1)
    return jnp.where((lax.rem(row, share) == line) & (col == row - line), e, same)


def early_kernel(share, fa_ref, fb_ref, oa_ref, out_ref):
    half = fa_ref.shape[1]
    fa, fb = fa_ref[...], fb_ref[...]
    same = tmm(fa, fa) + tmm(fb, fb)
    e = exponent(same)
    out_ref[:, :half] = with_code(share, 1, same * jnp.exp2(-e), e)
    out_ref[:, half:] = tmm(fa, oa_ref[...])


def early_terms(fa, fb, oa, share):
    half = fa.shape[1]
    shape = jax.ShapeDtypeStruct((half, 2 * half), jnp.float32)
    return call(functools.partial(early_kernel, share), shape, [VMEM] * 3)(fa, fb, oa)


def code_kernel(share, early_ref, fb_ref, ob_ref, out_ref):
    half = fb_ref.shape[1]
    cross = early_ref[:, half:] + tmm(fb_ref[...], ob_ref[...])
    e = exponent(cross)
    out_ref[:, :half] = with_code(share, 2, early_ref[:, :half], e)
    out_ref[:, half:] = cross * jnp.exp2(-e)


def code_terms(early, fb, ob, share):
    shape = jax.ShapeDtypeStruct(early.shape, jnp.float32)
    return call(functools.partial(code_kernel, share), shape, [VMEM] * 3)(early, fb, ob)


def pick(head, shift, share):
    col = lax.broadcasted_iota(jnp.int32, head.shape, 1)
    here = col == lax.axis_index("row") * share + shift
    return jnp.sum(jnp.where(here, head, 0.0), axis=1, keepdims=True)


def factors(head, share, order_total):
    scale = jnp.exp2(pick(head, 0, share)) / order_total
    return scale[1:2], scale[2:3]


def first_sum_kernel(order_total, coded_ref, piece_ref, out_ref):
    share, half = out_ref.shape[0], out_ref.shape[1] // 2
    mine = coded_ref.at[pl.ds(pl.multiple_of(lax.axis_index("row") * share, 8), share), :]
    own_same, own_cross = factors(mine[:8, :half], share, order_total)
    same, cross = factors(piece_ref[:8, :half], share, order_total)
    out_ref[:, :half] = mine[:, :half] * own_same + piece_ref[:, :half] * same
    out_ref[:, half:] = mine[:, half:] * own_cross + piece_ref[:, half:] * cross


def first_sum(coded, piece, order_total):
    shape = jax.ShapeDtypeStruct(piece.shape, jnp.float32)
    return call(functools.partial(first_sum_kernel, order_total), shape, [VMEM] * 2, LONG)(coded, piece)


def add_kernel(order_total, sum_ref, piece_ref, out_ref):
    share, half = out_ref.shape[0], out_ref.shape[1] // 2
    same, cross = factors(piece_ref[:8, :half], share, order_total)
    out_ref[:, :half] = sum_ref[:, :half] + piece_ref[:, :half] * same
    out_ref[:, half:] = sum_ref[:, half:] + piece_ref[:, half:] * cross


def add_piece(total, piece, order_total):
    shape = jax.ShapeDtypeStruct(total.shape, jnp.float32)
    return call(functools.partial(add_kernel, order_total), shape, [VMEM] * 2, LONG)(total, piece)


def last_kernel(order_total, sum_ref, piece_ref, out_ref):
    share, half = out_ref.shape[0], out_ref.shape[1] // 2
    same, cross = factors(piece_ref[:8, :half], share, order_total)
    sub = lax.axis_index("sub")
    at = pl.ds(pl.multiple_of(sub * half, half), half)
    other = pl.ds(pl.multiple_of((1 - sub) * half, half), half)
    out_ref[:, other] = sum_ref[:, half:] + piece_ref[:, half:] * cross
    out_ref[:, at] = sum_ref[:, :half] + piece_ref[:, :half] * same
    head = sum_ref[:8, :half] + piece_ref[:8, :half] * same
    row = lax.broadcasted_iota(jnp.int32, head.shape, 0)
    col = lax.broadcasted_iota(jnp.int32, head.shape, 1)
    start = col == lax.axis_index("row") * share
    for line in (1, 2):
        head = jnp.where((row == line) & start, pick(head[:1], line, share), head)
    out_ref[:8, at] = head


def last_sum(total, piece, order_total):
    shape = jax.ShapeDtypeStruct(total.shape, jnp.float32)
    return call(functools.partial(last_kernel, order_total), shape, [VMEM] * 2)(total, piece)


def image_kernel(band_ref, sa_ref, sb_ref, out_ref):
    wide = sa_ref.shape[0]
    out_ref[...] = mm(band_ref[:, :wide], sa_ref[...]) + mm(band_ref[:, wide:2 * wide], sb_ref[...])


def own_image(band, sa, sb):
    shape = jax.ShapeDtypeStruct((band.shape[0], sa.shape[1]), jnp.float32)
    return call(image_kernel, shape, [VMEM] * 3)(band, sa, sb)


def send_shares(coded, row_count, share):
    me = lax.axis_index("row")
    arrived = []
    for shift in range(1, row_count):
        part = lax.dynamic_slice_in_dim(coded, (me + shift) % row_count * share, share, axis=0)
        ring = [(i, (i + shift) % row_count) for i in range(row_count)]
        arrived.append(lax.ppermute(part, "row", ring))
    return arrived


def body(hop, pattern, vectors, counts, center, halfwidth):
    rows_dev = hop.shape[0]
    block = hop.shape[2]
    half = vectors.shape[2]
    row_count = lax.axis_size("row")
    total_blocks = rows_dev * row_count
    order_total = total_blocks * block
    wide = W * block
    share = half // row_count
    assert rows_dev == 2 * W
    forward = [(i, (i + 1) % row_count) for i in range(row_count)]
    backward = [(target, source) for source, target in forward]
    swap = [(0, 1), (1, 0)]

    def halos_of(low, high):
        return lax.ppermute(high, "row", forward), lax.ppermute(low, "row", backward)

    x = vectors[0]
    xa, xb = x[:wide], x[wide:]
    halo_a, halo_b = halos_of(xa, xb)
    ids = ids_of(half)
    table = table_of(center, halfwidth, ids)
    band, image = band_parts(table, hop, pattern, xa, xb, total_blocks)
    sb = step(1, table, image, band, halo_b, xb)
    sa = step(0, table, image, band, lax.optimization_barrier((halo_a, sb))[0], xa)
    halo_a, halo_b = halos_of(sa, sb)
    image = own_image(band, sa, sb)
    live = live_of(after(counts, sa), ids)
    fa = finish(0, table, live, image, band, halo_a, sa, xa)
    oa = lax.ppermute(fa, "sub", swap)
    fb = finish(1, table, live, image, band, lax.optimization_barrier((halo_b, fa))[0], sb, xb)
    ob = lax.ppermute(fb, "sub", swap)
    coded = code_terms(early_terms(fa, fb, oa, share), fb, ob, share)
    first, *middle, last = send_shares(coded.astype(jnp.float16), row_count, share)
    total = first_sum(coded, first.astype(jnp.float32), order_total)
    for piece in middle:
        total = add_piece(total, piece.astype(jnp.float32), order_total)
    total, last = lax.optimization_barrier((total, last))
    margin = last_sum(total, last.astype(jnp.float32), order_total)
    return margin.reshape(1, 1, share, 2 * half)


def solution(mesh):
    in_specs = (
        P(("groups", "row"), None, None, None),
        P(("groups", "row"), None),
        P("cuts", ("groups", "row"), "sub"),
        P(("groups", "cuts")),
        P(("groups", "cuts")),
        P(("groups", "cuts")),
    )
    out_specs = P(("groups", "cuts"), "sub", "row", None)
    return jax.shard_map(body, mesh=mesh, in_specs=in_specs, out_specs=out_specs, check_vma=False)
```

```python
import functools

import jax
import jax.numpy as jnp
from jax import lax
from jax.experimental import pallas as pl
from jax.experimental.pallas import tpu as pltpu
from jax.sharding import PartitionSpec as P

W = 3
LIMIT = 16 * 1024 * 1024
COST = pl.CostEstimate(flops=1000, bytes_accessed=1000, transcendentals=0)
LONG = pl.CostEstimate(flops=20_000_000_000, bytes_accessed=1000, transcendentals=0)
VMEM = pl.BlockSpec(memory_space=pltpu.VMEM)
SMEM = pl.BlockSpec(memory_space=pltpu.SMEM)


def call(kernel, out_shape, in_specs, cost=COST):
    return pl.pallas_call(
        kernel,
        out_shape=out_shape,
        in_specs=in_specs,
        out_specs=jax.tree.map(lambda _: VMEM, out_shape),
        compiler_params=pltpu.CompilerParams(vmem_limit_bytes=LIMIT),
        cost_estimate=cost,
    )


def mm(a, b):
    return jnp.dot(a, b, preferred_element_type=jnp.float32)


def tmm(a, b):
    return lax.dot_general(a, b, (((0,), (0,)), ((), ())), preferred_element_type=jnp.float32)


def after(value, other):
    return lax.optimization_barrier((value, other))[0]


def ids_kernel(out_ref):
    out_ref[...] = lax.broadcasted_iota(jnp.int32, out_ref.shape, 1) + lax.axis_index("sub") * out_ref.shape[1]


def ids_of(half):
    return call(ids_kernel, jax.ShapeDtypeStruct((8, half), jnp.int32), [], LONG)()


def table_kernel(center_ref, width_ref, ids_ref, table_ref):
    line = lax.broadcasted_iota(jnp.int32, table_ref.shape, 0)
    table_ref[...] = jnp.where(line == 0, center_ref[0], width_ref[0])


def table_of(center, halfwidth, ids):
    shape = jax.ShapeDtypeStruct(ids.shape, jnp.float32)
    return call(table_kernel, shape, [SMEM] * 2 + [VMEM])(after(center, ids), after(halfwidth, ids), ids)


def live_kernel(counts_ref, ids_ref, live_ref):
    live_ref[...] = jnp.where(ids_ref[...] < counts_ref[0], 1.0, 0.0)


def live_of(counts, ids):
    return call(live_kernel, jax.ShapeDtypeStruct(ids.shape, jnp.float32), [SMEM, VMEM])(counts, ids)


def band_kernel(total_blocks, table_ref, pattern_ref, hop_ref, xa_ref, xb_ref, band_ref, image_ref):
    rows_dev, stored, block, _ = hop_ref.shape
    wide = W * block
    first_block = lax.axis_index("row") * rows_dev
    band_ref[...] = jnp.zeros_like(band_ref)
    for r in range(rows_dev):
        rows = slice(r * block, (r + 1) * block)
        for k in range(stored):
            col = lax.rem(pattern_ref[r, k] - first_block + (W + total_blocks), total_blocks) - W
            inside = jnp.logical_and(col >= 0, col < rows_dev)
            halo = 2 * W + jnp.where(col < 0, col + W, col - rows_dev)
            at = jnp.where(inside, col, halo)
            band_ref[rows, pl.ds(pl.multiple_of(at * block, block), block)] = hop_ref[r, k]
    image_ref[...] = mm(band_ref[:, :wide], xa_ref[...]) + mm(band_ref[:, wide:2 * wide], xb_ref[...])


def band_parts(table, hop, pattern, xa, xb, total_blocks):
    rows_dev, _, block, _ = hop.shape
    wide, tall, half = W * block, rows_dev * block, xa.shape[1]
    return call(
        functools.partial(band_kernel, total_blocks),
        (
            jax.ShapeDtypeStruct((tall, 3 * wide), hop.dtype),
            jax.ShapeDtypeStruct((tall, half), jnp.float32),
        ),
        [VMEM, SMEM] + [VMEM] * 3,
    )(table, pattern, hop, xa, xb)


def halo_image(side, band_ref, image_ref, halo_ref):
    wide = halo_ref.shape[0]
    rows = slice(side * wide, (side + 1) * wide)
    return image_ref[rows, :] + mm(band_ref[rows, 2 * wide:], halo_ref[...])


def step_kernel(side, table_ref, image_ref, band_ref, halo_ref, x_ref, out_ref):
    shift, width = table_ref[0:1, :], table_ref[1:2, :]
    image = halo_image(side, band_ref, image_ref, halo_ref)
    out_ref[...] = ((image - shift * x_ref[...].astype(jnp.float32)) / width).astype(jnp.bfloat16)


def step(side, table, image, band, halo, x):
    shape = jax.ShapeDtypeStruct(x.shape, jnp.bfloat16)
    return call(functools.partial(step_kernel, side), shape, [VMEM] * 5)(table, image, band, halo, x)


def finish_kernel(side, table_ref, live_ref, image_ref, band_ref, halo_ref, s_ref, x_ref, out_ref):
    shift, width = table_ref[0:1, :], table_ref[1:2, :]
    live = live_ref[0:1, :] > 0.0
    image = halo_image(side, band_ref, image_ref, halo_ref)
    value = 2.0 * (image - shift * s_ref[...].astype(jnp.float32)) / width - x_ref[...].astype(jnp.float32)
    out_ref[...] = jnp.where(live, value, 0.0).astype(jnp.bfloat16)


def finish(side, table, live, image, band, halo, s, x):
    shape = jax.ShapeDtypeStruct(x.shape, jnp.bfloat16)
    return call(functools.partial(finish_kernel, side), shape, [VMEM] * 7)(table, live, image, band, halo, s, x)


def exponent(value):
    top = jnp.max(jnp.abs(value), axis=(0, 1), keepdims=True)
    return jnp.clip(jnp.ceil(jnp.log2(jnp.maximum(top, 1e-36))) - 14.0, -100.0, 60.0)


def with_code(share, line, same, e):
    row = lax.broadcasted_iota(jnp.int32, same.shape, 0)
    col = lax.broadcasted_iota(jnp.int32, same.shape, 1)
    return jnp.where((lax.rem(row, share) == line) & (col == row - line), e, same)


def early_kernel(share, fa_ref, fb_ref, oa_ref, out_ref, turned_ref):
    half = fa_ref.shape[1]
    fa, fb = fa_ref[...], fb_ref[...]
    same = tmm(fa, fa) + tmm(fb, fb)
    e = exponent(same)
    out_ref[:, :half] = with_code(share, 1, same * jnp.exp2(-e), e)
    out_ref[:, half:] = tmm(fa, oa_ref[...])
    turned_ref[...] = fb.T


def early_terms(fa, fb, oa, share):
    half = fa.shape[1]
    shapes = (jax.ShapeDtypeStruct((half, 2 * half), jnp.float32), jax.ShapeDtypeStruct(fb.shape[::-1], fb.dtype))
    return call(functools.partial(early_kernel, share), shapes, [VMEM] * 3)(fa, fb, oa)


def code_kernel(share, early_ref, turned_ref, ob_ref, out_ref):
    half = turned_ref.shape[0]
    cross = early_ref[:, half:] + mm(turned_ref[...], ob_ref[...])
    e = exponent(cross)
    out_ref[:, :half] = with_code(share, 2, early_ref[:, :half], e)
    out_ref[:, half:] = cross * jnp.exp2(-e)


def code_terms(early, turned, ob, share):
    shape = jax.ShapeDtypeStruct(early.shape, jnp.float32)
    return call(functools.partial(code_kernel, share), shape, [VMEM] * 3)(early, turned, ob)


def pick(head, shift, share):
    col = lax.broadcasted_iota(jnp.int32, head.shape, 1)
    here = col == lax.axis_index("row") * share + shift
    return jnp.sum(jnp.where(here, head, 0.0), axis=1, keepdims=True)


def factors(head, share, order_total):
    scale = jnp.exp2(pick(head, 0, share)) / order_total
    return scale[1:2], scale[2:3]


def first_sum_kernel(order_total, coded_ref, piece_ref, out_ref):
    share, half = out_ref.shape[0], out_ref.shape[1] // 2
    mine = coded_ref.at[pl.ds(pl.multiple_of(lax.axis_index("row") * share, 8), share), :]
    own_same, own_cross = factors(mine[:8, :half], share, order_total)
    same, cross = factors(piece_ref[:8, :half], share, order_total)
    out_ref[:, :half] = mine[:, :half] * own_same + piece_ref[:, :half] * same
    out_ref[:, half:] = mine[:, half:] * own_cross + piece_ref[:, half:] * cross


def first_sum(coded, piece, order_total):
    shape = jax.ShapeDtypeStruct(piece.shape, jnp.float32)
    return call(functools.partial(first_sum_kernel, order_total), shape, [VMEM] * 2, LONG)(coded, piece)


def add_kernel(order_total, sum_ref, piece_ref, out_ref):
    share, half = out_ref.shape[0], out_ref.shape[1] // 2
    same, cross = factors(piece_ref[:8, :half], share, order_total)
    out_ref[:, :half] = sum_ref[:, :half] + piece_ref[:, :half] * same
    out_ref[:, half:] = sum_ref[:, half:] + piece_ref[:, half:] * cross


def add_piece(total, piece, order_total):
    shape = jax.ShapeDtypeStruct(total.shape, jnp.float32)
    return call(functools.partial(add_kernel, order_total), shape, [VMEM] * 2, LONG)(total, piece)


def last_kernel(order_total, sum_ref, piece_ref, out_ref):
    share, half = out_ref.shape[0], out_ref.shape[1] // 2
    same, cross = factors(piece_ref[:8, :half], share, order_total)
    sub = lax.axis_index("sub")
    at = pl.ds(pl.multiple_of(sub * half, half), half)
    other = pl.ds(pl.multiple_of((1 - sub) * half, half), half)
    out_ref[:, other] = sum_ref[:, half:] + piece_ref[:, half:] * cross
    out_ref[:, at] = sum_ref[:, :half] + piece_ref[:, :half] * same
    head = sum_ref[:8, :half] + piece_ref[:8, :half] * same
    row = lax.broadcasted_iota(jnp.int32, head.shape, 0)
    col = lax.broadcasted_iota(jnp.int32, head.shape, 1)
    start = col == lax.axis_index("row") * share
    for line in (1, 2):
        head = jnp.where((row == line) & start, pick(head[:1], line, share), head)
    out_ref[:8, at] = head


def last_sum(total, piece, order_total):
    shape = jax.ShapeDtypeStruct(total.shape, jnp.float32)
    return call(functools.partial(last_kernel, order_total), shape, [VMEM] * 2)(total, piece)


def image_kernel(band_ref, sa_ref, sb_ref, out_ref):
    wide = sa_ref.shape[0]
    out_ref[...] = mm(band_ref[:, :wide], sa_ref[...]) + mm(band_ref[:, wide:2 * wide], sb_ref[...])


def own_image(band, sa, sb):
    shape = jax.ShapeDtypeStruct((band.shape[0], sa.shape[1]), jnp.float32)
    return call(image_kernel, shape, [VMEM] * 3)(band, sa, sb)


def send_shares(coded, row_count, share):
    me = lax.axis_index("row")
    arrived = []
    for shift in range(1, row_count):
        part = lax.dynamic_slice_in_dim(coded, (me + shift) % row_count * share, share, axis=0)
        ring = [(i, (i + shift) % row_count) for i in range(row_count)]
        arrived.append(lax.ppermute(part, "row", ring))
    return arrived


def body(hop, pattern, vectors, counts, center, halfwidth):
    rows_dev = hop.shape[0]
    block = hop.shape[2]
    half = vectors.shape[2]
    row_count = lax.axis_size("row")
    total_blocks = rows_dev * row_count
    order_total = total_blocks * block
    wide = W * block
    share = half // row_count
    assert rows_dev == 2 * W
    forward = [(i, (i + 1) % row_count) for i in range(row_count)]
    backward = [(target, source) for source, target in forward]
    swap = [(0, 1), (1, 0)]

    def halos_of(low, high):
        return lax.ppermute(high, "row", forward), lax.ppermute(low, "row", backward)

    x = vectors[0]
    xa, xb = x[:wide], x[wide:]
    halo_a, halo_b = halos_of(xa, xb)
    ids = ids_of(half)
    table = table_of(center, halfwidth, ids)
    band, image = band_parts(table, hop, pattern, xa, xb, total_blocks)
    sb = step(1, table, image, band, halo_b, xb)
    sa = step(0, table, image, band, lax.optimization_barrier((halo_a, sb))[0], xa)
    halo_a, halo_b = halos_of(sa, sb)
    image = own_image(band, sa, sb)
    live = live_of(after(counts, sa), ids)
    fa = finish(0, table, live, image, band, halo_a, sa, xa)
    oa = lax.ppermute(fa, "sub", swap)
    fb = finish(1, table, live, image, band, lax.optimization_barrier((halo_b, fa))[0], sb, xb)
    ob = lax.ppermute(fb, "sub", swap)
    early, turned = early_terms(fa, fb, oa, share)
    coded = code_terms(early, turned, ob, share)
    first, *middle, last = send_shares(coded.astype(jnp.float16), row_count, share)
    total = first_sum(coded, first.astype(jnp.float32), order_total)
    for piece in middle:
        total = add_piece(total, piece.astype(jnp.float32), order_total)
    total, last = lax.optimization_barrier((total, last))
    margin = last_sum(total, last.astype(jnp.float32), order_total)
    return margin.reshape(1, 1, share, 2 * half)


def solution(mesh):
    in_specs = (
        P(("groups", "row"), None, None, None),
        P(("groups", "row"), None),
        P("cuts", ("groups", "row"), "sub"),
        P(("groups", "cuts")),
        P(("groups", "cuts")),
        P(("groups", "cuts")),
    )
    out_specs = P(("groups", "cuts"), "sub", "row", None)
    return jax.shard_map(body, mesh=mesh, in_specs=in_specs, out_specs=out_specs, check_vma=False)
```

```python
import functools

import jax
import jax.numpy as jnp
from jax import lax
from jax.experimental import pallas as pl
from jax.experimental.pallas import tpu as pltpu
from jax.sharding import PartitionSpec as P

W = 3
LIMIT = 16 * 1024 * 1024
COST = pl.CostEstimate(flops=1000, bytes_accessed=1000, transcendentals=0)
LONG = pl.CostEstimate(flops=20_000_000_000, bytes_accessed=1000, transcendentals=0)
VMEM = pl.BlockSpec(memory_space=pltpu.VMEM)
SMEM = pl.BlockSpec(memory_space=pltpu.SMEM)


def call(kernel, out_shape, in_specs, cost=COST):
    return pl.pallas_call(
        kernel,
        out_shape=out_shape,
        in_specs=in_specs,
        out_specs=jax.tree.map(lambda _: VMEM, out_shape),
        compiler_params=pltpu.CompilerParams(vmem_limit_bytes=LIMIT),
        cost_estimate=cost,
    )


def mm(a, b):
    return jnp.dot(a, b, preferred_element_type=jnp.float32)


def tmm(a, b):
    return lax.dot_general(a, b, (((0,), (0,)), ((), ())), preferred_element_type=jnp.float32)


def after(value, other):
    return lax.optimization_barrier((value, other))[0]


def ids_kernel(out_ref):
    out_ref[...] = lax.broadcasted_iota(jnp.int32, out_ref.shape, 1) + lax.axis_index("sub") * out_ref.shape[1]


def ids_of(half):
    return call(ids_kernel, jax.ShapeDtypeStruct((8, half), jnp.int32), [], LONG)()


def table_kernel(center_ref, width_ref, ids_ref, table_ref):
    line = lax.broadcasted_iota(jnp.int32, table_ref.shape, 0)
    table_ref[...] = jnp.where(line == 0, center_ref[0], width_ref[0])


def table_of(center, halfwidth, ids):
    shape = jax.ShapeDtypeStruct(ids.shape, jnp.float32)
    return call(table_kernel, shape, [SMEM] * 2 + [VMEM])(after(center, ids), after(halfwidth, ids), ids)


def live_kernel(counts_ref, ids_ref, live_ref):
    live_ref[...] = jnp.where(ids_ref[...] < counts_ref[0], 1.0, 0.0)


def live_of(counts, ids):
    return call(live_kernel, jax.ShapeDtypeStruct(ids.shape, jnp.float32), [SMEM, VMEM])(counts, ids)


def band_kernel(total_blocks, table_ref, pattern_ref, hop_ref, xa_ref, xb_ref, band_ref, image_ref):
    rows_dev, stored, block, _ = hop_ref.shape
    wide = W * block
    first_block = lax.axis_index("row") * rows_dev
    band_ref[...] = jnp.zeros_like(band_ref)
    for r in range(rows_dev):
        rows = slice(r * block, (r + 1) * block)
        for k in range(stored):
            col = lax.rem(pattern_ref[r, k] - first_block + (W + total_blocks), total_blocks) - W
            inside = jnp.logical_and(col >= 0, col < rows_dev)
            halo = 2 * W + jnp.where(col < 0, col + W, col - rows_dev)
            at = jnp.where(inside, col, halo)
            band_ref[rows, pl.ds(pl.multiple_of(at * block, block), block)] = hop_ref[r, k]
    image_ref[...] = mm(band_ref[:, :wide], xa_ref[...]) + mm(band_ref[:, wide:2 * wide], xb_ref[...])


def band_parts(table, hop, pattern, xa, xb, total_blocks):
    rows_dev, _, block, _ = hop.shape
    wide, tall, half = W * block, rows_dev * block, xa.shape[1]
    return call(
        functools.partial(band_kernel, total_blocks),
        (
            jax.ShapeDtypeStruct((tall, 3 * wide), hop.dtype),
            jax.ShapeDtypeStruct((tall, half), jnp.float32),
        ),
        [VMEM, SMEM] + [VMEM] * 3,
    )(table, pattern, hop, xa, xb)


def halo_image(side, band_ref, image_ref, halo_ref):
    wide = halo_ref.shape[0]
    rows = slice(side * wide, (side + 1) * wide)
    return image_ref[rows, :] + mm(band_ref[rows, 2 * wide:], halo_ref[...])


def step_kernel(side, table_ref, image_ref, band_ref, halo_ref, x_ref, out_ref):
    shift, width = table_ref[0:1, :], table_ref[1:2, :]
    image = halo_image(side, band_ref, image_ref, halo_ref)
    out_ref[...] = ((image - shift * x_ref[...].astype(jnp.float32)) / width).astype(jnp.bfloat16)


def step(side, table, image, band, halo, x):
    shape = jax.ShapeDtypeStruct(x.shape, jnp.bfloat16)
    return call(functools.partial(step_kernel, side), shape, [VMEM] * 5)(table, image, band, halo, x)


def finish_kernel(side, table_ref, live_ref, image_ref, band_ref, halo_ref, s_ref, x_ref, out_ref):
    shift, width = table_ref[0:1, :], table_ref[1:2, :]
    live = live_ref[0:1, :] > 0.0
    image = halo_image(side, band_ref, image_ref, halo_ref)
    value = 2.0 * (image - shift * s_ref[...].astype(jnp.float32)) / width - x_ref[...].astype(jnp.float32)
    out_ref[...] = jnp.where(live, value, 0.0).astype(jnp.bfloat16)


def finish(side, table, live, image, band, halo, s, x):
    shape = jax.ShapeDtypeStruct(x.shape, jnp.bfloat16)
    return call(functools.partial(finish_kernel, side), shape, [VMEM] * 7)(table, live, image, band, halo, s, x)


def exponent(value):
    top = jnp.max(jnp.abs(value), axis=(0, 1), keepdims=True)
    return jnp.clip(jnp.ceil(jnp.log2(jnp.maximum(top, 1e-36))) - 14.0, -100.0, 60.0)


def with_code(share, line, same, e):
    row = lax.broadcasted_iota(jnp.int32, same.shape, 0)
    col = lax.broadcasted_iota(jnp.int32, same.shape, 1)
    return jnp.where((lax.rem(row, share) == line) & (col == row - line), e, same)


def early_kernel(share, fa_ref, fb_ref, oa_ref, out_ref, turned_ref):
    half = fa_ref.shape[1]
    fa, fb = fa_ref[...], fb_ref[...]
    same = tmm(fa, fa) + tmm(fb, fb)
    e = exponent(same)
    out_ref[:, :half] = with_code(share, 1, same * jnp.exp2(-e), e)
    out_ref[:, half:] = tmm(fa, oa_ref[...])
    turned_ref[...] = fb.T


def early_terms(fa, fb, oa, share):
    half = fa.shape[1]
    shapes = (jax.ShapeDtypeStruct((half, 2 * half), jnp.float32), jax.ShapeDtypeStruct(fb.shape[::-1], fb.dtype))
    return call(functools.partial(early_kernel, share), shapes, [VMEM] * 3)(fa, fb, oa)


def code_kernel(share, early_ref, turned_ref, ob_ref, out_ref):
    half = turned_ref.shape[0]
    cross = early_ref[:, half:] + mm(turned_ref[...], ob_ref[...])
    e = exponent(cross)
    out_ref[:, :half] = with_code(share, 2, early_ref[:, :half], e)
    out_ref[:, half:] = cross * jnp.exp2(-e)


def code_terms(early, turned, ob, share):
    shape = jax.ShapeDtypeStruct(early.shape, jnp.float32)
    return call(functools.partial(code_kernel, share), shape, [VMEM] * 3)(early, turned, ob)


def pick(head, shift, share):
    col = lax.broadcasted_iota(jnp.int32, head.shape, 1)
    here = col == lax.axis_index("row") * share + shift
    return jnp.sum(jnp.where(here, head, 0.0), axis=1, keepdims=True)


def factors(head, share, order_total):
    scale = jnp.exp2(pick(head, 0, share)) / order_total
    return scale[1:2], scale[2:3]


def first_sum_kernel(order_total, coded_ref, piece_ref, out_ref):
    share, half = out_ref.shape[0], out_ref.shape[1] // 2
    mine = coded_ref.at[pl.ds(pl.multiple_of(lax.axis_index("row") * share, 8), share), :]
    own_same, own_cross = factors(mine[:8, :half], share, order_total)
    same, cross = factors(piece_ref[:8, :half], share, order_total)
    out_ref[:, :half] = mine[:, :half] * own_same + piece_ref[:, :half] * same
    out_ref[:, half:] = mine[:, half:] * own_cross + piece_ref[:, half:] * cross


def first_sum(coded, piece, order_total):
    shape = jax.ShapeDtypeStruct(piece.shape, jnp.float32)
    return call(functools.partial(first_sum_kernel, order_total), shape, [VMEM] * 2, LONG)(coded, piece)


def add_kernel(order_total, sum_ref, piece_ref, out_ref):
    share, half = out_ref.shape[0], out_ref.shape[1] // 2
    same, cross = factors(piece_ref[:8, :half], share, order_total)
    out_ref[:, :half] = sum_ref[:, :half] + piece_ref[:, :half] * same
    out_ref[:, half:] = sum_ref[:, half:] + piece_ref[:, half:] * cross


def add_piece(total, piece, order_total):
    shape = jax.ShapeDtypeStruct(total.shape, jnp.float32)
    return call(functools.partial(add_kernel, order_total), shape, [VMEM] * 2, LONG)(total, piece)


def last_kernel(order_total, sum_ref, piece_ref, out_any, held_ref, sems):
    _, share, half = held_ref.shape
    same, cross = factors(piece_ref[:8, :half], share, order_total)
    sub = lax.axis_index("sub")

    def leave(slot, place):
        columns = pl.ds(pl.multiple_of(place * half, half), half)
        return pltpu.make_async_copy(held_ref.at[slot], out_any.at[:, columns], sems.at[slot])

    held_ref[0] = sum_ref[:, half:] + piece_ref[:, half:] * cross
    cross_copy = leave(0, 1 - sub)
    cross_copy.start()
    held_ref[1] = sum_ref[:, :half] + piece_ref[:, :half] * same
    head = sum_ref[:8, :half] + piece_ref[:8, :half] * same
    row = lax.broadcasted_iota(jnp.int32, head.shape, 0)
    col = lax.broadcasted_iota(jnp.int32, head.shape, 1)
    start = col == lax.axis_index("row") * share
    for line in (1, 2):
        head = jnp.where((row == line) & start, pick(head[:1], line, share), head)
    held_ref[1, :8, :] = head
    same_copy = leave(1, sub)
    same_copy.start()
    cross_copy.wait()
    same_copy.wait()


def last_sum(total, piece, order_total):
    share, columns = total.shape
    return pl.pallas_call(
        functools.partial(last_kernel, order_total),
        out_shape=jax.ShapeDtypeStruct(total.shape, jnp.float32),
        in_specs=[VMEM] * 2,
        out_specs=pl.BlockSpec(memory_space=pl.ANY),
        scratch_shapes=[
            pltpu.VMEM((2, share, columns // 2), jnp.float32),
            pltpu.SemaphoreType.DMA((2,)),
        ],
        compiler_params=pltpu.CompilerParams(vmem_limit_bytes=LIMIT),
        cost_estimate=COST,
    )(total, piece)


def image_kernel(band_ref, sa_ref, sb_ref, out_ref):
    wide = sa_ref.shape[0]
    out_ref[...] = mm(band_ref[:, :wide], sa_ref[...]) + mm(band_ref[:, wide:2 * wide], sb_ref[...])


def own_image(band, sa, sb):
    shape = jax.ShapeDtypeStruct((band.shape[0], sa.shape[1]), jnp.float32)
    return call(image_kernel, shape, [VMEM] * 3)(band, sa, sb)


def send_shares(coded, row_count, share):
    me = lax.axis_index("row")
    arrived = []
    for shift in range(1, row_count):
        part = lax.dynamic_slice_in_dim(coded, (me + shift) % row_count * share, share, axis=0)
        ring = [(i, (i + shift) % row_count) for i in range(row_count)]
        arrived.append(lax.ppermute(part, "row", ring))
    return arrived


def body(hop, pattern, vectors, counts, center, halfwidth):
    rows_dev = hop.shape[0]
    block = hop.shape[2]
    half = vectors.shape[2]
    row_count = lax.axis_size("row")
    total_blocks = rows_dev * row_count
    order_total = total_blocks * block
    wide = W * block
    share = half // row_count
    assert rows_dev == 2 * W
    forward = [(i, (i + 1) % row_count) for i in range(row_count)]
    backward = [(target, source) for source, target in forward]
    swap = [(0, 1), (1, 0)]

    def halos_of(low, high):
        return lax.ppermute(high, "row", forward), lax.ppermute(low, "row", backward)

    x = vectors[0]
    xa, xb = x[:wide], x[wide:]
    halo_a, halo_b = halos_of(xa, xb)
    ids = ids_of(half)
    table = table_of(center, halfwidth, ids)
    band, image = band_parts(table, hop, pattern, xa, xb, total_blocks)
    sb = step(1, table, image, band, halo_b, xb)
    sa = step(0, table, image, band, lax.optimization_barrier((halo_a, sb))[0], xa)
    halo_a, halo_b = halos_of(sa, sb)
    image = own_image(band, sa, sb)
    live = live_of(after(counts, sa), ids)
    fa = finish(0, table, live, image, band, halo_a, sa, xa)
    oa = lax.ppermute(fa, "sub", swap)
    fb = finish(1, table, live, image, band, lax.optimization_barrier((halo_b, fa))[0], sb, xb)
    ob = lax.ppermute(fb, "sub", swap)
    early, turned = early_terms(fa, fb, oa, share)
    coded = code_terms(early, turned, ob, share)
    first, *middle, last = send_shares(coded.astype(jnp.float16), row_count, share)
    total = first_sum(coded, first.astype(jnp.float32), order_total)
    for piece in middle:
        total = add_piece(total, piece.astype(jnp.float32), order_total)
    total, last = lax.optimization_barrier((total, last))
    margin = last_sum(total, last.astype(jnp.float32), order_total)
    return margin.reshape(1, 1, share, 2 * half)


def solution(mesh):
    in_specs = (
        P(("groups", "row"), None, None, None),
        P(("groups", "row"), None),
        P("cuts", ("groups", "row"), "sub"),
        P(("groups", "cuts")),
        P(("groups", "cuts")),
        P(("groups", "cuts")),
    )
    out_specs = P(("groups", "cuts"), "sub", "row", None)
    return jax.shard_map(body, mesh=mesh, in_specs=in_specs, out_specs=out_specs, check_vma=False)
```

```python
import functools

import jax
import jax.numpy as jnp
from jax import lax
from jax.experimental import pallas as pl
from jax.experimental.pallas import tpu as pltpu
from jax.sharding import PartitionSpec as P

W = 3
LIMIT = 16 * 1024 * 1024
COST = pl.CostEstimate(flops=1000, bytes_accessed=1000, transcendentals=0)
LONG = pl.CostEstimate(flops=20_000_000_000, bytes_accessed=1000, transcendentals=0)
VMEM = pl.BlockSpec(memory_space=pltpu.VMEM)
SMEM = pl.BlockSpec(memory_space=pltpu.SMEM)


def call(kernel, out_shape, in_specs, cost=COST):
    return pl.pallas_call(
        kernel,
        out_shape=out_shape,
        in_specs=in_specs,
        out_specs=jax.tree.map(lambda _: VMEM, out_shape),
        compiler_params=pltpu.CompilerParams(vmem_limit_bytes=LIMIT),
        cost_estimate=cost,
    )


def mm(a, b):
    return jnp.dot(a, b, preferred_element_type=jnp.float32)


def tmm(a, b):
    return lax.dot_general(a, b, (((0,), (0,)), ((), ())), preferred_element_type=jnp.float32)


def after(value, other):
    return lax.optimization_barrier((value, other))[0]


def ids_kernel(out_ref):
    out_ref[...] = lax.broadcasted_iota(jnp.int32, out_ref.shape, 1) + lax.axis_index("sub") * out_ref.shape[1]


def ids_of(half):
    return call(ids_kernel, jax.ShapeDtypeStruct((8, half), jnp.int32), [], LONG)()


def table_kernel(center_ref, width_ref, ids_ref, table_ref):
    line = lax.broadcasted_iota(jnp.int32, table_ref.shape, 0)
    table_ref[...] = jnp.where(line == 0, center_ref[0], width_ref[0])


def table_of(center, halfwidth, ids):
    shape = jax.ShapeDtypeStruct(ids.shape, jnp.float32)
    return call(table_kernel, shape, [SMEM] * 2 + [VMEM])(after(center, ids), after(halfwidth, ids), ids)


def live_kernel(counts_ref, ids_ref, live_ref):
    live_ref[...] = jnp.where(ids_ref[...] < counts_ref[0], 1.0, 0.0)


def live_of(counts, ids):
    return call(live_kernel, jax.ShapeDtypeStruct(ids.shape, jnp.float32), [SMEM, VMEM])(counts, ids)


def band_kernel(total_blocks, table_ref, pattern_ref, hop_ref, xa_ref, xb_ref, band_ref, image_ref):
    rows_dev, stored, block, _ = hop_ref.shape
    wide = W * block
    first_block = lax.axis_index("row") * rows_dev
    band_ref[...] = jnp.zeros_like(band_ref)
    for r in range(rows_dev):
        rows = slice(r * block, (r + 1) * block)
        for k in range(stored):
            col = lax.rem(pattern_ref[r, k] - first_block + (W + total_blocks), total_blocks) - W
            inside = jnp.logical_and(col >= 0, col < rows_dev)
            halo = 2 * W + jnp.where(col < 0, col + W, col - rows_dev)
            at = jnp.where(inside, col, halo)
            band_ref[rows, pl.ds(pl.multiple_of(at * block, block), block)] = hop_ref[r, k]
    image_ref[...] = mm(band_ref[:, :wide], xa_ref[...]) + mm(band_ref[:, wide:2 * wide], xb_ref[...])


def band_parts(table, hop, pattern, xa, xb, total_blocks):
    rows_dev, _, block, _ = hop.shape
    wide, tall, half = W * block, rows_dev * block, xa.shape[1]
    return call(
        functools.partial(band_kernel, total_blocks),
        (
            jax.ShapeDtypeStruct((tall, 3 * wide), hop.dtype),
            jax.ShapeDtypeStruct((tall, half), jnp.float32),
        ),
        [VMEM, SMEM] + [VMEM] * 3,
    )(table, pattern, hop, xa, xb)


def halo_image(side, band_ref, image_ref, halo_ref):
    wide = halo_ref.shape[0]
    rows = slice(side * wide, (side + 1) * wide)
    return image_ref[rows, :] + mm(band_ref[rows, 2 * wide:], halo_ref[...])


def step_kernel(side, table_ref, image_ref, band_ref, halo_ref, x_ref, out_ref):
    shift, width = table_ref[0:1, :], table_ref[1:2, :]
    image = halo_image(side, band_ref, image_ref, halo_ref)
    out_ref[...] = ((image - shift * x_ref[...].astype(jnp.float32)) / width).astype(jnp.bfloat16)


def step(side, table, image, band, halo, x):
    shape = jax.ShapeDtypeStruct(x.shape, jnp.bfloat16)
    return call(functools.partial(step_kernel, side), shape, [VMEM] * 5)(table, image, band, halo, x)


def finish_kernel(side, table_ref, live_ref, image_ref, band_ref, halo_ref, s_ref, x_ref, out_ref):
    shift, width = table_ref[0:1, :], table_ref[1:2, :]
    live = live_ref[0:1, :] > 0.0
    image = halo_image(side, band_ref, image_ref, halo_ref)
    value = 2.0 * (image - shift * s_ref[...].astype(jnp.float32)) / width - x_ref[...].astype(jnp.float32)
    out_ref[...] = jnp.where(live, value, 0.0).astype(jnp.bfloat16)


def finish(side, table, live, image, band, halo, s, x):
    shape = jax.ShapeDtypeStruct(x.shape, jnp.bfloat16)
    return call(functools.partial(finish_kernel, side), shape, [VMEM] * 7)(table, live, image, band, halo, s, x)


def exponent(value):
    top = jnp.max(jnp.abs(value), axis=(0, 1), keepdims=True)
    return jnp.clip(jnp.ceil(jnp.log2(jnp.maximum(top, 1e-36))) - 14.0, -100.0, 60.0)


def with_code(share, line, same, e):
    row = lax.broadcasted_iota(jnp.int32, same.shape, 0)
    col = lax.broadcasted_iota(jnp.int32, same.shape, 1)
    return jnp.where((lax.rem(row, share) == line) & (col == row - line), e, same)


def early_kernel(share, fa_ref, fb_ref, oa_ref, out_ref, turned_ref):
    half = fa_ref.shape[1]
    fa, fb = fa_ref[...], fb_ref[...]
    same = tmm(fa, fa) + tmm(fb, fb)
    e = exponent(same)
    out_ref[:, :half] = with_code(share, 1, same * jnp.exp2(-e), e)
    out_ref[:, half:] = tmm(fa, oa_ref[...])
    turned_ref[...] = fb.T


def early_terms(fa, fb, oa, share):
    half = fa.shape[1]
    shapes = (jax.ShapeDtypeStruct((half, 2 * half), jnp.float32), jax.ShapeDtypeStruct(fb.shape[::-1], fb.dtype))
    return call(functools.partial(early_kernel, share), shapes, [VMEM] * 3)(fa, fb, oa)


def code_kernel(share, early_ref, turned_ref, ob_ref, out_ref):
    half = turned_ref.shape[0]
    cross = early_ref[:, half:] + mm(turned_ref[...], ob_ref[...])
    e = exponent(cross)
    out_ref[:, :half] = with_code(share, 2, early_ref[:, :half], e)
    out_ref[:, half:] = cross * jnp.exp2(-e)


def code_terms(early, turned, ob, share):
    shape = jax.ShapeDtypeStruct(early.shape, jnp.float32)
    return call(functools.partial(code_kernel, share), shape, [VMEM] * 3)(early, turned, ob)


def pick(head, shift, share):
    col = lax.broadcasted_iota(jnp.int32, head.shape, 1)
    here = col == lax.axis_index("row") * share + shift
    return jnp.sum(jnp.where(here, head, 0.0), axis=1, keepdims=True)


def factors(head, share, order_total):
    scale = jnp.exp2(pick(head, 0, share)) / order_total
    return scale[1:2], scale[2:3]


def first_sum_kernel(order_total, coded_ref, piece_ref, out_ref):
    share, half = out_ref.shape[0], out_ref.shape[1] // 2
    mine = coded_ref.at[pl.ds(pl.multiple_of(lax.axis_index("row") * share, 8), share), :]
    own_same, own_cross = factors(mine[:8, :half], share, order_total)
    same, cross = factors(piece_ref[:8, :half], share, order_total)
    out_ref[:, :half] = mine[:, :half] * own_same + piece_ref[:, :half] * same
    out_ref[:, half:] = mine[:, half:] * own_cross + piece_ref[:, half:] * cross


def first_sum(coded, piece, order_total):
    shape = jax.ShapeDtypeStruct(piece.shape, jnp.float32)
    return call(functools.partial(first_sum_kernel, order_total), shape, [VMEM] * 2, LONG)(coded, piece)


def add_kernel(order_total, sum_ref, piece_ref, out_ref):
    share, half = out_ref.shape[0], out_ref.shape[1] // 2
    same, cross = factors(piece_ref[:8, :half], share, order_total)
    out_ref[:, :half] = sum_ref[:, :half] + piece_ref[:, :half] * same
    out_ref[:, half:] = sum_ref[:, half:] + piece_ref[:, half:] * cross


def add_piece(total, piece, order_total):
    shape = jax.ShapeDtypeStruct(total.shape, jnp.float32)
    return call(functools.partial(add_kernel, order_total), shape, [VMEM] * 2, LONG)(total, piece)


def last_kernel(order_total, sum_ref, piece_ref, same_ref, cross_ref):
    share, half = same_ref.shape
    same, cross = factors(piece_ref[:8, :half], share, order_total)
    cross_ref[...] = sum_ref[:, half:] + piece_ref[:, half:] * cross
    same_ref[...] = sum_ref[:, :half] + piece_ref[:, :half] * same
    head = sum_ref[:8, :half] + piece_ref[:8, :half] * same
    row = lax.broadcasted_iota(jnp.int32, head.shape, 0)
    col = lax.broadcasted_iota(jnp.int32, head.shape, 1)
    start = col == lax.axis_index("row") * share
    for line in (1, 2):
        head = jnp.where((row == line) & start, pick(head[:1], line, share), head)
    same_ref[:8, :] = head


def last_sum(total, piece, order_total):
    share, columns = total.shape
    shape = jax.ShapeDtypeStruct((share, columns // 2), jnp.float32)
    same, cross = call(functools.partial(last_kernel, order_total), (shape, shape), [VMEM] * 2)(total, piece)
    first = lax.axis_index("sub") == 0
    return jnp.concatenate([jnp.where(first, same, cross), jnp.where(first, cross, same)], axis=1)


def image_kernel(band_ref, sa_ref, sb_ref, out_ref):
    wide = sa_ref.shape[0]
    out_ref[...] = mm(band_ref[:, :wide], sa_ref[...]) + mm(band_ref[:, wide:2 * wide], sb_ref[...])


def own_image(band, sa, sb):
    shape = jax.ShapeDtypeStruct((band.shape[0], sa.shape[1]), jnp.float32)
    return call(image_kernel, shape, [VMEM] * 3)(band, sa, sb)


def send_shares(coded, row_count, share):
    me = lax.axis_index("row")
    arrived = []
    for shift in range(1, row_count):
        part = lax.dynamic_slice_in_dim(coded, (me + shift) % row_count * share, share, axis=0)
        ring = [(i, (i + shift) % row_count) for i in range(row_count)]
        arrived.append(lax.ppermute(part, "row", ring))
    return arrived


def body(hop, pattern, vectors, counts, center, halfwidth):
    rows_dev = hop.shape[0]
    block = hop.shape[2]
    half = vectors.shape[2]
    row_count = lax.axis_size("row")
    total_blocks = rows_dev * row_count
    order_total = total_blocks * block
    wide = W * block
    share = half // row_count
    assert rows_dev == 2 * W
    forward = [(i, (i + 1) % row_count) for i in range(row_count)]
    backward = [(target, source) for source, target in forward]
    swap = [(0, 1), (1, 0)]

    def halos_of(low, high):
        return lax.ppermute(high, "row", forward), lax.ppermute(low, "row", backward)

    x = vectors[0]
    xa, xb = x[:wide], x[wide:]
    halo_a, halo_b = halos_of(xa, xb)
    ids = ids_of(half)
    table = table_of(center, halfwidth, ids)
    band, image = band_parts(table, hop, pattern, xa, xb, total_blocks)
    sb = step(1, table, image, band, halo_b, xb)
    sa = step(0, table, image, band, lax.optimization_barrier((halo_a, sb))[0], xa)
    halo_a, halo_b = halos_of(sa, sb)
    image = own_image(band, sa, sb)
    live = live_of(after(counts, sa), ids)
    fa = finish(0, table, live, image, band, halo_a, sa, xa)
    oa = lax.ppermute(fa, "sub", swap)
    fb = finish(1, table, live, image, band, lax.optimization_barrier((halo_b, fa))[0], sb, xb)
    ob = lax.ppermute(fb, "sub", swap)
    early, turned = early_terms(fa, fb, oa, share)
    coded = code_terms(early, turned, ob, share)
    first, *middle, last = send_shares(coded.astype(jnp.float16), row_count, share)
    total = first_sum(coded, first.astype(jnp.float32), order_total)
    for piece in middle:
        total = add_piece(total, piece.astype(jnp.float32), order_total)
    total, last = lax.optimization_barrier((total, last))
    margin = last_sum(total, last.astype(jnp.float32), order_total)
    return margin.reshape(1, 1, share, 2 * half)


def solution(mesh):
    in_specs = (
        P(("groups", "row"), None, None, None),
        P(("groups", "row"), None),
        P("cuts", ("groups", "row"), "sub"),
        P(("groups", "cuts")),
        P(("groups", "cuts")),
        P(("groups", "cuts")),
    )
    out_specs = P(("groups", "cuts"), "sub", "row", None)
    return jax.shard_map(body, mesh=mesh, in_specs=in_specs, out_specs=out_specs, check_vma=False)
```

```python
import functools

import jax
import jax.numpy as jnp
from jax import lax
from jax.experimental import pallas as pl
from jax.experimental.pallas import tpu as pltpu
from jax.sharding import PartitionSpec as P

W = 3
LIMIT = 16 * 1024 * 1024
COST = pl.CostEstimate(flops=1000, bytes_accessed=1000, transcendentals=0)
LONG = pl.CostEstimate(flops=20_000_000_000, bytes_accessed=1000, transcendentals=0)
VMEM = pl.BlockSpec(memory_space=pltpu.VMEM)
SMEM = pl.BlockSpec(memory_space=pltpu.SMEM)


def call(kernel, out_shape, in_specs, cost=COST):
    return pl.pallas_call(
        kernel,
        out_shape=out_shape,
        in_specs=in_specs,
        out_specs=jax.tree.map(lambda _: VMEM, out_shape),
        compiler_params=pltpu.CompilerParams(vmem_limit_bytes=LIMIT),
        cost_estimate=cost,
    )


def mm(a, b):
    return jnp.dot(a, b, preferred_element_type=jnp.float32)


def tmm(a, b):
    return lax.dot_general(a, b, (((0,), (0,)), ((), ())), preferred_element_type=jnp.float32)


def after(value, other):
    return lax.optimization_barrier((value, other))[0]


def ids_kernel(out_ref):
    out_ref[...] = lax.broadcasted_iota(jnp.int32, out_ref.shape, 1) + lax.axis_index("sub") * out_ref.shape[1]


def ids_of(half):
    return call(ids_kernel, jax.ShapeDtypeStruct((8, half), jnp.int32), [], LONG)()


def table_kernel(center_ref, width_ref, ids_ref, table_ref):
    line = lax.broadcasted_iota(jnp.int32, table_ref.shape, 0)
    table_ref[...] = jnp.where(line == 0, center_ref[0], width_ref[0])


def table_of(center, halfwidth, ids):
    shape = jax.ShapeDtypeStruct(ids.shape, jnp.float32)
    return call(table_kernel, shape, [SMEM] * 2 + [VMEM])(after(center, ids), after(halfwidth, ids), ids)


def live_kernel(counts_ref, ids_ref, live_ref):
    live_ref[...] = jnp.where(ids_ref[...] < counts_ref[0], 1.0, 0.0)


def live_of(counts, ids):
    return call(live_kernel, jax.ShapeDtypeStruct(ids.shape, jnp.float32), [SMEM, VMEM])(counts, ids)


def band_kernel(total_blocks, table_ref, pattern_ref, hop_ref, xa_ref, xb_ref, band_ref, image_ref):
    rows_dev, stored, block, _ = hop_ref.shape
    wide = W * block
    first_block = lax.axis_index("row") * rows_dev
    band_ref[...] = jnp.zeros_like(band_ref)
    for r in range(rows_dev):
        rows = slice(r * block, (r + 1) * block)
        for k in range(stored):
            col = lax.rem(pattern_ref[r, k] - first_block + (W + total_blocks), total_blocks) - W
            inside = jnp.logical_and(col >= 0, col < rows_dev)
            halo = 2 * W + jnp.where(col < 0, col + W, col - rows_dev)
            at = jnp.where(inside, col, halo)
            band_ref[rows, pl.ds(pl.multiple_of(at * block, block), block)] = hop_ref[r, k]
    image_ref[...] = mm(band_ref[:, :wide], xa_ref[...]) + mm(band_ref[:, wide:2 * wide], xb_ref[...])


def band_parts(table, hop, pattern, xa, xb, total_blocks):
    rows_dev, _, block, _ = hop.shape
    wide, tall, half = W * block, rows_dev * block, xa.shape[1]
    return call(
        functools.partial(band_kernel, total_blocks),
        (
            jax.ShapeDtypeStruct((tall, 3 * wide), hop.dtype),
            jax.ShapeDtypeStruct((tall, half), jnp.float32),
        ),
        [VMEM, SMEM] + [VMEM] * 3,
    )(table, pattern, hop, xa, xb)


def halo_image(side, band_ref, image_ref, halo_ref):
    wide = halo_ref.shape[0]
    rows = slice(side * wide, (side + 1) * wide)
    return image_ref[rows, :] + mm(band_ref[rows, 2 * wide:], halo_ref[...])


def step_kernel(side, table_ref, image_ref, band_ref, halo_ref, x_ref, out_ref):
    shift, width = table_ref[0:1, :], table_ref[1:2, :]
    image = halo_image(side, band_ref, image_ref, halo_ref)
    out_ref[...] = ((image - shift * x_ref[...].astype(jnp.float32)) / width).astype(jnp.bfloat16)


def step(side, table, image, band, halo, x):
    shape = jax.ShapeDtypeStruct(x.shape, jnp.bfloat16)
    return call(functools.partial(step_kernel, side), shape, [VMEM] * 5)(table, image, band, halo, x)


def finish_kernel(side, table_ref, live_ref, image_ref, band_ref, halo_ref, s_ref, x_ref, out_ref):
    shift, width = table_ref[0:1, :], table_ref[1:2, :]
    live = live_ref[0:1, :] > 0.0
    image = halo_image(side, band_ref, image_ref, halo_ref)
    value = 2.0 * (image - shift * s_ref[...].astype(jnp.float32)) / width - x_ref[...].astype(jnp.float32)
    out_ref[...] = jnp.where(live, value, 0.0).astype(jnp.bfloat16)


def finish(side, table, live, image, band, halo, s, x):
    shape = jax.ShapeDtypeStruct(x.shape, jnp.bfloat16)
    return call(functools.partial(finish_kernel, side), shape, [VMEM] * 7)(table, live, image, band, halo, s, x)


def exponent(value):
    top = jnp.max(jnp.abs(value), axis=(0, 1), keepdims=True)
    return jnp.clip(jnp.ceil(jnp.log2(jnp.maximum(top, 1e-36))) - 14.0, -100.0, 60.0)


def with_code(share, line, same, e):
    row = lax.broadcasted_iota(jnp.int32, same.shape, 0)
    col = lax.broadcasted_iota(jnp.int32, same.shape, 1)
    return jnp.where((lax.rem(row, share) == line) & (col == row - line), e, same)


def early_kernel(share, fa_ref, fb_ref, oa_ref, out_ref, turned_ref):
    half = fa_ref.shape[1]
    fa, fb = fa_ref[...], fb_ref[...]
    same = tmm(fa, fa) + tmm(fb, fb)
    e = exponent(same)
    out_ref[:, :half] = with_code(share, 1, same * jnp.exp2(-e), e)
    out_ref[:, half:] = tmm(fa, oa_ref[...])
    turned_ref[...] = fb.T


def early_terms(fa, fb, oa, share):
    half = fa.shape[1]
    shapes = (jax.ShapeDtypeStruct((half, 2 * half), jnp.float32), jax.ShapeDtypeStruct(fb.shape[::-1], fb.dtype))
    return call(functools.partial(early_kernel, share), shapes, [VMEM] * 3)(fa, fb, oa)


def code_kernel(share, early_ref, turned_ref, ob_ref, out_ref):
    half = turned_ref.shape[0]
    cross = early_ref[:, half:] + mm(turned_ref[...], ob_ref[...])
    e = exponent(cross)
    out_ref[:, :half] = with_code(share, 2, early_ref[:, :half], e)
    out_ref[:, half:] = cross * jnp.exp2(-e)


def code_terms(early, turned, ob, share):
    shape = jax.ShapeDtypeStruct(early.shape, jnp.float32)
    return call(functools.partial(code_kernel, share), shape, [VMEM] * 3)(early, turned, ob)


def pick(head, shift, share):
    col = lax.broadcasted_iota(jnp.int32, head.shape, 1)
    here = col == lax.axis_index("row") * share + shift
    return jnp.sum(jnp.where(here, head, 0.0), axis=1, keepdims=True)


def factors(head, share, order_total):
    scale = jnp.exp2(pick(head, 0, share)) / order_total
    return scale[1:2], scale[2:3]


def first_sum_kernel(order_total, coded_ref, piece_ref, out_ref):
    share, half = out_ref.shape[0], out_ref.shape[1] // 2
    mine = coded_ref.at[pl.ds(pl.multiple_of(lax.axis_index("row") * share, 8), share), :]
    own_same, own_cross = factors(mine[:8, :half], share, order_total)
    same, cross = factors(piece_ref[:8, :half], share, order_total)
    out_ref[:, :half] = mine[:, :half] * own_same + piece_ref[:, :half] * same
    out_ref[:, half:] = mine[:, half:] * own_cross + piece_ref[:, half:] * cross


def first_sum(coded, piece, order_total):
    shape = jax.ShapeDtypeStruct(piece.shape, jnp.float32)
    return call(functools.partial(first_sum_kernel, order_total), shape, [VMEM] * 2, LONG)(coded, piece)


def add_kernel(order_total, sum_ref, piece_ref, out_ref):
    share, half = out_ref.shape[0], out_ref.shape[1] // 2
    same, cross = factors(piece_ref[:8, :half], share, order_total)
    out_ref[:, :half] = sum_ref[:, :half] + piece_ref[:, :half] * same
    out_ref[:, half:] = sum_ref[:, half:] + piece_ref[:, half:] * cross


def add_piece(total, piece, order_total):
    shape = jax.ShapeDtypeStruct(total.shape, jnp.float32)
    return call(functools.partial(add_kernel, order_total), shape, [VMEM] * 2, LONG)(total, piece)


def last_kernel(order_total, sum_ref, piece_ref, out_any, held_ref, sems):
    _, share, half = held_ref.shape
    same, cross = factors(piece_ref[:8, :half], share, order_total)
    sub = lax.axis_index("sub")

    def leave(slot, place):
        columns = pl.ds(pl.multiple_of(place * half, half), half)
        return pltpu.make_async_copy(held_ref.at[slot], out_any.at[:, columns], sems.at[slot])

    held_ref[0] = sum_ref[:, half:] + piece_ref[:, half:] * cross
    cross_copy = leave(0, 1 - sub)
    cross_copy.start()
    held_ref[1] = sum_ref[:, :half] + piece_ref[:, :half] * same
    head = sum_ref[:8, :half] + piece_ref[:8, :half] * same
    row = lax.broadcasted_iota(jnp.int32, head.shape, 0)
    col = lax.broadcasted_iota(jnp.int32, head.shape, 1)
    start = col == lax.axis_index("row") * share
    for line in (1, 2):
        head = jnp.where((row == line) & start, pick(head[:1], line, share), head)
    held_ref[1, :8, :] = head
    same_copy = leave(1, sub)
    same_copy.start()
    cross_copy.wait()
    same_copy.wait()


def last_sum(total, piece, order_total):
    share, columns = total.shape
    return pl.pallas_call(
        functools.partial(last_kernel, order_total),
        out_shape=jax.ShapeDtypeStruct(total.shape, jnp.float32),
        in_specs=[VMEM] * 2,
        out_specs=pl.BlockSpec(memory_space=pl.ANY),
        scratch_shapes=[
            pltpu.VMEM((2, share, columns // 2), jnp.float32),
            pltpu.SemaphoreType.DMA((2,)),
        ],
        compiler_params=pltpu.CompilerParams(vmem_limit_bytes=LIMIT),
        cost_estimate=COST,
    )(total, piece)


def image_kernel(band_ref, sa_ref, sb_ref, out_ref):
    wide = sa_ref.shape[0]
    out_ref[...] = mm(band_ref[:, :wide], sa_ref[...]) + mm(band_ref[:, wide:2 * wide], sb_ref[...])


def own_image(band, sa, sb):
    shape = jax.ShapeDtypeStruct((band.shape[0], sa.shape[1]), jnp.float32)
    return call(image_kernel, shape, [VMEM] * 3)(band, sa, sb)


def send_shares(coded, row_count, share):
    me = lax.axis_index("row")
    arrived = []
    middle = row_count // 2
    for shift in [middle, *range(1, middle), *range(middle + 1, row_count)]:
        part = lax.dynamic_slice_in_dim(coded, (me + shift) % row_count * share, share, axis=0)
        ring = [(i, (i + shift) % row_count) for i in range(row_count)]
        arrived.append(lax.ppermute(part, "row", ring))
    return arrived


def body(hop, pattern, vectors, counts, center, halfwidth):
    rows_dev = hop.shape[0]
    block = hop.shape[2]
    half = vectors.shape[2]
    row_count = lax.axis_size("row")
    total_blocks = rows_dev * row_count
    order_total = total_blocks * block
    wide = W * block
    share = half // row_count
    assert rows_dev == 2 * W
    forward = [(i, (i + 1) % row_count) for i in range(row_count)]
    backward = [(target, source) for source, target in forward]
    swap = [(0, 1), (1, 0)]

    def halos_of(low, high):
        return lax.ppermute(high, "row", forward), lax.ppermute(low, "row", backward)

    x = vectors[0]
    xa, xb = x[:wide], x[wide:]
    halo_a, halo_b = halos_of(xa, xb)
    ids = ids_of(half)
    table = table_of(center, halfwidth, ids)
    band, image = band_parts(table, hop, pattern, xa, xb, total_blocks)
    sb = step(1, table, image, band, halo_b, xb)
    sa = step(0, table, image, band, lax.optimization_barrier((halo_a, sb))[0], xa)
    halo_a, halo_b = halos_of(sa, sb)
    image = own_image(band, sa, sb)
    live = live_of(after(counts, sa), ids)
    fa = finish(0, table, live, image, band, halo_a, sa, xa)
    oa = lax.ppermute(fa, "sub", swap)
    fb = finish(1, table, live, image, band, lax.optimization_barrier((halo_b, fa))[0], sb, xb)
    ob = lax.ppermute(fb, "sub", swap)
    early, turned = early_terms(fa, fb, oa, share)
    coded = code_terms(early, turned, ob, share)
    first, *middle, last = send_shares(coded.astype(jnp.float16), row_count, share)
    total = first_sum(coded, first.astype(jnp.float32), order_total)
    for piece in middle:
        total = add_piece(total, piece.astype(jnp.float32), order_total)
    total, last = lax.optimization_barrier((total, last))
    margin = last_sum(total, last.astype(jnp.float32), order_total)
    return margin.reshape(1, 1, share, 2 * half)


def solution(mesh):
    in_specs = (
        P(("groups", "row"), None, None, None),
        P(("groups", "row"), None),
        P("cuts", ("groups", "row"), "sub"),
        P(("groups", "cuts")),
        P(("groups", "cuts")),
        P(("groups", "cuts")),
    )
    out_specs = P(("groups", "cuts"), "sub", "row", None)
    return jax.shard_map(body, mesh=mesh, in_specs=in_specs, out_specs=out_specs, check_vma=False)
```
